128 devices in a mesh: gx: 8 (over x, core), gy: 16 (over y, z).
Axes of the slice: x: 4, y: 4, z: 4, core: 2. Of those that a mesh axis runs over, the one named last changes fastest.
Arguments:
- features: bfloat16 [16, 32, 16, 512, 128], P('gx', 'gy'), may hold values from -6 to 6
- owner: int32 [16, 32, 16], P('gx', 'gy'), may hold values from -1 to 255, as said below
- norm_gain: float32 [8, 128], replicated, may hold values from 0.1 to 1.9
- time_shift: float32 [8, 512], replicated, may hold values from -4 to 4
- w_in: bfloat16 [8, 128, 512], replicated, may hold values from -0.5 to 0.5
- w_out: bfloat16 [8, 512, 128], replicated, may hold values from -0.25 to 0.25
- w_down: bfloat16 [2, 2, 2, 128, 128], replicated, may hold values from -0.1875 to 0.1875
- w_conv: bfloat16 [3, 3, 3, 128, 128], replicated, may hold values from -0.109375 to 0.109375
- w_up: bfloat16 [2, 2, 2, 128, 128], replicated, may hold values from -0.5 to 0.5
Outputs:
- denoised: bfloat16 [16, 32, 16, 512, 128], P('gx', 'gy')
The draws below stay inside these ranges and needn't reach their ends.
Inputs may be any that keep to these rules, and one draw needn't show every extreme that they name: Within each gx index and gy group, every owner along gy gets exactly 16 bricks, one in each compute slot; at most 2 bricks of one device go to one owner, and some device sends 2 to some owner; a device holds at most 32 occupied bricks, and some device holds exactly that many.
All inputs are finite; a program needn't handle non-finite values.
Results may differ from the reference program's by a relative error of at most 0.029.
Values may be sent and summed in bfloat16 or wider, within the bound.
A program may use at most 192 MiB of HBM per device.

```python
import jax
import jax.numpy as jnp
from jax import lax

C = 128
HID = 512
LAYERS = 8
BX = 2
BY = 2
ZCAP = 16
LOAD = 16
NBX = 16
NBY = 32


def draw_owner(key, part):
    key = jax.random.fold_in(key, 7)
    groups = NBX // BX
    width = NBY // BY
    slots = BX * BY * ZCAP
    half = width // 2
    steps_i = jnp.arange(half, dtype=jnp.int32)
    delta = LOAD * steps_i // max(half - 1, 1)
    pattern = jnp.concatenate([LOAD + delta, LOAD - delta]).astype(jnp.int32)

    def one_group(group_key):
        keys = jax.random.split(group_key, width + 2)
        counts = pattern[jax.random.permutation(keys[0], width)]
        starts = jnp.cumsum(counts) - counts
        offset = jax.random.randint(keys[1], (), 0, width)
        ranks = jax.vmap(lambda k: jax.random.permutation(k, slots))(keys[2:]).astype(jnp.int32)
        placed = starts[:, None] + ranks
        codes = (placed + offset) % width * LOAD + placed // width
        codes = jnp.where(ranks < counts[:, None], codes, -1)
        return codes.reshape(width, BX, BY, ZCAP).transpose(1, 0, 2, 3).reshape(BX, NBY, ZCAP)
    group_keys = jax.random.split(key, groups)
    return jax.vmap(one_group)(group_keys).reshape(NBX, NBY, ZCAP).astype(jnp.int32)


def block_scale(key, extent, cuts, low, largest):
    gain = 1.0
    for dim, shards_of in cuts:
        heights = jax.random.uniform(jax.random.fold_in(jax.random.fold_in(key, 6), dim), (shards_of,), jnp.float32, low / len(cuts), largest / len(cuts))
        gain = gain * jnp.repeat(jnp.exp(heights), extent[dim] // shards_of).reshape((-1,) + (1,) * (len(extent) - 1 - dim))
    return gain


def normal_values(own_key, extent, spread, reach, pieces=(), kind=jnp.bfloat16):
    entries = spread * jax.random.normal(own_key, extent, jnp.float32)
    if pieces:
        entries = entries * block_scale(own_key, extent, pieces, -0.22, 0.18)
    return jnp.clip(entries, -reach, reach).astype(kind)


def setup_inputs(seed: int = 0) -> dict:
    key_of = jax.random.split(jax.random.key(seed), 10)
    features = normal_values(key_of[0], (NBX, NBY, ZCAP, 512, C), 1.0, 6.0, ((0, 8), (1, 16)))
    owner = draw_owner(jax.random.fold_in(key_of[9], 71), 0)
    norm_gain = jnp.clip(1.0 + 0.18 * jax.random.normal(key_of[2], (LAYERS, C), jnp.float32), 0.1, 1.9)
    time_shift = normal_values(key_of[3], (LAYERS, HID), 1.0, 4.0, (), jnp.float32)
    w_in = normal_values(key_of[4], (LAYERS, C, HID), C ** -0.5, 0.5)
    w_out = normal_values(key_of[5], (LAYERS, HID, C), HID ** -0.5, 0.25)
    w_down = normal_values(key_of[6], (2, 2, 2, C, C), (8 * C) ** -0.5, 0.1875)
    w_conv = normal_values(key_of[7], (3, 3, 3, C, C), (27 * C) ** -0.5, 0.109375)
    w_up = normal_values(key_of[8], (2, 2, 2, C, C), C ** -0.5, 0.5)
    return {"features": features, "owner": owner, "norm_gain": norm_gain, "time_shift": time_shift, "w_in": w_in, "w_out": w_out, "w_down": w_down, "w_conv": w_conv, "w_up": w_up}


def brick_down(bricks, live, norm_gain, time_shift, w_in, w_out, w_down):
    count, voxels, chan = bricks.shape
    stream = bricks.reshape(-1, chan)
    for layer in range(w_in.shape[0]):
        whole = stream.astype(jnp.float32)
        scale = lax.rsqrt(lax.optimization_barrier(jnp.mean(whole * whole, axis=-1, keepdims=True)) + 1e-06)
        normed = (whole * scale * norm_gain[layer]).astype(jnp.bfloat16)
        hidden = jax.nn.silu(jnp.dot(normed, w_in[layer], preferred_element_type=jnp.float32) + time_shift[layer]).astype(jnp.bfloat16)
        stream = (whole + jnp.dot(hidden, w_out[layer], preferred_element_type=jnp.float32)).astype(jnp.bfloat16)
    cells = stream.reshape(count, 4, 2, 4, 2, 4, 2, chan).astype(jnp.float32)
    down = jnp.einsum('giajbkcd,abcde->gijke', cells, w_down.astype(jnp.float32))
    return (jax.nn.silu(down).reshape(count, 64, chan) * live[:, None, None]).astype(jnp.bfloat16)

def brick_up(bricks, mixed, live, w_up):
    count, voxels, chan = bricks.shape
    coarse = mixed.reshape(count, 4, 4, 4, chan).astype(jnp.float32)
    upward = jnp.einsum('gijkd,abcde->giajbkce', coarse, w_up.astype(jnp.float32)).reshape(count, voxels, chan)
    return ((bricks.astype(jnp.float32) + upward) * live[:, None, None]).astype(jnp.bfloat16)

def reference(features, owner, norm_gain, time_shift, w_in, w_out, w_down, w_conv, w_up):
    columns = features.reshape(NBX * NBY, ZCAP, 512, C)
    live = (owner >= 0).astype(jnp.float32).reshape(NBX * NBY, ZCAP)
    coarse = lax.map(lambda pair: brick_down(pair[0], pair[1], norm_gain, time_shift, w_in, w_out, w_down), (columns, live))
    grid = coarse.reshape(NBX, NBY, ZCAP, 4, 4, 4, C).transpose(0, 3, 1, 4, 2, 5, 6).reshape(NBX * 4, NBY * 4, ZCAP * 4, C)
    padded = jnp.pad(grid, ((1, 1), (1, 1), (1, 1), (0, 0)))
    total = grid.astype(jnp.float32)
    for d in range(3):
        for e in range(3):
            for f in range(3):
                moved = padded[d:d + NBX * 4, e:e + NBY * 4, f:f + ZCAP * 4].reshape(-1, C)
                total = total + jnp.dot(moved, w_conv[d, e, f], preferred_element_type=jnp.float32).reshape(total.shape)
    live_grid = jnp.broadcast_to(live.reshape(NBX, 1, NBY, 1, ZCAP, 1, 1), (NBX, 4, NBY, 4, ZCAP, 4, 1)).reshape(NBX * 4, NBY * 4, ZCAP * 4, 1)
    mixed = (total * live_grid).astype(jnp.bfloat16)
    mixed = mixed.reshape(NBX, 4, NBY, 4, ZCAP, 4, C).transpose(0, 2, 4, 1, 3, 5, 6).reshape(NBX * NBY, ZCAP, 64, C)
    result = lax.map(lambda trio: brick_up(trio[0], trio[1], trio[2], w_up), (columns, mixed, live))
    return result.reshape(NBX, NBY, ZCAP, 512, C)
```

```python
import functools

import jax
import jax.numpy as jnp
from jax import lax
from jax.experimental import pallas as pl
from jax.experimental.pallas import tpu as pltpu
from jax.sharding import PartitionSpec as P

BF16 = jnp.bfloat16
F32 = jnp.float32
GROUP = 4
CHUNK = 512


def transposed(eye, block):
    return lax.dot_general(eye, block, (((1,), (1,)), ((), ())), preferred_element_type=F32)


def identity(n):
    rows = lax.broadcasted_iota(jnp.int32, (n, n), 0)
    return (rows == lax.broadcasted_iota(jnp.int32, (n, n), 1)).astype(BF16)


def prepare_weights(eye, gain_ref, shift_ref, w_in_ref, w_out_ref, wi_ref, wo_ref):
    layers, chan, hid = w_in_ref.shape
    row = lax.broadcasted_iota(jnp.int32, (chan, hid), 0)

    def one(l, _):
        gain = gain_ref[l] * 0.5
        shift = shift_ref[l] * 0.5
        high = shift.astype(BF16).astype(F32)
        mid = (shift - high).astype(BF16).astype(F32)
        low = shift - high - mid
        parts = jnp.where(row == 0, high, jnp.where(row == 1, mid, jnp.where(row == 2, low, 0.0))).astype(BF16)
        w_in = w_in_ref[l]
        w_out = w_out_ref[l]
        for m in range(hid // chan):
            cut = slice(m * chan, (m + 1) * chan)
            wi_ref[l, cut, :chan] = (transposed(eye, w_in[:, cut]) * gain).astype(BF16)
            wi_ref[l, cut, chan:] = transposed(eye, parts[:, cut]).astype(BF16)
            wo_ref[l, :, cut] = transposed(eye, w_out[cut, :]).astype(BF16)
        return 0

    lax.fori_loop(0, layers, one, 0)


def feed_forward(s_ref, wi_ref, wo_ref):
    layers = wi_ref.shape[0]
    chan, width = s_ref.shape
    count = width // CHUNK
    ones = jnp.ones((chan, CHUNK), BF16)

    def hidden(step):
        l, c = divmod(step, count)
        x = s_ref[:, c * CHUNK : (c + 1) * CHUNK]
        scale = lax.rsqrt(jnp.mean(x * x, axis=0, keepdims=True) + 1e-06)
        normed = jnp.concatenate([(x * scale).astype(BF16), ones], axis=0)
        u = jnp.dot(wi_ref[l], normed, preferred_element_type=F32)
        return (u * jnp.tanh(u) + u).astype(BF16)

    def update(step, h):
        l, c = divmod(step, count)
        s_ref[:, c * CHUNK : (c + 1) * CHUNK] += jnp.dot(wo_ref[l], h, preferred_element_type=F32)

    held = hidden(0)
    for step in range(layers * count):
        following = hidden(step + 1) if step + 1 < layers * count else None
        update(step, held)
        held = following


def coarse_kernel(
    owner_ref, features_ref, gain_ref, shift_ref, w_in_ref, w_out_ref, w_down_ref,
    out_ref,
    list_ref, buf_ref, s_ref, t_ref, wi_ref, wo_ref, grid_ref, sems,
):
    slots = owner_ref.shape[0]
    chan = s_ref.shape[0]
    zcap = slots // 4
    eye = identity(chan)

    def note(slot, n):
        @pl.when(owner_ref[slot] >= 0)
        def _():
            list_ref[n] = slot

        return n + (owner_ref[slot] >= 0).astype(jnp.int32)

    total = lax.fori_loop(0, slots, note, 0)
    groups = (total + GROUP - 1) // GROUP

    def brick(g, t):
        return list_ref[jnp.minimum(g * GROUP + t, total - 1)]

    def copy(g, t):
        return pltpu.make_async_copy(
            features_ref.at[brick(g, t)], buf_ref.at[lax.rem(g, 2), t], sems.at[lax.rem(g, 2), t]
        )

    @pl.when(groups > 0)
    def _():
        for t in range(GROUP):
            copy(0, t).start()

    prepare_weights(eye, gain_ref, shift_ref, w_in_ref, w_out_ref, wi_ref, wo_ref)
    grid_ref[...] = jnp.zeros_like(grid_ref)
    half = lax.broadcasted_iota(jnp.int32, (16, 8, 1), 1) // 4

    def body(g, _):
        @pl.when(g + 1 < groups)
        def _():
            for t in range(GROUP):
                copy(g + 1, t).start()

        for t in range(GROUP):
            copy(g, t).wait()
        for t in range(GROUP):
            s_ref[:, t * 512 : (t + 1) * 512] = transposed(eye, buf_ref[lax.rem(g, 2), t])
        feed_forward(s_ref, wi_ref, wo_ref)
        for t in range(GROUP):
            for m in range(4):
                block = s_ref[:, t * 512 + m * 128 : t * 512 + (m + 1) * 128].astype(BF16)
                t_ref[t, m * 128 : (m + 1) * 128, :] = transposed(eye, block)
        for t in range(GROUP):
            total_down = jnp.zeros((128, 2 * chan), F32)
            for a in range(2):
                for c in range(2):
                    rows = jnp.concatenate(
                        [t_ref[t, pl.ds(128 * i + 64 * a + c, 32, stride=2), :] for i in range(4)], axis=0
                    ).astype(BF16)
                    weights = jnp.concatenate([w_down_ref[a, 0, c], w_down_ref[a, 1, c]], axis=1)
                    total_down += jnp.dot(rows, weights, preferred_element_type=F32)
            both = total_down.reshape(16, 8, 2 * chan)
            own = jnp.where(half == 0, both[:, :, :chan], both[:, :, chan:])
            down = own + jnp.concatenate([own[:, 4:, :], own[:, :4, :]], axis=1)
            made = down / (1.0 + jnp.exp(-down))
            slot = brick(g, t)
            column, r = slot // zcap, lax.rem(slot, zcap)
            x0, y0, zpair, odd = (column // 2) * 4, lax.rem(column, 2) * 4, r // 2, lax.rem(r, 2)

            @pl.when(g * GROUP + t < total)
            def _():
                for i in range(4):
                    for j in range(4):
                        old = grid_ref[x0 + i, y0 + j, zpair]
                        grid_ref[x0 + i, y0 + j, zpair] = jnp.where(half[0] == odd, made[4 * i + j], old)

        return 0

    lax.fori_loop(0, groups, body, 0)

    def finish(x, _):
        out_ref[x] = grid_ref[x].reshape(out_ref.shape[1:]).astype(BF16)
        return 0

    lax.fori_loop(0, out_ref.shape[0], finish, 0)


def coarse_grid(features, owner, gain, shift, w_in, w_out, w_down):
    slots, voxels, chan = features.shape
    layers, _, hid = w_in.shape
    vmem = pl.BlockSpec(memory_space=pltpu.VMEM)
    return pl.pallas_call(
        coarse_kernel,
        out_shape=jax.ShapeDtypeStruct((8, 8, slots, chan), BF16),
        in_specs=[pl.BlockSpec(memory_space=pltpu.SMEM), pl.BlockSpec(memory_space=pl.ANY)] + [vmem] * 5,
        out_specs=vmem,
        scratch_shapes=[
            pltpu.SMEM((slots,), jnp.int32),
            pltpu.VMEM((2, GROUP, voxels, chan), BF16),
            pltpu.VMEM((chan, GROUP * voxels), F32),
            pltpu.VMEM((GROUP, voxels, chan), F32),
            pltpu.VMEM((layers, hid, 2 * chan), BF16),
            pltpu.VMEM((layers, chan, hid), BF16),
            pltpu.VMEM((8, 8, slots // 8, 8, chan), F32),
            pltpu.SemaphoreType.DMA((2, GROUP)),
        ],
        compiler_params=pltpu.CompilerParams(vmem_limit_bytes=48 * 2**20),
        cost_estimate=pl.CostEstimate(flops=32 * 10**9, bytes_accessed=8 * 2**20, transcendentals=10**8),
        name="coarse",
    )(owner, features, gain[:, None, :], shift[:, None, :], w_in, w_out, w_down)


def lift_kernel(
    rim_ref, features_ref, live_ref, w_conv_ref, w_up_ref,
    out_ref,
    z_ref, wc_ref, a_ref,
):
    chan = rim_ref.shape[-1]
    gsz = rim_ref.shape[2]
    step = pl.program_id(0)

    @pl.when(step == 0)
    def _():
        row = lax.broadcasted_iota(jnp.int32, (gsz, chan), 0)
        wide = rim_ref.shape[1]

        def shift(n, _):
            x, y = n // wide, lax.rem(n, wide)
            whole = rim_ref[x, y].astype(F32)
            z_ref[0, x, y] = jnp.where(row == 0, 0.0, pltpu.roll(whole, 1, 0)).astype(BF16)
            z_ref[1, x, y] = rim_ref[x, y]
            z_ref[2, x, y] = jnp.where(row == gsz - 1, 0.0, pltpu.roll(whole, gsz - 1, 0)).astype(BF16)
            return 0

        lax.fori_loop(0, rim_ref.shape[0] * wide, shift, 0, unroll=4)
        empty = jnp.zeros((chan, chan), BF16)
        for d in range(3):
            for f in range(3):
                for k in range(4):
                    for o in range(2):
                        e = k - o
                        wc_ref[3 * d + f, k * chan : (k + 1) * chan, o * chan : (o + 1) * chan] = (
                            w_conv_ref[d, e, f] if 0 <= e <= 2 else empty
                        )
        a_ref[...] = jnp.zeros_like(a_ref)

    x0, y0 = (step // 2) * 4, lax.rem(step, 2) * 4
    live = live_ref[0]
    for pair in range(2):
        y = y0 + 2 * pair
        total = jnp.zeros((4 * gsz, 2 * chan), F32)
        for d in range(3):
            for f in range(3):
                rows = jnp.concatenate(
                    [z_ref[f, pl.ds(x0 + d, 4), y + k].reshape(4 * gsz, chan) for k in range(4)], axis=1
                )
                total += jnp.dot(rows, wc_ref[3 * d + f], preferred_element_type=F32)
        for o in range(2):
            own = rim_ref[pl.ds(x0 + 1, 4), y + o + 1].reshape(4 * gsz, chan).astype(F32)
            mixed = total[:, o * chan : (o + 1) * chan] + own
            a_ref[o, 0, pl.ds(0, 4 * gsz, stride=2), :] = mixed
            a_ref[o, 1, pl.ds(1, 4 * gsz, stride=2), :] = mixed
            spread = jnp.concatenate([a_ref[o, 0], a_ref[o, 1]], axis=1).astype(BF16)
            j = 2 * pair + o
            for a in range(2):
                weights = jnp.concatenate(
                    [jnp.concatenate([w_up_ref[a, b, c] for b in range(2)], axis=1) for c in range(2)], axis=0
                )
                upward = jnp.dot(spread, weights, preferred_element_type=F32)
                for i in range(4):
                    part = upward[2 * gsz * i : 2 * gsz * (i + 1)].reshape(gsz // 4, 8, 2 * chan)
                    part = jnp.concatenate([part[:, :, :chan], part[:, :, chan:]], axis=1)
                    base = 128 * i + 64 * a + 16 * j
                    given = features_ref[:, base : base + 16, :].astype(F32)
                    out_ref[:, base : base + 16, :] = ((given + part) * live).astype(BF16)


def lift(rim, features, live, w_conv, w_up):
    slots, voxels, chan = features.shape
    gsx, gsy, gsz, _ = rim.shape
    columns = 4
    zcap = slots // columns
    vmem = pl.BlockSpec(memory_space=pltpu.VMEM)
    block = pl.BlockSpec((zcap, voxels, chan), lambda s: (s, 0, 0))
    return pl.pallas_call(
        lift_kernel,
        grid=(columns,),
        out_shape=jax.ShapeDtypeStruct(features.shape, BF16),
        in_specs=[
            vmem,
            block,
            pl.BlockSpec((1, zcap, 1, chan), lambda s: (s, 0, 0, 0)),
            vmem,
            vmem,
        ],
        out_specs=block,
        scratch_shapes=[
            pltpu.VMEM((3, gsx, gsy, gsz, chan), BF16),
            pltpu.VMEM((9, 4 * chan, 2 * chan), BF16),
            pltpu.VMEM((2, 2, 8 * gsz, chan), F32),
        ],
        compiler_params=pltpu.CompilerParams(vmem_limit_bytes=48 * 2**20),
        cost_estimate=pl.CostEstimate(flops=5 * 10**9, bytes_accessed=18 * 2**20, transcendentals=0),
        name="lift",
    )(rim, features, live, w_conv, w_up)


def extended(cells, sides, width):
    for axis, dim in sides:
        count = lax.axis_size(axis)
        ends = count - 1
        head = lax.slice_in_dim(cells, 0, width, axis=dim)
        tail = lax.slice_in_dim(cells, cells.shape[dim] - width, cells.shape[dim], axis=dim)
        cells = jnp.concatenate(
            [
                lax.ppermute(tail, axis, [(i, (i + 1) % count) for i in range(ends)]),
                cells,
                lax.ppermute(head, axis, [((i + 1) % count, i) for i in range(ends)]),
            ],
            axis=dim,
        )
    return cells


def local(features, owner, norm_gain, time_shift, w_in, w_out, w_down, w_conv, w_up):
    cols_x, cols_y, zcap, voxels, chan = features.shape
    slots = cols_x * cols_y * zcap
    flat = features.reshape(slots, voxels, chan)
    code = owner.reshape(slots)
    grid = coarse_grid(flat, code, norm_gain, time_shift, w_in, w_out, w_down)
    rimmed = extended(grid, (("gx", 0), ("gy", 1)), 1)
    live = jnp.broadcast_to(
        (code >= 0).astype(F32).reshape(cols_x * cols_y, zcap, 1, 1), (cols_x * cols_y, zcap, 1, chan)
    )
    result = lift(rimmed, flat, live, w_conv, w_up)
    return result.reshape(features.shape)


def solution(mesh):
    in_specs = (
        P("gx", "gy", None, None, None),
        P("gx", "gy", None),
        P(),
        P(),
        P(),
        P(),
        P(),
        P(),
        P(),
    )
    out_specs = P("gx", "gy", None, None, None)
    return jax.shard_map(local, mesh=mesh, in_specs=in_specs, out_specs=out_specs, check_vma=False)
```

```python
import functools

import jax
import jax.numpy as jnp
from jax import lax
from jax.experimental import pallas as pl
from jax.experimental.pallas import tpu as pltpu
from jax.sharding import PartitionSpec as P

BF16 = jnp.bfloat16
F32 = jnp.float32
GROUP = 4
CHUNK = 512


def transposed(eye, block):
    return lax.dot_general(eye, block, (((1,), (1,)), ((), ())), preferred_element_type=F32)


def identity(n):
    rows = lax.broadcasted_iota(jnp.int32, (n, n), 0)
    return (rows == lax.broadcasted_iota(jnp.int32, (n, n), 1)).astype(BF16)


def prepare_weights(eye, gain_ref, shift_ref, w_in_ref, w_out_ref, wi_ref, wo_ref):
    layers, chan, hid = w_in_ref.shape
    row = lax.broadcasted_iota(jnp.int32, (chan, hid), 0)

    def one(l, _):
        gain = gain_ref[pl.ds(l, 1), :] * 0.5
        shift = shift_ref[pl.ds(l, 1), :] * 0.5
        high = shift.astype(BF16).astype(F32)
        mid = (shift - high).astype(BF16).astype(F32)
        low = shift - high - mid
        parts = jnp.where(row == 0, high, jnp.where(row == 1, mid, jnp.where(row == 2, low, 0.0))).astype(BF16)
        w_in = w_in_ref[l]
        w_out = w_out_ref[l]
        for m in range(hid // chan):
            cut = slice(m * chan, (m + 1) * chan)
            wi_ref[l, cut, :chan] = (transposed(eye, w_in[:, cut]) * gain).astype(BF16)
            wi_ref[l, cut, chan:] = transposed(eye, parts[:, cut]).astype(BF16)
            wo_ref[l, :, cut] = transposed(eye, w_out[cut, :]).astype(BF16)
        return 0

    lax.fori_loop(0, layers, one, 0)


def feed_forward(s_ref, wi_ref, wo_ref):
    layers = wi_ref.shape[0]
    chan, width = s_ref.shape
    count = width // CHUNK
    ones = jnp.ones((chan, CHUNK), BF16)

    def hidden(step):
        l, c = divmod(step, count)
        x = s_ref[:, c * CHUNK : (c + 1) * CHUNK]
        scale = lax.rsqrt(jnp.mean(x * x, axis=0, keepdims=True) + 1e-06)
        normed = jnp.concatenate([(x * scale).astype(BF16), ones], axis=0)
        u = jnp.dot(wi_ref[l], normed, preferred_element_type=F32)
        return (u * jnp.tanh(u) + u).astype(BF16)

    def update(step, h):
        l, c = divmod(step, count)
        s_ref[:, c * CHUNK : (c + 1) * CHUNK] += jnp.dot(wo_ref[l], h, preferred_element_type=F32)

    held = hidden(0)
    for step in range(layers * count):
        following = hidden(step + 1) if step + 1 < layers * count else None
        update(step, held)
        held = following


def coarse_kernel(
    owner_ref, features_ref, gain_ref, shift_ref, w_in_hbm, w_out_hbm, w_down_hbm,
    out_ref,
    list_ref, buf_ref, s_ref, t_ref, wi_ref, wo_ref, grid_ref, w_in_ref, w_out_ref, w_down_ref, sems, w_sems,
):
    _, cols_y, zcap = owner_ref.shape
    slots = out_ref.shape[2]
    chan = s_ref.shape[0]
    eye = identity(chan)
    weights = [
        pltpu.make_async_copy(src, dst, w_sems.at[n])
        for n, (src, dst) in enumerate(((w_in_hbm, w_in_ref), (w_out_hbm, w_out_ref), (w_down_hbm, w_down_ref)))
    ]
    for w in weights:
        w.start()

    def note(slot, n):
        column, r = slot // zcap, lax.rem(slot, zcap)
        alive = owner_ref[column // cols_y, lax.rem(column, cols_y), r] >= 0

        @pl.when(alive)
        def _():
            list_ref[n] = slot

        return n + alive.astype(jnp.int32)

    total = lax.fori_loop(0, slots, note, 0)
    groups = (total + GROUP - 1) // GROUP

    def brick(g, t):
        return list_ref[jnp.minimum(g * GROUP + t, total - 1)]

    def copy(g, t):
        return pltpu.make_async_copy(
            features_ref.at[brick(g, t)], buf_ref.at[lax.rem(g, 2), t], sems.at[lax.rem(g, 2), t]
        )

    @pl.when(groups > 0)
    def _():
        for t in range(GROUP):
            copy(0, t).start()

    grid_ref[...] = jnp.zeros_like(grid_ref)
    for w in weights:
        w.wait()
    prepare_weights(eye, gain_ref, shift_ref, w_in_ref, w_out_ref, wi_ref, wo_ref)
    half = lax.broadcasted_iota(jnp.int32, (16, 8, 1), 1) // 4

    def body(g, _):
        @pl.when(g + 1 < groups)
        def _():
            for t in range(GROUP):
                copy(g + 1, t).start()

        for t in range(GROUP):
            copy(g, t).wait()
        for t in range(GROUP):
            s_ref[:, t * 512 : (t + 1) * 512] = transposed(eye, buf_ref[lax.rem(g, 2), t])
        feed_forward(s_ref, wi_ref, wo_ref)
        for t in range(GROUP):
            for m in range(4):
                block = s_ref[:, t * 512 + m * 128 : t * 512 + (m + 1) * 128].astype(BF16)
                t_ref[t, m * 128 : (m + 1) * 128, :] = transposed(eye, block)
        for t in range(GROUP):
            total_down = jnp.zeros((128, 2 * chan), F32)
            for a in range(2):
                for c in range(2):
                    rows = jnp.concatenate(
                        [t_ref[t, pl.ds(128 * i + 64 * a + c, 32, stride=2), :] for i in range(4)], axis=0
                    ).astype(BF16)
                    weights = jnp.concatenate([w_down_ref[a, 0, c], w_down_ref[a, 1, c]], axis=1)
                    total_down += jnp.dot(rows, weights, preferred_element_type=F32)
            both = total_down.reshape(16, 8, 2 * chan)
            own = jnp.where(half == 0, both[:, :, :chan], both[:, :, chan:])
            down = own + jnp.concatenate([own[:, 4:, :], own[:, :4, :]], axis=1)
            made = down / (1.0 + jnp.exp(-down))
            slot = brick(g, t)
            column, r = slot // zcap, lax.rem(slot, zcap)
            x0, y0, zpair, odd = (column // 2) * 4, lax.rem(column, 2) * 4, r // 2, lax.rem(r, 2)

            @pl.when(g * GROUP + t < total)
            def _():
                for i in range(4):
                    for j in range(4):
                        old = grid_ref[x0 + i, y0 + j, zpair]
                        grid_ref[x0 + i, y0 + j, zpair] = jnp.where(half[0] == odd, made[4 * i + j], old)

        return 0

    lax.fori_loop(0, groups, body, 0)

    def finish(x, _):
        out_ref[x] = grid_ref[x].reshape(out_ref.shape[1:]).astype(BF16)
        return 0

    lax.fori_loop(0, out_ref.shape[0], finish, 0)


def coarse_grid(features, owner, gain, shift, w_in, w_out, w_down):
    slots, voxels, chan = features.shape
    layers, _, hid = w_in.shape
    vmem = pl.BlockSpec(memory_space=pltpu.VMEM)
    hbm = pl.BlockSpec(memory_space=pl.ANY)
    return pl.pallas_call(
        coarse_kernel,
        out_shape=jax.ShapeDtypeStruct((8, 8, slots, chan), BF16),
        in_specs=[pl.BlockSpec(memory_space=pltpu.SMEM), hbm, vmem, vmem, hbm, hbm, hbm],
        out_specs=vmem,
        scratch_shapes=[
            pltpu.SMEM((slots,), jnp.int32),
            pltpu.VMEM((2, GROUP, voxels, chan), BF16),
            pltpu.VMEM((chan, GROUP * voxels), F32),
            pltpu.VMEM((GROUP, voxels, chan), F32),
            pltpu.VMEM((layers, hid, 2 * chan), BF16),
            pltpu.VMEM((layers, chan, hid), BF16),
            pltpu.VMEM((8, 8, slots // 8, 8, chan), F32),
            pltpu.VMEM(w_in.shape, BF16),
            pltpu.VMEM(w_out.shape, BF16),
            pltpu.VMEM(w_down.shape, BF16),
            pltpu.SemaphoreType.DMA((2, GROUP)),
            pltpu.SemaphoreType.DMA((3,)),
        ],
        compiler_params=pltpu.CompilerParams(vmem_limit_bytes=48 * 2**20),
        cost_estimate=pl.CostEstimate(flops=32 * 10**9, bytes_accessed=8 * 2**20, transcendentals=10**8),
        name="coarse",
    )(owner, features, gain, shift, w_in, w_out, w_down)


def lift_kernel(
    owner_ref, rim_ref, features_ref, w_conv_ref, w_up_ref,
    out_ref,
    wc_ref, a_ref,
):
    chan = rim_ref.shape[-1]
    gsz = rim_ref.shape[2]
    zcap = owner_ref.shape[2]
    step = pl.program_id(0)
    p, q = step // 2, lax.rem(step, 2)

    @pl.when(step == 0)
    def _():
        empty = jnp.zeros((chan, chan), BF16)
        for d in range(3):
            for k in range(4):
                for o in range(2):
                    e = k - o
                    for f in range(3):
                        col = (2 * f + o) * chan
                        wc_ref[d, k * chan : (k + 1) * chan, col : col + chan] = (
                            w_conv_ref[d, e, f] if 0 <= e <= 2 else empty
                        )
        a_ref[...] = jnp.zeros_like(a_ref)

    x0, y0 = p * 4, q * 4
    live = jnp.concatenate(
        [jnp.full((1, 16, chan), (owner_ref[p, q, r] >= 0).astype(F32)) for r in range(zcap)], axis=0
    )
    z = lax.rem(lax.broadcasted_iota(jnp.int32, (4 * gsz, 2 * chan), 0), gsz)
    for pair in range(2):
        y = y0 + 2 * pair
        total = jnp.zeros((4 * gsz, 6 * chan), F32)
        for d in range(3):
            rows = jnp.concatenate(
                [rim_ref[pl.ds(x0 + d, 4), y + k].reshape(4 * gsz, chan) for k in range(4)], axis=1
            )
            total += jnp.dot(rows, wc_ref[d], preferred_element_type=F32)
        below = pltpu.roll(total[:, : 2 * chan], 1, 0)
        above = pltpu.roll(total[:, 4 * chan :], 4 * gsz - 1, 0)
        summed = total[:, 2 * chan : 4 * chan] + jnp.where(z == 0, 0.0, below) + jnp.where(z == gsz - 1, 0.0, above)
        for o in range(2):
            own = rim_ref[pl.ds(x0 + 1, 4), y + o + 1].reshape(4 * gsz, chan).astype(F32)
            mixed = summed[:, o * chan : (o + 1) * chan] + own
            j = 2 * pair + o
            a_ref[j, 0, pl.ds(0, 4 * gsz, stride=2), :] = mixed
            a_ref[j, 1, pl.ds(1, 4 * gsz, stride=2), :] = mixed
            spread = jnp.concatenate([a_ref[j, 0], a_ref[j, 1]], axis=1).astype(BF16)
            for a in range(2):
                weights = jnp.concatenate(
                    [jnp.concatenate([w_up_ref[a, b, c] for b in range(2)], axis=1) for c in range(2)], axis=0
                )
                upward = jnp.dot(spread, weights, preferred_element_type=F32)
                for i in range(4):
                    part = upward[2 * gsz * i : 2 * gsz * (i + 1)].reshape(gsz // 4, 8, 2 * chan)
                    part = jnp.concatenate([part[:, :, :chan], part[:, :, chan:]], axis=1)
                    base = 128 * i + 64 * a + 16 * j
                    given = features_ref[:, base : base + 16, :].astype(F32)
                    out_ref[:, base : base + 16, :] = ((given + part) * live).astype(BF16)


def lift(owner, rim, features, w_conv, w_up):
    slots, voxels, chan = features.shape
    gsz = rim.shape[2]
    columns = 4
    vmem = pl.BlockSpec(memory_space=pltpu.VMEM)
    block = pl.BlockSpec((slots // columns, voxels, chan), lambda s: (s, 0, 0))
    return pl.pallas_call(
        lift_kernel,
        grid=(columns,),
        out_shape=jax.ShapeDtypeStruct(features.shape, BF16),
        in_specs=[pl.BlockSpec(memory_space=pltpu.SMEM), vmem, block, vmem, vmem],
        out_specs=block,
        scratch_shapes=[
            pltpu.VMEM((3, 4 * chan, 6 * chan), BF16),
            pltpu.VMEM((4, 2, 8 * gsz, chan), F32),
        ],
        compiler_params=pltpu.CompilerParams(vmem_limit_bytes=48 * 2**20),
        cost_estimate=pl.CostEstimate(flops=5 * 10**9, bytes_accessed=18 * 2**20, transcendentals=0),
        name="lift",
    )(owner, rim, features, w_conv, w_up)


def rim_kernel(grid_ref, out_ref, send_sems, recv_sems):
    gsx, gsy = grid_ref.shape[:2]
    gx, gy = lax.axis_index("gx"), lax.axis_index("gy")
    nx, ny = lax.axis_size("gx"), lax.axis_size("gy")
    sides = [(dx, dy) for dx in (-1, 0, 1) for dy in (-1, 0, 1) if (dx, dy) != (0, 0)]

    def device(dx, dy):
        return (lax.rem(gx + dx + nx, nx), lax.rem(gy + dy + ny, ny))

    barrier = pltpu.get_barrier_semaphore()
    for side in sides:
        pl.semaphore_signal(barrier, inc=1, device_id=device(*side), device_id_type=pl.DeviceIdType.MESH)
    pl.semaphore_wait(barrier, len(sides))

    def cut(side, size):
        return {-1: pl.ds(0, 1), 0: pl.ds(0, size), 1: pl.ds(size - 1, 1)}[side]

    def place(side, size):
        return {-1: pl.ds(size + 1, 1), 0: pl.ds(1, size), 1: pl.ds(0, 1)}[side]

    copies = []
    for n, (dx, dy) in enumerate(sides):
        copy = pltpu.make_async_remote_copy(
            src_ref=grid_ref.at[cut(dx, gsx), cut(dy, gsy)],
            dst_ref=out_ref.at[place(dx, gsx), place(dy, gsy)],
            send_sem=send_sems.at[n],
            recv_sem=recv_sems.at[n],
            device_id=device(dx, dy),
            device_id_type=pl.DeviceIdType.MESH,
        )
        copy.start()
        copies.append(copy)
    out_ref[pl.ds(1, gsx), pl.ds(1, gsy)] = grid_ref[...]
    for copy in copies:
        copy.wait()

    @pl.when(gx == 0)
    def _():
        out_ref[0] = jnp.zeros_like(out_ref[0])

    @pl.when(gx == nx - 1)
    def _():
        out_ref[gsx + 1] = jnp.zeros_like(out_ref[gsx + 1])

    @pl.when(gy == 0)
    def _():
        out_ref[:, 0] = jnp.zeros_like(out_ref[:, 0])

    @pl.when(gy == ny - 1)
    def _():
        out_ref[:, gsy + 1] = jnp.zeros_like(out_ref[:, gsy + 1])


def with_rim(grid):
    gsx, gsy, gsz, chan = grid.shape
    vmem = pl.BlockSpec(memory_space=pltpu.VMEM)
    return pl.pallas_call(
        rim_kernel,
        out_shape=jax.ShapeDtypeStruct((gsx + 2, gsy + 2, gsz, chan), BF16),
        in_specs=[vmem],
        out_specs=vmem,
        scratch_shapes=[pltpu.SemaphoreType.DMA((8,)), pltpu.SemaphoreType.DMA((8,))],
        compiler_params=pltpu.CompilerParams(
            collective_id=0, has_side_effects=True, vmem_limit_bytes=32 * 2**20
        ),
        name="rim",
    )(grid)


def local(features, owner, norm_gain, time_shift, w_in, w_out, w_down, w_conv, w_up):
    cols_x, cols_y, zcap, voxels, chan = features.shape
    flat = features.reshape(cols_x * cols_y * zcap, voxels, chan)
    grid = coarse_grid(flat, owner, norm_gain, time_shift, w_in, w_out, w_down)
    result = lift(owner, with_rim(grid), flat, w_conv, w_up)
    return result.reshape(features.shape)


def solution(mesh):
    in_specs = (
        P("gx", "gy", None, None, None),
        P("gx", "gy", None),
        P(),
        P(),
        P(),
        P(),
        P(),
        P(),
        P(),
    )
    out_specs = P("gx", "gy", None, None, None)
    return jax.shard_map(local, mesh=mesh, in_specs=in_specs, out_specs=out_specs, check_vma=False)
```

```python
import functools

import jax
import jax.numpy as jnp
from jax import lax
from jax.experimental import pallas as pl
from jax.experimental.pallas import tpu as pltpu
from jax.sharding import PartitionSpec as P

BF16 = jnp.bfloat16
F32 = jnp.float32
GROUP = 4
CHUNK = 512


def transposed(eye, block):
    return lax.dot_general(eye, block, (((1,), (1,)), ((), ())), preferred_element_type=F32)


def identity(n):
    rows = lax.broadcasted_iota(jnp.int32, (n, n), 0)
    return (rows == lax.broadcasted_iota(jnp.int32, (n, n), 1)).astype(BF16)


def prepare_weights(eye, gain_ref, shift_ref, w_in_ref, w_out_ref, wi_ref, wo_ref):
    layers, chan, hid = w_in_ref.shape
    row = lax.broadcasted_iota(jnp.int32, (chan, hid), 0)

    def one(l, _):
        gain = gain_ref[pl.ds(l, 1), :] * 0.5
        shift = shift_ref[pl.ds(l, 1), :] * 0.5
        high = shift.astype(BF16).astype(F32)
        mid = (shift - high).astype(BF16).astype(F32)
        low = shift - high - mid
        parts = jnp.where(row == 0, high, jnp.where(row == 1, mid, jnp.where(row == 2, low, 0.0))).astype(BF16)
        w_in = w_in_ref[l]
        w_out = w_out_ref[l]
        for m in range(hid // chan):
            cut = slice(m * chan, (m + 1) * chan)
            wi_ref[l, cut, :chan] = (transposed(eye, w_in[:, cut]) * gain).astype(BF16)
            wi_ref[l, cut, chan:] = transposed(eye, parts[:, cut]).astype(BF16)
            wo_ref[l, :, cut] = transposed(eye, w_out[cut, :]).astype(BF16)
        return 0

    lax.fori_loop(0, layers, one, 0)


def feed_forward(s_ref, wi_ref, wo_ref):
    layers = wi_ref.shape[0]
    chan, width = s_ref.shape
    count = width // CHUNK
    ones = jnp.ones((chan, CHUNK), BF16)

    def hidden(step):
        l, c = divmod(step, count)
        x = s_ref[:, c * CHUNK : (c + 1) * CHUNK]
        scale = lax.rsqrt(jnp.mean(x * x, axis=0, keepdims=True) + 1e-06)
        normed = jnp.concatenate([(x * scale).astype(BF16), ones], axis=0)
        u = jnp.dot(wi_ref[l], normed, preferred_element_type=F32)
        return (u * jnp.tanh(u) + u).astype(BF16)

    def update(step, h):
        l, c = divmod(step, count)
        s_ref[:, c * CHUNK : (c + 1) * CHUNK] += jnp.dot(wo_ref[l], h, preferred_element_type=F32)

    held = hidden(0)
    for step in range(layers * count):
        following = hidden(step + 1) if step + 1 < layers * count else None
        update(step, held)
        held = following


def list_kernel(owner_ref, list_ref, count_ref):
    cols_x, cols_y, zcap = owner_ref.shape
    slots = cols_x * cols_y * zcap

    def note(slot, n):
        column, r = slot // zcap, lax.rem(slot, zcap)
        alive = owner_ref[column // cols_y, lax.rem(column, cols_y), r] >= 0

        @pl.when(alive)
        def _():
            list_ref[n] = slot

        return n + alive.astype(jnp.int32)

    def clear(k, _):
        list_ref[k] = 0
        return 0

    lax.fori_loop(0, list_ref.shape[0], clear, 0)
    total = lax.fori_loop(0, slots, note, 0)
    list_ref[slots] = total
    count_ref[...] = jnp.full(count_ref.shape, total, jnp.int32)


def occupied(owner):
    return pl.pallas_call(
        list_kernel,
        out_shape=(jax.ShapeDtypeStruct((128,), jnp.int32), jax.ShapeDtypeStruct((8, 128), jnp.int32)),
        in_specs=[pl.BlockSpec(memory_space=pltpu.SMEM)],
        out_specs=(pl.BlockSpec(memory_space=pltpu.SMEM), pl.BlockSpec(memory_space=pltpu.VMEM)),
        name="occupied",
    )(owner)


PAIRS = ("x0", "y0", "z0", "x1", "y1", "z1", "c")
CAPS = {"c": 4}
NEAR = 3
SWEEPS = 3


def cap_of(name):
    return CAPS.get(name, NEAR)


BASES = {name: sum(cap_of(other) for other in PAIRS[:k]) for k, name in enumerate(PAIRS)}
PLACES = sum(cap_of(name) for name in PAIRS)


def partner_device(name):
    gx, gy = lax.axis_index("gx"), lax.axis_index("gy")
    if name == "c":
        return (gx + 1 - 2 * lax.rem(gx, 2), gy)
    parity = int(name[1])
    if name[0] == "x":
        sign = 1 - 2 * lax.rem(gx // 2 + parity, 2)
        return (lax.rem(gx + 2 * sign + 8, 8), gy)
    if name[0] == "y":
        sign = 1 - 2 * lax.rem(gy // 4 + parity, 2)
        return (gx, lax.rem(gy + 4 * sign + 16, 16))
    sign = 1 - 2 * lax.rem(lax.rem(gy, 4) + parity, 2)
    return (gx, (gy // 4) * 4 + lax.rem(lax.rem(gy, 4) + sign + 4, 4))


def make_plan(count):
    gx, gy = lax.axis_index("gx"), lax.axis_index("gy")
    ax = lax.rem(lax.broadcasted_iota(jnp.int32, count.shape, 0) + gx, 8)
    ay = lax.rem(lax.broadcasted_iota(jnp.int32, count.shape, 1) + gy, 16)
    core, x, y, z = lax.rem(ax, 2), ax // 2, ay // 4, lax.rem(ay, 4)

    def ahead(v, by, axis):
        return pltpu.roll(v, (-by) % v.shape[axis], axis)

    def partner(v, name, low):
        if name == "c":
            return jnp.where(low, ahead(v, 1, 0), ahead(v, -1, 0))
        if name[0] == "x":
            return jnp.where(low, ahead(v, 2, 0), ahead(v, -2, 0))
        if name[0] == "y":
            return jnp.where(low, ahead(v, 4, 1), ahead(v, -4, 1))
        if name == "z0":
            return jnp.where(low, ahead(v, 1, 1), ahead(v, -1, 1))
        up = jnp.where(z == 3, ahead(v, -3, 1), ahead(v, 1, 1))
        down = jnp.where(z == 0, ahead(v, 3, 1), ahead(v, -1, 1))
        return jnp.where(low, up, down)

    low = {"c": core == 0}
    for k in range(2):
        low.update({"x%d" % k: lax.rem(x, 2) == k, "y%d" % k: lax.rem(y, 2) == k, "z%d" % k: lax.rem(z, 2) == k})
    flow = {name: jnp.zeros_like(count) for name in PAIRS}
    load, spare = count, count
    order = ("c", "x0", "y0", "z0", "x1", "y1", "z1")
    for k in range(SWEEPS * len(order)):
        name = order[k % len(order)]
        up = k % 2
        given = flow[name]
        diff = load - partner(load, name, low[name])
        limit = jnp.maximum(given, 0) + spare
        want = given + jnp.where(low[name], (diff + up) >> 1, -((up - diff) >> 1))
        want = jnp.clip(want, -cap_of(name), cap_of(name))
        want = jnp.maximum(jnp.minimum(want, limit), -partner(limit, name, low[name]))
        spare = limit - jnp.maximum(want, 0)
        load = load + given - want
        flow[name] = want
    return flow


def spread_kernel(
    list_ref, count_ref, features_hbm, gain_ref, shift_ref, w_in_hbm, w_out_hbm,
    plan_ref, got_hbm, wi_hbm, wo_hbm,
    bricks_ref, send_ref, first_ref, second_ref, own_ref, plan_smem, w_in_ref, w_out_ref, wi_ref, wo_ref,
    sems, count_send, count_recv, brick_send, brick_recv,
):
    gx, gy = lax.axis_index("gx"), lax.axis_index("gy")
    eye = identity(w_out_ref.shape[2])
    load_bricks = pltpu.make_async_copy(features_hbm, bricks_ref, sems.at[0])
    load_in = pltpu.make_async_copy(w_in_hbm, w_in_ref, sems.at[1])
    load_out = pltpu.make_async_copy(w_out_hbm, w_out_ref, sems.at[2])
    load_in.start()
    load_out.start()
    load_bricks.start()

    along_x = [(lax.rem(gx + k, 8), gy) for k in range(1, 8)]
    along_y = [(gx, lax.rem(gy + k, 16)) for k in range(1, 16)]
    barrier = pltpu.get_barrier_semaphore()
    for device in along_x + along_y:
        pl.semaphore_signal(barrier, inc=1, device_id=device, device_id_type=pl.DeviceIdType.MESH)
    pl.semaphore_wait(barrier, len(along_x) + len(along_y))

    def send(src, dst, send_sem, recv_sem, device):
        copy = pltpu.make_async_remote_copy(
            src_ref=src, dst_ref=dst, send_sem=send_sem, recv_sem=recv_sem,
            device_id=device, device_id_type=pl.DeviceIdType.MESH,
        )
        copy.start()
        return copy

    copies = [
        send(count_ref, first_ref.at[k], count_send.at[k], count_recv.at[k], along_x[k - 1]) for k in range(1, 8)
    ]
    load_in.wait()
    load_out.wait()
    for copy in copies:
        copy.wait()
    row = lax.broadcasted_iota(jnp.int32, count_ref.shape, 0)
    lane = lax.rem(lax.broadcasted_iota(jnp.int32, count_ref.shape, 1), 16)
    column = count_ref[...]
    for k in range(1, 8):
        column = jnp.where(row == 8 - k, first_ref[k], column)
    own_ref[...] = column
    copies = [
        send(own_ref, second_ref.at[k], count_send.at[7 + k], count_recv.at[7 + k], along_y[k - 1])
        for k in range(1, 16)
    ]
    prepare_weights(eye, gain_ref, shift_ref, w_in_ref, w_out_ref, wi_ref, wo_ref)
    store_wi = pltpu.make_async_copy(wi_ref, wi_hbm, sems.at[1])
    store_wo = pltpu.make_async_copy(wo_ref, wo_hbm, sems.at[2])
    store_wi.start()
    store_wo.start()
    for copy in copies:
        copy.wait()
    counts = column
    for k in range(1, 16):
        counts = jnp.where(lane == 16 - k, second_ref[k], counts)

    flow = make_plan(counts)
    sent = jnp.zeros_like(counts)
    got = jnp.zeros_like(counts)
    for k, name in enumerate(PAIRS):
        sent = jnp.where(row == k, pltpu.roll(jnp.maximum(flow[name], 0), k, 0), sent)
        got = jnp.where(row == k, pltpu.roll(jnp.maximum(-flow[name], 0), k, 0), got)
    plan_ref[0:8, :] = sent
    plan_ref[8:16, :] = got
    to_smem = pltpu.make_async_copy(plan_ref, plan_smem, sems.at[3])
    to_smem.start()
    load_bricks.wait()
    to_smem.wait()

    last = list_ref[64] - 1
    copies = []
    for k, name in enumerate(PAIRS):
        for t in range(cap_of(name)):
            slot = list_ref[jnp.clip(last - t, 0, 63)]
            send_ref[BASES[name] + t] = bricks_ref[slot]
        last = last - plan_smem[k, 0]
        places = pl.ds(BASES[name], cap_of(name))
        copies.append(
            send(send_ref.at[places], got_hbm.at[places], brick_send.at[k], brick_recv.at[k], partner_device(name))
        )
    for copy in copies:
        copy.wait()
    store_wi.wait()
    store_wo.wait()


def spread(listed, count, features, gain, shift, w_in, w_out):
    slots, voxels, chan = features.shape
    layers, _, hid = w_in.shape
    vmem = pl.BlockSpec(memory_space=pltpu.VMEM)
    hbm = pl.BlockSpec(memory_space=pltpu.HBM)
    return pl.pallas_call(
        spread_kernel,
        out_shape=(
            jax.ShapeDtypeStruct((16, 128), jnp.int32),
            jax.ShapeDtypeStruct((PLACES, voxels, chan), BF16),
            jax.ShapeDtypeStruct((layers, hid, 2 * chan), BF16),
            jax.ShapeDtypeStruct((layers, chan, hid), BF16),
        ),
        in_specs=[pl.BlockSpec(memory_space=pltpu.SMEM), vmem, hbm, vmem, vmem, hbm, hbm],
        out_specs=(vmem, hbm, hbm, hbm),
        scratch_shapes=[
            pltpu.VMEM(features.shape, BF16),
            pltpu.VMEM((PLACES, voxels, chan), BF16),
            pltpu.VMEM((8, 8, 128), jnp.int32),
            pltpu.VMEM((16, 8, 128), jnp.int32),
            pltpu.VMEM((8, 128), jnp.int32),
            pltpu.SMEM((16, 128), jnp.int32),
            pltpu.VMEM(w_in.shape, BF16),
            pltpu.VMEM(w_out.shape, BF16),
            pltpu.VMEM((layers, hid, 2 * chan), BF16),
            pltpu.VMEM((layers, chan, hid), BF16),
            pltpu.SemaphoreType.DMA((4,)),
            pltpu.SemaphoreType.DMA((23,)),
            pltpu.SemaphoreType.DMA((23,)),
            pltpu.SemaphoreType.DMA((7,)),
            pltpu.SemaphoreType.DMA((7,)),
        ],
        compiler_params=pltpu.CompilerParams(
            collective_id=0, has_side_effects=True, vmem_limit_bytes=48 * 2**20
        ),
        name="spread",
    )(listed, count, features, gain, shift, w_in, w_out)


def coarse_kernel(
    list_ref, plan_ref, features_ref, got_ref, wi_hbm, wo_hbm, w_down_hbm,
    out_ref, back_ref, map_ref,
    place_ref, buf_ref, s_ref, t_ref, grid_ref, wi_ref, wo_ref, w_down_ref, sems, w_sems,
):
    zcap = 16
    chan = s_ref.shape[0]
    eye = identity(chan)
    weights = [
        pltpu.make_async_copy(src, dst, w_sems.at[n])
        for n, (src, dst) in enumerate(((wi_hbm, wi_ref), (wo_hbm, wo_ref), (w_down_hbm, w_down_ref)))
    ]
    for w in weights:
        w.start()

    def clear(k, _):
        map_ref[k] = -1
        return 0

    lax.fori_loop(0, map_ref.shape[0], clear, 0)
    kept, others = list_ref[64], 0
    for k, name in enumerate(PAIRS):
        sent, came = plan_ref[k, 0], plan_ref[8 + k, 0]
        for t in range(cap_of(name)):

            @pl.when(t < sent)
            def _():
                map_ref[list_ref[kept - 1 - t]] = BASES[name] + t

            @pl.when(t < came)
            def _():
                place_ref[others + t] = BASES[name] + t

        kept, others = kept - sent, others + came
    total = kept + others
    groups = (total + GROUP - 1) // GROUP

    def copies(g, t):
        k = jnp.minimum(g * GROUP + t, total - 1)
        half = lax.rem(g, 2)
        own = pltpu.make_async_copy(features_ref.at[list_ref[jnp.clip(k, 0, 63)]], buf_ref.at[half, t], sems.at[half, t])
        other = pltpu.make_async_copy(
            got_ref.at[place_ref[jnp.clip(k - kept, 0, PLACES - 1)]], buf_ref.at[half, t], sems.at[half, t]
        )
        return k, own, other

    def fetch(g):
        for t in range(GROUP):
            k, own, other = copies(g, t)

            @pl.when(k < kept)
            def _():
                own.start()

            @pl.when(k >= kept)
            def _():
                other.start()

    @pl.when(groups > 0)
    def _():
        fetch(0)

    grid_ref[...] = jnp.zeros_like(grid_ref)
    for w in weights:
        w.wait()
    half = lax.broadcasted_iota(jnp.int32, (16, 8, 1), 1) // 4

    def body(g, _):
        @pl.when(g + 1 < groups)
        def _():
            fetch(g + 1)

        for t in range(GROUP):
            pltpu.make_async_copy(features_ref.at[0], buf_ref.at[lax.rem(g, 2), t], sems.at[lax.rem(g, 2), t]).wait()
        for t in range(GROUP):
            s_ref[:, t * 512 : (t + 1) * 512] = transposed(eye, buf_ref[lax.rem(g, 2), t])
        feed_forward(s_ref, wi_ref, wo_ref)
        for t in range(GROUP):
            for m in range(4):
                block = s_ref[:, t * 512 + m * 128 : t * 512 + (m + 1) * 128].astype(BF16)
                t_ref[t, m * 128 : (m + 1) * 128, :] = transposed(eye, block)
        for t in range(GROUP):
            total_down = jnp.zeros((128, 2 * chan), F32)
            for a in range(2):
                for c in range(2):
                    rows = jnp.concatenate(
                        [t_ref[t, pl.ds(128 * i + 64 * a + c, 32, stride=2), :] for i in range(4)], axis=0
                    ).astype(BF16)
                    both_b = jnp.concatenate([w_down_ref[a, 0, c], w_down_ref[a, 1, c]], axis=1)
                    total_down += jnp.dot(rows, both_b, preferred_element_type=F32)
            both = total_down.reshape(16, 8, 2 * chan)
            own = jnp.where(half == 0, both[:, :, :chan], both[:, :, chan:])
            down = own + jnp.concatenate([own[:, 4:, :], own[:, :4, :]], axis=1)
            made = down / (1.0 + jnp.exp(-down))
            k = g * GROUP + t

            @pl.when(k < kept)
            def _():
                slot = list_ref[jnp.minimum(k, 63)]
                column, r = slot // zcap, lax.rem(slot, zcap)
                x0, y0, zpair, odd = (column // 2) * 4, lax.rem(column, 2) * 4, r // 2, lax.rem(r, 2)
                for i in range(4):
                    for j in range(4):
                        old = grid_ref[x0 + i, y0 + j, zpair]
                        grid_ref[x0 + i, y0 + j, zpair] = jnp.where(half[0] == odd, made[4 * i + j], old)

            @pl.when((k >= kept) & (k < total))
            def _():
                place = place_ref[jnp.clip(k - kept, 0, PLACES - 1)]
                back_ref[place] = made.reshape(128, chan).astype(BF16)

        return 0

    lax.fori_loop(0, groups, body, 0)

    def finish(x, _):
        out_ref[x] = grid_ref[x].reshape(out_ref.shape[1:]).astype(BF16)
        return 0

    lax.fori_loop(0, out_ref.shape[0], finish, 0)


def coarse_grid(listed, plan, features, got, wi, wo, w_down):
    slots, voxels, chan = features.shape
    vmem = pl.BlockSpec(memory_space=pltpu.VMEM)
    hbm = pl.BlockSpec(memory_space=pltpu.HBM)
    smem = pl.BlockSpec(memory_space=pltpu.SMEM)
    return pl.pallas_call(
        coarse_kernel,
        out_shape=(
            jax.ShapeDtypeStruct((8, 8, slots, chan), BF16),
            jax.ShapeDtypeStruct((PLACES, 128, chan), BF16),
            jax.ShapeDtypeStruct((slots,), jnp.int32),
        ),
        in_specs=[smem, smem, hbm, hbm, hbm, hbm, hbm],
        out_specs=(vmem, vmem, smem),
        scratch_shapes=[
            pltpu.SMEM((PLACES,), jnp.int32),
            pltpu.VMEM((2, GROUP, voxels, chan), BF16),
            pltpu.VMEM((chan, GROUP * voxels), F32),
            pltpu.VMEM((GROUP, voxels, chan), F32),
            pltpu.VMEM((8, 8, slots // 8, 8, chan), F32),
            pltpu.VMEM(wi.shape, BF16),
            pltpu.VMEM(wo.shape, BF16),
            pltpu.VMEM(w_down.shape, BF16),
            pltpu.SemaphoreType.DMA((2, GROUP)),
            pltpu.SemaphoreType.DMA((3,)),
        ],
        compiler_params=pltpu.CompilerParams(vmem_limit_bytes=48 * 2**20),
        cost_estimate=pl.CostEstimate(flops=17 * 10**9, bytes_accessed=8 * 2**20, transcendentals=10**8),
        name="coarse",
    )(listed, plan, features, got, wi, wo, w_down)


def lift_kernel(
    owner_ref, rim_ref, features_ref, w_conv_ref, w_up_ref,
    out_ref,
    wc_ref, a_ref,
):
    chan = rim_ref.shape[-1]
    gsz = rim_ref.shape[2]
    zcap = owner_ref.shape[2]
    step = pl.program_id(0)
    p, q = step // 2, lax.rem(step, 2)

    @pl.when(step == 0)
    def _():
        empty = jnp.zeros((chan, chan), BF16)
        for d in range(3):
            for k in range(4):
                for o in range(2):
                    e = k - o
                    for f in range(3):
                        col = (2 * f + o) * chan
                        wc_ref[d, k * chan : (k + 1) * chan, col : col + chan] = (
                            w_conv_ref[d, e, f] if 0 <= e <= 2 else empty
                        )
        a_ref[...] = jnp.zeros_like(a_ref)

    x0, y0 = p * 4, q * 4
    live = jnp.concatenate(
        [jnp.full((1, 16, chan), (owner_ref[p, q, r] >= 0).astype(F32)) for r in range(zcap)], axis=0
    )
    z = lax.rem(lax.broadcasted_iota(jnp.int32, (4 * gsz, 2 * chan), 0), gsz)
    for pair in range(2):
        y = y0 + 2 * pair
        total = jnp.zeros((4 * gsz, 6 * chan), F32)
        for d in range(3):
            rows = jnp.concatenate(
                [rim_ref[pl.ds(x0 + d, 4), y + k].reshape(4 * gsz, chan) for k in range(4)], axis=1
            )
            total += jnp.dot(rows, wc_ref[d], preferred_element_type=F32)
        below = pltpu.roll(total[:, : 2 * chan], 1, 0)
        above = pltpu.roll(total[:, 4 * chan :], 4 * gsz - 1, 0)
        summed = total[:, 2 * chan : 4 * chan] + jnp.where(z == 0, 0.0, below) + jnp.where(z == gsz - 1, 0.0, above)
        for o in range(2):
            own = rim_ref[pl.ds(x0 + 1, 4), y + o + 1].reshape(4 * gsz, chan).astype(F32)
            mixed = summed[:, o * chan : (o + 1) * chan] + own
            j = 2 * pair + o
            a_ref[j, 0, pl.ds(0, 4 * gsz, stride=2), :] = mixed
            a_ref[j, 1, pl.ds(1, 4 * gsz, stride=2), :] = mixed
            spread = jnp.concatenate([a_ref[j, 0], a_ref[j, 1]], axis=1).astype(BF16)
            for a in range(2):
                weights = jnp.concatenate(
                    [jnp.concatenate([w_up_ref[a, b, c] for b in range(2)], axis=1) for c in range(2)], axis=0
                )
                upward = jnp.dot(spread, weights, preferred_element_type=F32)
                for i in range(4):
                    part = upward[2 * gsz * i : 2 * gsz * (i + 1)].reshape(gsz // 4, 8, 2 * chan)
                    part = jnp.concatenate([part[:, :, :chan], part[:, :, chan:]], axis=1)
                    base = 128 * i + 64 * a + 16 * j
                    given = features_ref[:, base : base + 16, :].astype(F32)
                    out_ref[:, base : base + 16, :] = ((given + part) * live).astype(BF16)


def lift(owner, rim, features, w_conv, w_up):
    slots, voxels, chan = features.shape
    gsz = rim.shape[2]
    columns = 4
    vmem = pl.BlockSpec(memory_space=pltpu.VMEM)
    block = pl.BlockSpec((slots // columns, voxels, chan), lambda s: (s, 0, 0))
    return pl.pallas_call(
        lift_kernel,
        grid=(columns,),
        out_shape=jax.ShapeDtypeStruct(features.shape, BF16),
        in_specs=[pl.BlockSpec(memory_space=pltpu.SMEM), vmem, block, vmem, vmem],
        out_specs=block,
        scratch_shapes=[
            pltpu.VMEM((3, 4 * chan, 6 * chan), BF16),
            pltpu.VMEM((4, 2, 8 * gsz, chan), F32),
        ],
        compiler_params=pltpu.CompilerParams(vmem_limit_bytes=48 * 2**20),
        cost_estimate=pl.CostEstimate(flops=5 * 10**9, bytes_accessed=18 * 2**20, transcendentals=0),
        name="lift",
    )(owner, rim, features, w_conv, w_up)


def rim_kernel(
    map_ref, grid_ref, back_ref,
    out_ref,
    whole_ref, home_ref, send_sems, recv_sems,
):
    gsx, gsy, gsz, chan = grid_ref.shape
    gx, gy = lax.axis_index("gx"), lax.axis_index("gy")
    nx, ny = lax.axis_size("gx"), lax.axis_size("gy")
    sides = [(dx, dy) for dx in (-1, 0, 1) for dy in (-1, 0, 1) if (dx, dy) != (0, 0)]
    devices = [(lax.rem(gx + dx + nx, nx), lax.rem(gy + dy + ny, ny)) for dx, dy in sides]
    partners = [partner_device(name) for name in PAIRS]

    barrier = pltpu.get_barrier_semaphore()
    for device in devices + partners:
        pl.semaphore_signal(barrier, inc=1, device_id=device, device_id_type=pl.DeviceIdType.MESH)
    pl.semaphore_wait(barrier, len(devices) + len(partners))

    def send(n, src, dst, device):
        copy = pltpu.make_async_remote_copy(
            src_ref=src, dst_ref=dst, send_sem=send_sems.at[n], recv_sem=recv_sems.at[n],
            device_id=device, device_id_type=pl.DeviceIdType.MESH,
        )
        copy.start()
        return copy

    copies = []
    for k, name in enumerate(PAIRS):
        places = pl.ds(BASES[name], cap_of(name))
        copies.append(send(len(sides) + k, back_ref.at[places], home_ref.at[places], partners[k]))
    for copy in copies:
        copy.wait()

    odd = lax.broadcasted_iota(jnp.int32, (16, 8, chan), 1) // 4
    for column in range(4):
        x0, y0 = (column // 2) * 4, (column % 2) * 4

        def merge(m, _):
            zs = pl.ds(pl.multiple_of(m * 16, 16), 16)
            old = grid_ref[x0 : x0 + 4, y0 : y0 + 4, zs, :].astype(F32).reshape(16, 16, chan)
            new = []
            for pair in range(2):
                value = old[:, 8 * pair : 8 * pair + 8, :]
                for side in range(2):
                    place = map_ref[column * 16 + m * 4 + 2 * pair + side]
                    brick = home_ref[jnp.maximum(place, 0)].astype(F32).reshape(16, 8, chan)
                    taken = jnp.full((16, 8, chan), place, jnp.int32) >= 0
                    value = jnp.where(taken & (odd == side), brick, value)
                new.append(value)
            merged = jnp.concatenate(new, axis=1).reshape(4, 4, 16, chan).astype(BF16)
            whole_ref[x0 : x0 + 4, y0 : y0 + 4, zs, :] = merged
            return 0

        lax.fori_loop(0, gsz // 16, merge, 0)

    def cut(side, size):
        return {-1: pl.ds(0, 1), 0: pl.ds(0, size), 1: pl.ds(size - 1, 1)}[side]

    def place_of(side, size):
        return {-1: pl.ds(size + 1, 1), 0: pl.ds(1, size), 1: pl.ds(0, 1)}[side]

    copies = [
        send(
            n,
            whole_ref.at[cut(dx, gsx), cut(dy, gsy)],
            out_ref.at[place_of(dx, gsx), place_of(dy, gsy)],
            devices[n],
        )
        for n, (dx, dy) in enumerate(sides)
    ]
    out_ref[pl.ds(1, gsx), pl.ds(1, gsy)] = whole_ref[...]
    for copy in copies:
        copy.wait()

    @pl.when(gx == 0)
    def _():
        out_ref[0] = jnp.zeros_like(out_ref[0])

    @pl.when(gx == nx - 1)
    def _():
        out_ref[gsx + 1] = jnp.zeros_like(out_ref[gsx + 1])

    @pl.when(gy == 0)
    def _():
        out_ref[:, 0] = jnp.zeros_like(out_ref[:, 0])

    @pl.when(gy == ny - 1)
    def _():
        out_ref[:, gsy + 1] = jnp.zeros_like(out_ref[:, gsy + 1])


def with_rim(where, grid, back):
    gsx, gsy, gsz, chan = grid.shape
    vmem = pl.BlockSpec(memory_space=pltpu.VMEM)
    return pl.pallas_call(
        rim_kernel,
        out_shape=jax.ShapeDtypeStruct((gsx + 2, gsy + 2, gsz, chan), BF16),
        in_specs=[pl.BlockSpec(memory_space=pltpu.SMEM), vmem, vmem],
        out_specs=vmem,
        scratch_shapes=[
            pltpu.VMEM(grid.shape, BF16),
            pltpu.VMEM(back.shape, BF16),
            pltpu.SemaphoreType.DMA((15,)),
            pltpu.SemaphoreType.DMA((15,)),
        ],
        compiler_params=pltpu.CompilerParams(
            collective_id=1, has_side_effects=True, vmem_limit_bytes=32 * 2**20
        ),
        name="rim",
    )(where, grid, back)


def local(features, owner, norm_gain, time_shift, w_in, w_out, w_down, w_conv, w_up):
    cols_x, cols_y, zcap, voxels, chan = features.shape
    flat = features.reshape(cols_x * cols_y * zcap, voxels, chan)
    listed, count = occupied(owner)
    plan, got, wi, wo = spread(listed, count, flat, norm_gain, time_shift, w_in, w_out)
    grid, back, where = coarse_grid(listed, plan, flat, got, wi, wo, w_down)
    result = lift(owner, with_rim(where, grid, back), flat, w_conv, w_up)
    return result.reshape(features.shape)


def solution(mesh):
    in_specs = (
        P("gx", "gy", None, None, None),
        P("gx", "gy", None),
        P(),
        P(),
        P(),
        P(),
        P(),
        P(),
        P(),
    )
    out_specs = P("gx", "gy", None, None, None)
    return jax.shard_map(local, mesh=mesh, in_specs=in_specs, out_specs=out_specs, check_vma=False)
```

```python
import functools

import jax
import jax.numpy as jnp
from jax import lax
from jax.experimental import pallas as pl
from jax.experimental.pallas import tpu as pltpu
from jax.sharding import PartitionSpec as P

BF16 = jnp.bfloat16
F32 = jnp.float32
GROUP = 3
CHUNK = 512


def transposed(eye, block):
    return lax.dot_general(eye, block, (((1,), (1,)), ((), ())), preferred_element_type=F32)


def identity(n):
    rows = lax.broadcasted_iota(jnp.int32, (n, n), 0)
    return (rows == lax.broadcasted_iota(jnp.int32, (n, n), 1)).astype(BF16)


def prepare_weights(first, last, eye, gain_ref, shift_ref, w_in_ref, w_out_ref, wi_ref, wo_ref):
    _, chan, hid = w_in_ref.shape
    row = lax.broadcasted_iota(jnp.int32, (chan, hid), 0)

    def one(l, _):
        gain = gain_ref[pl.ds(l, 1), :] * 0.5
        shift = shift_ref[pl.ds(l, 1), :] * 0.5
        high = shift.astype(BF16).astype(F32)
        mid = (shift - high).astype(BF16).astype(F32)
        low = shift - high - mid
        parts = jnp.where(row == 0, high, jnp.where(row == 1, mid, jnp.where(row == 2, low, 0.0))).astype(BF16)
        w_in = w_in_ref[l]
        w_out = w_out_ref[l]
        for m in range(hid // chan):
            cut = slice(m * chan, (m + 1) * chan)
            wi_ref[l, cut, :chan] = (transposed(eye, w_in[:, cut]) * gain).astype(BF16)
            wi_ref[l, cut, chan:] = transposed(eye, parts[:, cut]).astype(BF16)
            wo_ref[l, :, cut] = transposed(eye, w_out[cut, :]).astype(BF16)
        return 0

    lax.fori_loop(first, last, one, 0)


def hidden_units(x, ones, wi):
    scale = lax.rsqrt(jnp.mean(x * x, axis=0, keepdims=True) + 1e-06)
    normed = jnp.concatenate([(x * scale).astype(BF16), ones], axis=0)
    u = jnp.dot(wi, normed, preferred_element_type=F32)
    return (u * jnp.tanh(u) + u).astype(BF16)


def feed_forward(s_ref, wi_ref, wo_ref, unrolled):
    layers = wi_ref.shape[0]
    chan, width = s_ref.shape
    count = width // CHUNK
    ones = jnp.ones((chan, CHUNK), BF16)

    def hidden(l, c):
        return hidden_units(s_ref[:, c * CHUNK : (c + 1) * CHUNK], ones, wi_ref[l])

    def update(l, c, h):
        s_ref[:, c * CHUNK : (c + 1) * CHUNK] += jnp.dot(wo_ref[l], h, preferred_element_type=F32)

    def run(steps):
        held = hidden(*steps[0])
        for k, step in enumerate(steps):
            following = hidden(*steps[k + 1]) if k + 1 < len(steps) else None
            update(*step, held)
            held = following

    if unrolled:
        run([divmod(step, count) for step in range(layers * count)])
    else:

        def layer(l, _):
            run([(l, c) for c in range(count)])
            return 0

        lax.fori_loop(0, layers, layer, 0)


def reduced(t, eye, s_ref, t_ref, w_down_ref):
    chan = s_ref.shape[0]
    half = lax.broadcasted_iota(jnp.int32, (16, 8, 1), 1) // 4
    for m in range(4):
        block = s_ref[:, t * 512 + m * 128 : t * 512 + (m + 1) * 128].astype(BF16)
        t_ref[t, m * 128 : (m + 1) * 128, :] = transposed(eye, block)
    total = jnp.zeros((128, 2 * chan), F32)
    for a in range(2):
        for c in range(2):
            rows = jnp.concatenate(
                [t_ref[t, pl.ds(128 * i + 64 * a + c, 32, stride=2), :] for i in range(4)], axis=0
            ).astype(BF16)
            both_b = jnp.concatenate([w_down_ref[a, 0, c], w_down_ref[a, 1, c]], axis=1)
            total += jnp.dot(rows, both_b, preferred_element_type=F32)
    both = total.reshape(16, 8, 2 * chan)
    own = jnp.where(half == 0, both[:, :, :chan], both[:, :, chan:])
    down = own + jnp.concatenate([own[:, 4:, :], own[:, :4, :]], axis=1)
    return down / (1.0 + jnp.exp(-down))


PAIRS = ("x0", "y0", "z0", "x1", "y1", "z1", "c")
CAPS = {"c": 4}
NEAR = 3
SWEEPS = 3
FULL_VMEM = 127 * 2**19


def cap_of(name):
    return CAPS.get(name, NEAR)


BASES = {name: sum(cap_of(other) for other in PAIRS[:k]) for k, name in enumerate(PAIRS)}
PLACES = sum(cap_of(name) for name in PAIRS)


def partner_device(name):
    gx, gy = lax.axis_index("gx"), lax.axis_index("gy")
    if name == "c":
        return (gx + 1 - 2 * lax.rem(gx, 2), gy)
    parity = int(name[1])
    if name[0] == "x":
        sign = 1 - 2 * lax.rem(gx // 2 + parity, 2)
        return (lax.rem(gx + 2 * sign + 8, 8), gy)
    if name[0] == "y":
        sign = 1 - 2 * lax.rem(gy // 4 + parity, 2)
        return (gx, lax.rem(gy + 4 * sign + 16, 16))
    sign = 1 - 2 * lax.rem(lax.rem(gy, 4) + parity, 2)
    return (gx, (gy // 4) * 4 + lax.rem(lax.rem(gy, 4) + sign + 4, 4))


def make_plan(count):
    gx, gy = lax.axis_index("gx"), lax.axis_index("gy")
    ax = lax.rem(lax.broadcasted_iota(jnp.int32, count.shape, 0) + gx, 8)
    ay = lax.rem(lax.broadcasted_iota(jnp.int32, count.shape, 1) + gy, 16)
    core, x, y, z = lax.rem(ax, 2), ax // 2, ay // 4, lax.rem(ay, 4)

    def ahead(v, by, axis):
        return pltpu.roll(v, (-by) % v.shape[axis], axis)

    def partner(v, name, low):
        if name == "c":
            return jnp.where(low, ahead(v, 1, 0), ahead(v, -1, 0))
        if name[0] == "x":
            return jnp.where(low, ahead(v, 2, 0), ahead(v, -2, 0))
        if name[0] == "y":
            return jnp.where(low, ahead(v, 4, 1), ahead(v, -4, 1))
        if name == "z0":
            return jnp.where(low, ahead(v, 1, 1), ahead(v, -1, 1))
        up = jnp.where(z == 3, ahead(v, -3, 1), ahead(v, 1, 1))
        down = jnp.where(z == 0, ahead(v, 3, 1), ahead(v, -1, 1))
        return jnp.where(low, up, down)

    low = {"c": core == 0}
    for k in range(2):
        low.update({"x%d" % k: lax.rem(x, 2) == k, "y%d" % k: lax.rem(y, 2) == k, "z%d" % k: lax.rem(z, 2) == k})
    flow = {name: jnp.zeros_like(count) for name in PAIRS}
    load, spare = count, count
    order = ("c", "x0", "y0", "z0", "x1", "y1", "z1")
    for k in range(SWEEPS * len(order)):
        name = order[k % len(order)]
        up = k % 2
        given = flow[name]
        diff = load - partner(load, name, low[name])
        limit = jnp.maximum(given, 0) + spare
        want = given + jnp.where(low[name], (diff + up) >> 1, -((up - diff) >> 1))
        want = jnp.clip(want, -cap_of(name), cap_of(name))
        want = jnp.maximum(jnp.minimum(want, limit), -partner(limit, name, low[name]))
        spare = limit - jnp.maximum(want, 0)
        load = load + given - want
        flow[name] = want
    return flow


def spread_kernel(
    owner_ref, features_hbm, gain_hbm, shift_hbm, w_in_hbm, w_out_hbm, w_down_hbm,
    plan_ref, early_ref, got_hbm, wi_hbm, wo_hbm,
    bricks_ref, send_ref, count_ref, first_ref, second_ref, own_ref, pick_ref, pick_smem,
    gain_ref, shift_ref, w_in_ref, w_out_ref, w_down_ref, wi_ref, wo_ref, s_ref, t_ref,
    sems, count_send, count_recv, brick_send, brick_recv,
):
    gx, gy = lax.axis_index("gx"), lax.axis_index("gy")
    cols_x, cols_y, zcap = owner_ref.shape
    layers = w_in_ref.shape[0]
    eye = identity(w_out_ref.shape[2])
    loads = [
        pltpu.make_async_copy(src, dst, sems.at[n])
        for n, (src, dst) in enumerate(
            (
                (gain_hbm, gain_ref),
                (shift_hbm, shift_ref),
                (w_in_hbm, w_in_ref),
                (w_out_hbm, w_out_ref),
                (w_down_hbm, w_down_ref),
                (features_hbm, bricks_ref),
            )
        )
    ]
    for load in loads:
        load.start()

    along_x = [(lax.rem(gx + k, 8), gy) for k in range(1, 8)]
    along_y = [(gx, lax.rem(gy + k, 16)) for k in range(1, 16)]
    barrier = pltpu.get_barrier_semaphore()
    for device in along_x + along_y:
        pl.semaphore_signal(barrier, inc=1, device_id=device, device_id_type=pl.DeviceIdType.MESH)

    row = lax.broadcasted_iota(jnp.int32, count_ref.shape, 0)
    lane = lax.broadcasted_iota(jnp.int32, count_ref.shape, 1)
    alive = jnp.zeros_like(lane)
    total = 0
    for slot in range(cols_x * cols_y * zcap):
        column, r = divmod(slot, zcap)
        mark = (owner_ref[column // cols_y, column % cols_y, r] >= 0).astype(jnp.int32)
        alive = jnp.where(lane == slot, mark, alive)
        total = total + mark
    order = alive
    for by in (1, 2, 4, 8, 16, 32):
        order = order + jnp.where(lane >= by, pltpu.roll(order, by, 1), 0)
    order = order - alive
    count_ref[...] = jnp.full(count_ref.shape, total, jnp.int32)
    pl.semaphore_wait(barrier, len(along_x) + len(along_y))

    def send(src, dst, send_sem, recv_sem, device):
        copy = pltpu.make_async_remote_copy(
            src_ref=src, dst_ref=dst, send_sem=send_sem, recv_sem=recv_sem,
            device_id=device, device_id_type=pl.DeviceIdType.MESH,
        )
        copy.start()
        return copy

    copies = [
        send(count_ref, first_ref.at[k], count_send.at[k], count_recv.at[k], along_x[k - 1]) for k in range(1, 8)
    ]
    for load in loads[:5]:
        load.wait()
    prepare_weights(0, layers // 2, eye, gain_ref, shift_ref, w_in_ref, w_out_ref, wi_ref, wo_ref)
    for copy in copies:
        copy.wait()
    column = count_ref[...]
    for k in range(1, 8):
        column = jnp.where(row == 8 - k, first_ref[k], column)
    own_ref[...] = column
    copies = [
        send(own_ref, second_ref.at[k], count_send.at[7 + k], count_recv.at[7 + k], along_y[k - 1])
        for k in range(1, 16)
    ]
    prepare_weights(layers // 2, layers, eye, gain_ref, shift_ref, w_in_ref, w_out_ref, wi_ref, wo_ref)
    stores = [
        pltpu.make_async_copy(wi_ref, wi_hbm, sems.at[2]),
        pltpu.make_async_copy(wo_ref, wo_hbm, sems.at[3]),
    ]
    for store in stores:
        store.start()
    for copy in copies:
        copy.wait()
    counts = column
    for k in range(1, 16):
        counts = jnp.where(lax.rem(lane, 16) == 16 - k, second_ref[k], counts)

    flow = make_plan(jnp.maximum(counts - GROUP, 0))
    sent = jnp.zeros_like(counts)
    got = jnp.zeros_like(counts)
    places = lax.broadcasted_iota(jnp.int32, pick_ref.shape, 0)
    want = places - PLACES
    left = jnp.full((1, 1), total, jnp.int32)
    for k, name in enumerate(PAIRS):
        leaving = jnp.maximum(flow[name], 0)
        sent = jnp.where(row == k, pltpu.roll(leaving, k, 0), sent)
        got = jnp.where(row == k, pltpu.roll(jnp.maximum(-flow[name], 0), k, 0), got)
        base = BASES[name]
        here = (places >= base) & (places < base + cap_of(name))
        want = jnp.where(here, jnp.broadcast_to(left - 1, want.shape) - (places - base), want)
        left = left - leaving[0:1, 0:1]
    plan_ref[0:8, :] = sent
    plan_ref[8:16, :] = got
    repeat = pick_ref.shape[0] // 8
    hit = (jnp.concatenate([order] * repeat, axis=0) == want) & (jnp.concatenate([alive] * repeat, axis=0) > 0)
    pick = jnp.where(hit, jnp.concatenate([lane] * repeat, axis=0), 0)
    for by in (1, 2, 4, 8, 16, 32, 64):
        pick = pick + pltpu.roll(pick, by, 1)
    pick_ref[...] = pick
    to_smem = pltpu.make_async_copy(pick_ref, pick_smem, sems.at[0])
    to_smem.start()
    loads[5].wait()
    to_smem.wait()

    copies = []
    for k, name in enumerate(PAIRS):
        for t in range(cap_of(name)):
            send_ref[BASES[name] + t] = bricks_ref[pick_smem[BASES[name] + t, 0]]
        part = pl.ds(BASES[name], cap_of(name))
        copies.append(
            send(send_ref.at[part], got_hbm.at[part], brick_send.at[k], brick_recv.at[k], partner_device(name))
        )
    for t in range(GROUP):
        s_ref[:, t * 512 : (t + 1) * 512] = transposed(eye, bricks_ref[pick_smem[PLACES + t, 0]])
    feed_forward(s_ref, wi_ref, wo_ref, False)
    for t in range(GROUP):
        made = reduced(t, eye, s_ref, t_ref, w_down_ref)
        early_ref[t] = made.reshape(early_ref.shape[1:]).astype(BF16)
    for copy in copies:
        copy.wait()
    for store in stores:
        store.wait()


def spread(owner, features, gain, shift, w_in, w_out, w_down):
    slots, voxels, chan = features.shape
    layers, _, hid = w_in.shape
    vmem = pl.BlockSpec(memory_space=pltpu.VMEM)
    hbm = pl.BlockSpec(memory_space=pltpu.HBM)
    return pl.pallas_call(
        spread_kernel,
        out_shape=(
            jax.ShapeDtypeStruct((16, 128), jnp.int32),
            jax.ShapeDtypeStruct((GROUP, 128, chan), BF16),
            jax.ShapeDtypeStruct((PLACES, voxels, chan), BF16),
            jax.ShapeDtypeStruct((layers, hid, 2 * chan), BF16),
            jax.ShapeDtypeStruct((layers, chan, hid), BF16),
        ),
        in_specs=[pl.BlockSpec(memory_space=pltpu.SMEM)] + [hbm] * 6,
        out_specs=(vmem, vmem, hbm, hbm, hbm),
        scratch_shapes=[
            pltpu.VMEM(features.shape, BF16),
            pltpu.VMEM((PLACES, voxels, chan), BF16),
            pltpu.VMEM((8, 128), jnp.int32),
            pltpu.VMEM((8, 8, 128), jnp.int32),
            pltpu.VMEM((16, 8, 128), jnp.int32),
            pltpu.VMEM((8, 128), jnp.int32),
            pltpu.VMEM((32, 128), jnp.int32),
            pltpu.SMEM((32, 128), jnp.int32),
            pltpu.VMEM(gain.shape, F32),
            pltpu.VMEM(shift.shape, F32),
            pltpu.VMEM(w_in.shape, BF16),
            pltpu.VMEM(w_out.shape, BF16),
            pltpu.VMEM(w_down.shape, BF16),
            pltpu.VMEM((layers, hid, 2 * chan), BF16),
            pltpu.VMEM((layers, chan, hid), BF16),
            pltpu.VMEM((chan, GROUP * voxels), F32),
            pltpu.VMEM((GROUP, voxels, chan), F32),
            pltpu.SemaphoreType.DMA((6,)),
            pltpu.SemaphoreType.DMA((23,)),
            pltpu.SemaphoreType.DMA((23,)),
            pltpu.SemaphoreType.DMA((7,)),
            pltpu.SemaphoreType.DMA((7,)),
        ],
        compiler_params=pltpu.CompilerParams(
            collective_id=0, has_side_effects=True, vmem_limit_bytes=FULL_VMEM
        ),
        name="spread",
    )(owner, features, gain, shift, w_in, w_out, w_down)


def coarse_kernel(
    owner_ref, plan_ref, early_ref, features_ref, got_ref, wi_hbm, wo_hbm, w_down_hbm,
    out_ref, back_ref, map_ref,
    list_ref, place_ref, buf_ref, s_ref, t_ref, grid_ref, wi_ref, wo_ref, w_down_ref, sems, w_sems,
):
    cols_x, cols_y, zcap = owner_ref.shape
    slots = cols_x * cols_y * zcap
    chan = s_ref.shape[0]
    eye = identity(chan)
    weights = [
        pltpu.make_async_copy(src, dst, w_sems.at[n])
        for n, (src, dst) in enumerate(((wi_hbm, wi_ref), (wo_hbm, wo_ref), (w_down_hbm, w_down_ref)))
    ]
    for w in weights:
        w.start()

    total = 0
    for slot in range(slots):
        column, r = divmod(slot, zcap)
        map_ref[slot] = -1
        list_ref[total] = slot
        total = total + (owner_ref[column // cols_y, column % cols_y, r] >= 0).astype(jnp.int32)
    kept, others = total, 0
    for k, name in enumerate(PAIRS):
        sent, came = plan_ref[k, 0], plan_ref[8 + k, 0]
        for t in range(cap_of(name)):

            @pl.when(t < sent)
            def _():
                map_ref[list_ref[kept - 1 - t]] = BASES[name] + t

            @pl.when(t < came)
            def _():
                place_ref[others + t] = BASES[name] + t

        kept, others = kept - sent, others + came
    ours = jnp.maximum(kept - GROUP, 0)
    work = ours + others
    groups = (work + GROUP - 1) // GROUP

    def fetch(g):
        half = lax.rem(g, 2)
        for t in range(GROUP):
            k = jnp.minimum(g * GROUP + t, work - 1)

            @pl.when(k < ours)
            def _():
                slot = list_ref[GROUP + k]
                pltpu.make_async_copy(features_ref.at[slot], buf_ref.at[half, t], sems.at[half, t]).start()

            @pl.when(k >= ours)
            def _():
                place = place_ref[k - ours]
                pltpu.make_async_copy(got_ref.at[place], buf_ref.at[half, t], sems.at[half, t]).start()

    @pl.when(groups > 0)
    def _():
        fetch(0)

    grid_ref[...] = jnp.zeros_like(grid_ref)
    side = lax.broadcasted_iota(jnp.int32, (8, 1), 0) // 4

    def put(slot, made):
        column, r = slot // zcap, lax.rem(slot, zcap)
        x0, y0, zpair, odd = (column // 2) * 4, lax.rem(column, 2) * 4, r // 2, lax.rem(r, 2)
        for i in range(4):
            for j in range(4):
                old = grid_ref[x0 + i, y0 + j, zpair]
                grid_ref[x0 + i, y0 + j, zpair] = jnp.where(side == odd, made[4 * i + j], old)

    for t in range(GROUP):

        @pl.when(t < total)
        def _():
            put(list_ref[t], early_ref[t].astype(F32).reshape(16, 8, chan))

    for w in weights:
        w.wait()

    def body(g, _):
        @pl.when(g + 1 < groups)
        def _():
            fetch(g + 1)

        for t in range(GROUP):
            pltpu.make_async_copy(features_ref.at[0], buf_ref.at[lax.rem(g, 2), t], sems.at[lax.rem(g, 2), t]).wait()
        for t in range(GROUP):
            s_ref[:, t * 512 : (t + 1) * 512] = transposed(eye, buf_ref[lax.rem(g, 2), t])
        feed_forward(s_ref, wi_ref, wo_ref, True)
        for t in range(GROUP):
            made = reduced(t, eye, s_ref, t_ref, w_down_ref)
            k = g * GROUP + t

            @pl.when(k < ours)
            def _():
                put(list_ref[GROUP + k], made)

            @pl.when((k >= ours) & (k < work))
            def _():
                back_ref[place_ref[k - ours]] = made.reshape(128, chan).astype(BF16)

        return 0

    lax.fori_loop(0, groups, body, 0)

    def finish(x, _):
        out_ref[x] = grid_ref[x].reshape(out_ref.shape[1:]).astype(BF16)
        return 0

    lax.fori_loop(0, out_ref.shape[0], finish, 0)


def coarse_grid(owner, plan, early, features, got, wi, wo, w_down):
    slots, voxels, chan = features.shape
    vmem = pl.BlockSpec(memory_space=pltpu.VMEM)
    hbm = pl.BlockSpec(memory_space=pltpu.HBM)
    smem = pl.BlockSpec(memory_space=pltpu.SMEM)
    return pl.pallas_call(
        coarse_kernel,
        out_shape=(
            jax.ShapeDtypeStruct((8, 8, slots, chan), BF16),
            jax.ShapeDtypeStruct((PLACES, 128, chan), BF16),
            jax.ShapeDtypeStruct((slots,), jnp.int32),
        ),
        in_specs=[smem, smem, vmem, hbm, hbm, hbm, hbm, hbm],
        out_specs=(vmem, vmem, smem),
        scratch_shapes=[
            pltpu.SMEM((2 * slots,), jnp.int32),
            pltpu.SMEM((PLACES,), jnp.int32),
            pltpu.VMEM((2, GROUP, voxels, chan), BF16),
            pltpu.VMEM((chan, GROUP * voxels), F32),
            pltpu.VMEM((GROUP, voxels, chan), F32),
            pltpu.VMEM((8, 8, slots // 8, 8, chan), F32),
            pltpu.VMEM(wi.shape, BF16),
            pltpu.VMEM(wo.shape, BF16),
            pltpu.VMEM(w_down.shape, BF16),
            pltpu.SemaphoreType.DMA((2, GROUP)),
            pltpu.SemaphoreType.DMA((3,)),
        ],
        compiler_params=pltpu.CompilerParams(vmem_limit_bytes=62 * 2**20),
        cost_estimate=pl.CostEstimate(flops=17 * 10**9, bytes_accessed=8 * 2**20, transcendentals=10**8),
        name="coarse",
    )(owner, plan, early, features, got, wi, wo, w_down)


def lift_kernel(
    owner_ref, rim_ref, features_ref, w_conv_ref, w_up_ref,
    out_ref,
    wc_ref, a_ref,
):
    chan = rim_ref.shape[-1]
    gsz = rim_ref.shape[2]
    zcap = owner_ref.shape[2]
    step = pl.program_id(0)
    p, q = step // 2, lax.rem(step, 2)

    @pl.when(step == 0)
    def _():
        empty = jnp.zeros((chan, chan), BF16)
        for d in range(3):
            for k in range(4):
                for o in range(2):
                    e = k - o
                    for f in range(3):
                        col = (2 * f + o) * chan
                        wc_ref[d, k * chan : (k + 1) * chan, col : col + chan] = (
                            w_conv_ref[d, e, f] if 0 <= e <= 2 else empty
                        )
        a_ref[...] = jnp.zeros_like(a_ref)

    x0, y0 = p * 4, q * 4
    live = jnp.concatenate(
        [jnp.full((1, 16, chan), (owner_ref[p, q, r] >= 0).astype(F32)) for r in range(zcap)], axis=0
    )
    z = lax.rem(lax.broadcasted_iota(jnp.int32, (4 * gsz, 2 * chan), 0), gsz)
    for pair in range(2):
        y = y0 + 2 * pair
        total = jnp.zeros((4 * gsz, 6 * chan), F32)
        for d in range(3):
            rows = jnp.concatenate(
                [rim_ref[pl.ds(x0 + d, 4), y + k].reshape(4 * gsz, chan) for k in range(4)], axis=1
            )
            total += jnp.dot(rows, wc_ref[d], preferred_element_type=F32)
        below = pltpu.roll(total[:, : 2 * chan], 1, 0)
        above = pltpu.roll(total[:, 4 * chan :], 4 * gsz - 1, 0)
        summed = total[:, 2 * chan : 4 * chan] + jnp.where(z == 0, 0.0, below) + jnp.where(z == gsz - 1, 0.0, above)
        for o in range(2):
            own = rim_ref[pl.ds(x0 + 1, 4), y + o + 1].reshape(4 * gsz, chan).astype(F32)
            mixed = summed[:, o * chan : (o + 1) * chan] + own
            j = 2 * pair + o
            a_ref[j, 0, pl.ds(0, 4 * gsz, stride=2), :] = mixed
            a_ref[j, 1, pl.ds(1, 4 * gsz, stride=2), :] = mixed
            spread = jnp.concatenate([a_ref[j, 0], a_ref[j, 1]], axis=1).astype(BF16)
            for a in range(2):
                weights = jnp.concatenate(
                    [jnp.concatenate([w_up_ref[a, b, c] for b in range(2)], axis=1) for c in range(2)], axis=0
                )
                upward = jnp.dot(spread, weights, preferred_element_type=F32)
                for i in range(4):
                    part = upward[2 * gsz * i : 2 * gsz * (i + 1)].reshape(gsz // 4, 8, 2 * chan)
                    part = jnp.concatenate([part[:, :, :chan], part[:, :, chan:]], axis=1)
                    base = 128 * i + 64 * a + 16 * j
                    given = features_ref[:, base : base + 16, :].astype(F32)
                    out_ref[:, base : base + 16, :] = ((given + part) * live).astype(BF16)


def lift(owner, rim, features, w_conv, w_up):
    slots, voxels, chan = features.shape
    gsz = rim.shape[2]
    columns = 4
    vmem = pl.BlockSpec(memory_space=pltpu.VMEM)
    block = pl.BlockSpec((slots // columns, voxels, chan), lambda s: (s, 0, 0))
    return pl.pallas_call(
        lift_kernel,
        grid=(columns,),
        out_shape=jax.ShapeDtypeStruct(features.shape, BF16),
        in_specs=[pl.BlockSpec(memory_space=pltpu.SMEM), vmem, block, vmem, vmem],
        out_specs=block,
        scratch_shapes=[
            pltpu.VMEM((3, 4 * chan, 6 * chan), BF16),
            pltpu.VMEM((4, 2, 8 * gsz, chan), F32),
        ],
        compiler_params=pltpu.CompilerParams(vmem_limit_bytes=48 * 2**20),
        cost_estimate=pl.CostEstimate(flops=5 * 10**9, bytes_accessed=18 * 2**20, transcendentals=0),
        name="lift",
    )(owner, rim, features, w_conv, w_up)


def rim_kernel(
    map_ref, grid_ref, back_ref,
    out_ref,
    whole_ref, home_ref, send_sems, recv_sems,
):
    gsx, gsy, gsz, chan = grid_ref.shape
    gx, gy = lax.axis_index("gx"), lax.axis_index("gy")
    nx, ny = lax.axis_size("gx"), lax.axis_size("gy")
    sides = [(dx, dy) for dx in (-1, 0, 1) for dy in (-1, 0, 1) if (dx, dy) != (0, 0)]
    devices = [(lax.rem(gx + dx + nx, nx), lax.rem(gy + dy + ny, ny)) for dx, dy in sides]
    partners = [partner_device(name) for name in PAIRS]

    barrier = pltpu.get_barrier_semaphore()
    for device in devices + partners:
        pl.semaphore_signal(barrier, inc=1, device_id=device, device_id_type=pl.DeviceIdType.MESH)
    pl.semaphore_wait(barrier, len(devices) + len(partners))

    def send(n, src, dst, device):
        copy = pltpu.make_async_remote_copy(
            src_ref=src, dst_ref=dst, send_sem=send_sems.at[n], recv_sem=recv_sems.at[n],
            device_id=device, device_id_type=pl.DeviceIdType.MESH,
        )
        copy.start()
        return copy

    copies = []
    for k, name in enumerate(PAIRS):
        places = pl.ds(BASES[name], cap_of(name))
        copies.append(send(len(sides) + k, back_ref.at[places], home_ref.at[places], partners[k]))
    for copy in copies:
        copy.wait()

    odd = lax.broadcasted_iota(jnp.int32, (16, 8, chan), 1) // 4
    for column in range(4):
        x0, y0 = (column // 2) * 4, (column % 2) * 4

        def merge(m, _):
            zs = pl.ds(pl.multiple_of(m * 16, 16), 16)
            old = grid_ref[x0 : x0 + 4, y0 : y0 + 4, zs, :].astype(F32).reshape(16, 16, chan)
            new = []
            for pair in range(2):
                value = old[:, 8 * pair : 8 * pair + 8, :]
                for side in range(2):
                    place = map_ref[column * 16 + m * 4 + 2 * pair + side]
                    brick = home_ref[jnp.maximum(place, 0)].astype(F32).reshape(16, 8, chan)
                    taken = jnp.full((16, 8, chan), place, jnp.int32) >= 0
                    value = jnp.where(taken & (odd == side), brick, value)
                new.append(value)
            merged = jnp.concatenate(new, axis=1).reshape(4, 4, 16, chan).astype(BF16)
            whole_ref[x0 : x0 + 4, y0 : y0 + 4, zs, :] = merged
            return 0

        lax.fori_loop(0, gsz // 16, merge, 0)

    def cut(side, size):
        return {-1: pl.ds(0, 1), 0: pl.ds(0, size), 1: pl.ds(size - 1, 1)}[side]

    def place_of(side, size):
        return {-1: pl.ds(size + 1, 1), 0: pl.ds(1, size), 1: pl.ds(0, 1)}[side]

    copies = [
        send(
            n,
            whole_ref.at[cut(dx, gsx), cut(dy, gsy)],
            out_ref.at[place_of(dx, gsx), place_of(dy, gsy)],
            devices[n],
        )
        for n, (dx, dy) in enumerate(sides)
    ]
    out_ref[pl.ds(1, gsx), pl.ds(1, gsy)] = whole_ref[...]
    for copy in copies:
        copy.wait()

    @pl.when(gx == 0)
    def _():
        out_ref[0] = jnp.zeros_like(out_ref[0])

    @pl.when(gx == nx - 1)
    def _():
        out_ref[gsx + 1] = jnp.zeros_like(out_ref[gsx + 1])

    @pl.when(gy == 0)
    def _():
        out_ref[:, 0] = jnp.zeros_like(out_ref[:, 0])

    @pl.when(gy == ny - 1)
    def _():
        out_ref[:, gsy + 1] = jnp.zeros_like(out_ref[:, gsy + 1])


def with_rim(where, grid, back):
    gsx, gsy, gsz, chan = grid.shape
    vmem = pl.BlockSpec(memory_space=pltpu.VMEM)
    return pl.pallas_call(
        rim_kernel,
        out_shape=jax.ShapeDtypeStruct((gsx + 2, gsy + 2, gsz, chan), BF16),
        in_specs=[pl.BlockSpec(memory_space=pltpu.SMEM), vmem, vmem],
        out_specs=vmem,
        scratch_shapes=[
            pltpu.VMEM(grid.shape, BF16),
            pltpu.VMEM(back.shape, BF16),
            pltpu.SemaphoreType.DMA((15,)),
            pltpu.SemaphoreType.DMA((15,)),
        ],
        compiler_params=pltpu.CompilerParams(
            collective_id=1, has_side_effects=True, vmem_limit_bytes=32 * 2**20
        ),
        name="rim",
    )(where, grid, back)


def local(features, owner, norm_gain, time_shift, w_in, w_out, w_down, w_conv, w_up):
    cols_x, cols_y, zcap, voxels, chan = features.shape
    flat = features.reshape(cols_x * cols_y * zcap, voxels, chan)
    plan, early, got, wi, wo = spread(owner, flat, norm_gain, time_shift, w_in, w_out, w_down)
    grid, back, where = coarse_grid(owner, plan, early, flat, got, wi, wo, w_down)
    result = lift(owner, with_rim(where, grid, back), flat, w_conv, w_up)
    return result.reshape(features.shape)


def solution(mesh):
    in_specs = (
        P("gx", "gy", None, None, None),
        P("gx", "gy", None),
        P(),
        P(),
        P(),
        P(),
        P(),
        P(),
        P(),
    )
    out_specs = P("gx", "gy", None, None, None)
    return jax.shard_map(local, mesh=mesh, in_specs=in_specs, out_specs=out_specs, check_vma=False)
```

```python
import functools

import jax
import jax.numpy as jnp
from jax import lax
from jax.experimental import pallas as pl
from jax.experimental.pallas import tpu as pltpu
from jax.sharding import PartitionSpec as P

BF16 = jnp.bfloat16
F32 = jnp.float32
GROUP = 3
EARLY = 2 * GROUP
CHUNK = 512


def transposed(eye, block):
    return lax.dot_general(eye, block, (((1,), (1,)), ((), ())), preferred_element_type=F32)


def identity(n):
    rows = lax.broadcasted_iota(jnp.int32, (n, n), 0)
    return (rows == lax.broadcasted_iota(jnp.int32, (n, n), 1)).astype(BF16)


def prepare_weights(first, last, eye, gain_ref, shift_ref, w_in_ref, w_out_ref, w_ref):
    _, chan, hid = w_in_ref.shape
    row = lax.broadcasted_iota(jnp.int32, (chan, hid), 0)

    def one(l, _):
        gain = gain_ref[pl.ds(l, 1), :] * 0.5
        shift = shift_ref[pl.ds(l, 1), :] * 0.5
        high = shift.astype(BF16).astype(F32)
        mid = (shift - high).astype(BF16).astype(F32)
        low = shift - high - mid
        parts = jnp.where(row == 0, high, jnp.where(row == 1, mid, jnp.where(row == 2, low, 0.0))).astype(BF16)
        w_in = w_in_ref[l]
        w_out = w_out_ref[l]
        for m in range(hid // chan):
            cut = slice(m * chan, (m + 1) * chan)
            w_ref[l, cut, :chan] = (transposed(eye, w_in[:, cut]) * gain).astype(BF16)
            w_ref[l, cut, chan:] = transposed(eye, parts[:, cut]).astype(BF16)
            rows = slice(hid + (m // 2) * chan, hid + (m // 2 + 1) * chan)
            w_ref[l, rows, (m % 2) * chan : (m % 2 + 1) * chan] = transposed(eye, w_out[cut, :]).astype(BF16)
        return 0

    lax.fori_loop(first, last, one, 0)


def hidden_units(x, ones, wi):
    scale = lax.rsqrt(jnp.mean(x * x, axis=0, keepdims=True) + 1e-06)
    normed = jnp.concatenate([(x * scale).astype(BF16), ones], axis=0)
    u = jnp.dot(wi, normed, preferred_element_type=F32)
    return (u * jnp.tanh(u) + u).astype(BF16)


def feed_forward(s_ref, w_ref, first, last, between=None):
    _, rows, _ = w_ref.shape
    chan, width = s_ref.shape
    hid = rows - 2 * chan
    count = width // CHUNK
    ones = jnp.ones((chan, CHUNK), BF16)

    def hidden(l, c):
        return hidden_units(s_ref[:, c * CHUNK : (c + 1) * CHUNK], ones, w_ref[l, :hid, :])

    def update(l, c, h):
        w_out = jnp.concatenate([w_ref[l, hid : hid + chan, :], w_ref[l, hid + chan :, :]], axis=1)
        s_ref[:, c * CHUNK : (c + 1) * CHUNK] += jnp.dot(w_out, h, preferred_element_type=F32)

    def run(steps):
        held = hidden(*steps[0])
        for k, step in enumerate(steps):
            following = hidden(*steps[k + 1]) if k + 1 < len(steps) else None
            if between is not None:
                between(k)
            update(*step, held)
            held = following

    if between is not None:
        run([divmod(step, count) for step in range(first * count, last * count)])
    else:

        def layer(l, _):
            run([(l, c) for c in range(count)])
            return 0

        lax.fori_loop(first, last, layer, 0, unroll=2)


def reduced(t, eye, last_ref, t_ref, w_down_ref):
    chan = last_ref.shape[0]
    half = lax.broadcasted_iota(jnp.int32, (16, 8, 1), 1) // 4
    for m in range(4):
        block = last_ref[:, t * 512 + m * 128 : t * 512 + (m + 1) * 128]
        t_ref[t, m * 128 : (m + 1) * 128, :] = transposed(eye, block)
    total = jnp.zeros((128, 2 * chan), F32)
    for a in range(2):
        for c in range(2):
            rows = jnp.concatenate(
                [t_ref[t, pl.ds(128 * i + 64 * a + c, 32, stride=2), :] for i in range(4)], axis=0
            ).astype(BF16)
            both_b = jnp.concatenate([w_down_ref[a, 0, c], w_down_ref[a, 1, c]], axis=1)
            total += jnp.dot(rows, both_b, preferred_element_type=F32)
    both = total.reshape(16, 8, 2 * chan)
    own = jnp.where(half == 0, both[:, :, :chan], both[:, :, chan:])
    down = own + jnp.concatenate([own[:, 4:, :], own[:, :4, :]], axis=1)
    return down / (1.0 + jnp.exp(-down))


PAIRS = ("x0", "y0", "z0", "x1", "y1", "z1", "c")
CAPS = {"c": 4}
NEAR = 3
SWEEPS = 3
FULL_VMEM = 127 * 2**19
COARSE_VMEM = 61 * 2**20
RIM_VMEM = 484 * 2**17
LIFT_VMEM = 62 * 2**20


def cap_of(name):
    return CAPS.get(name, NEAR)


BASES = {name: sum(cap_of(other) for other in PAIRS[:k]) for k, name in enumerate(PAIRS)}
PLACES = sum(cap_of(name) for name in PAIRS)


def partner_device(name):
    gx, gy = lax.axis_index("gx"), lax.axis_index("gy")
    if name == "c":
        return (gx + 1 - 2 * lax.rem(gx, 2), gy)
    parity = int(name[1])
    if name[0] == "x":
        sign = 1 - 2 * lax.rem(gx // 2 + parity, 2)
        return (lax.rem(gx + 2 * sign + 8, 8), gy)
    if name[0] == "y":
        sign = 1 - 2 * lax.rem(gy // 4 + parity, 2)
        return (gx, lax.rem(gy + 4 * sign + 16, 16))
    sign = 1 - 2 * lax.rem(lax.rem(gy, 4) + parity, 2)
    return (gx, (gy // 4) * 4 + lax.rem(lax.rem(gy, 4) + sign + 4, 4))


def make_plan(count):
    gx, gy = lax.axis_index("gx"), lax.axis_index("gy")
    ax = lax.rem(lax.broadcasted_iota(jnp.int32, count.shape, 0) + gx, 8)
    ay = lax.rem(lax.broadcasted_iota(jnp.int32, count.shape, 1) + gy, 16)
    core, x, y, z = lax.rem(ax, 2), ax // 2, ay // 4, lax.rem(ay, 4)

    def ahead(v, by, axis):
        return pltpu.roll(v, (-by) % v.shape[axis], axis)

    def partner(v, name, low):
        if name == "c":
            return jnp.where(low, ahead(v, 1, 0), ahead(v, -1, 0))
        if name[0] == "x":
            return jnp.where(low, ahead(v, 2, 0), ahead(v, -2, 0))
        if name[0] == "y":
            return jnp.where(low, ahead(v, 4, 1), ahead(v, -4, 1))
        if name == "z0":
            return jnp.where(low, ahead(v, 1, 1), ahead(v, -1, 1))
        up = jnp.where(z == 3, ahead(v, -3, 1), ahead(v, 1, 1))
        down = jnp.where(z == 0, ahead(v, 3, 1), ahead(v, -1, 1))
        return jnp.where(low, up, down)

    low = {"c": core == 0}
    for k in range(2):
        low.update({"x%d" % k: lax.rem(x, 2) == k, "y%d" % k: lax.rem(y, 2) == k, "z%d" % k: lax.rem(z, 2) == k})
    flow = {name: jnp.zeros_like(count) for name in PAIRS}
    load, spare = count, count
    order = ("c", "x0", "y0", "z0", "x1", "y1", "z1")
    for k in range(SWEEPS * len(order)):
        name = order[k % len(order)]
        up = k % 2
        given = flow[name]
        diff = load - partner(load, name, low[name])
        limit = jnp.maximum(given, 0) + spare
        want = given + jnp.where(low[name], (diff + up) >> 1, -((up - diff) >> 1))
        want = jnp.clip(want, -cap_of(name), cap_of(name))
        want = jnp.maximum(jnp.minimum(want, limit), -partner(limit, name, low[name]))
        spare = limit - jnp.maximum(want, 0)
        load = load + given - want
        flow[name] = want
    return flow


def spread_kernel(
    owner_ref, features_hbm, gain_hbm, shift_hbm, w_in_hbm, w_out_hbm, w_down_hbm,
    plan_ref, early_ref, got_hbm, w_hbm,
    bricks_ref, send_ref, count_ref, first_ref, second_ref, own_ref, pick_ref, pick_smem, head_ref, head_smem,
    gain_ref, shift_ref, w_in_ref, w_out_ref, w_down_ref, w_ref, s_ref, last_ref, t_ref,
    sems, count_send, count_recv, brick_send, brick_recv,
):
    gx, gy = lax.axis_index("gx"), lax.axis_index("gy")
    cols_x, cols_y, zcap = owner_ref.shape
    layers = w_in_ref.shape[0]
    eye = identity(w_out_ref.shape[2])
    loads = [
        pltpu.make_async_copy(src, dst, sems.at[n])
        for n, (src, dst) in enumerate(
            (
                (gain_hbm, gain_ref),
                (shift_hbm, shift_ref),
                (w_in_hbm, w_in_ref),
                (w_out_hbm, w_out_ref),
                (w_down_hbm, w_down_ref),
                (features_hbm, bricks_ref),
            )
        )
    ]
    for load in loads:
        load.start()

    along_x = [(lax.rem(gx + k, 8), gy) for k in range(1, 8)]
    along_y = [(gx, lax.rem(gy + k, 16)) for k in range(1, 16)]
    barrier = pltpu.get_barrier_semaphore()
    for device in along_x + along_y:
        pl.semaphore_signal(barrier, inc=1, device_id=device, device_id_type=pl.DeviceIdType.MESH)

    row = lax.broadcasted_iota(jnp.int32, count_ref.shape, 0)
    lane = lax.broadcasted_iota(jnp.int32, count_ref.shape, 1)
    alive = jnp.zeros_like(lane)
    total = 0
    for slot in range(cols_x * cols_y * zcap):
        column, r = divmod(slot, zcap)
        mark = (owner_ref[column // cols_y, column % cols_y, r] >= 0).astype(jnp.int32)
        alive = jnp.where(lane == slot, mark, alive)
        total = total + mark
    order = alive
    for by in (1, 2, 4, 8, 16, 32):
        order = order + jnp.where(lane >= by, pltpu.roll(order, by, 1), 0)
    order = order - alive
    count_ref[...] = jnp.full(count_ref.shape, total, jnp.int32)

    def slots_of(wanted):
        repeat = wanted.shape[0] // 8
        hit = (jnp.concatenate([order] * repeat, axis=0) == wanted) & (jnp.concatenate([alive] * repeat, axis=0) > 0)
        slot = jnp.where(hit, jnp.concatenate([lane] * repeat, axis=0), 0)
        for by in (1, 2, 4, 8, 16, 32, 64):
            slot = slot + pltpu.roll(slot, by, 1)
        return slot

    head_ref[...] = slots_of(row)
    head_to_smem = pltpu.make_async_copy(head_ref, head_smem, sems.at[6])
    head_to_smem.start()
    pl.semaphore_wait(barrier, len(along_x) + len(along_y))

    def send(src, dst, send_sem, recv_sem, device):
        copy = pltpu.make_async_remote_copy(
            src_ref=src, dst_ref=dst, send_sem=send_sem, recv_sem=recv_sem,
            device_id=device, device_id_type=pl.DeviceIdType.MESH,
        )
        copy.start()
        return copy

    copies = [
        send(count_ref, first_ref.at[k], count_send.at[k], count_recv.at[k], along_x[k - 1]) for k in range(1, 8)
    ]
    for load in loads[:5]:
        load.wait()
    prepare_weights(0, layers, eye, gain_ref, shift_ref, w_in_ref, w_out_ref, w_ref)
    store = pltpu.make_async_copy(w_ref, w_hbm, sems.at[2])
    store.start()
    for copy in copies:
        copy.wait()
    column = count_ref[...]
    for k in range(1, 8):
        column = jnp.where(row == 8 - k, first_ref[k], column)
    own_ref[...] = column
    copies = [
        send(own_ref, second_ref.at[k], count_send.at[7 + k], count_recv.at[7 + k], along_y[k - 1])
        for k in range(1, 16)
    ]
    loads[5].wait()
    head_to_smem.wait()

    def begin(group):
        for t in range(GROUP):
            brick = bricks_ref[head_smem[group * GROUP + t, 0]]
            s_ref[:, t * 512 : (t + 1) * 512] = transposed(eye, brick)

    def end(group):
        last_ref[...] = s_ref[...].astype(BF16)
        for t in range(GROUP):
            made = reduced(t, eye, last_ref, t_ref, w_down_ref)
            early_ref[group * GROUP + t] = made.reshape(early_ref.shape[1:]).astype(BF16)

    begin(0)
    feed_forward(s_ref, w_ref, 0, layers // 2)
    for copy in copies:
        copy.wait()
    counts = column
    for k in range(1, 16):
        counts = jnp.where(lax.rem(lane, 16) == 16 - k, second_ref[k], counts)

    flow = make_plan(jnp.maximum(counts - EARLY, 0))
    sent = jnp.zeros_like(counts)
    got = jnp.zeros_like(counts)
    places = lax.broadcasted_iota(jnp.int32, pick_ref.shape, 0)
    want = jnp.full_like(places, -1)
    left = jnp.full((1, 1), total, jnp.int32)
    for k, name in enumerate(PAIRS):
        leaving = jnp.maximum(flow[name], 0)
        sent = jnp.where(row == k, pltpu.roll(leaving, k, 0), sent)
        got = jnp.where(row == k, pltpu.roll(jnp.maximum(-flow[name], 0), k, 0), got)
        base = BASES[name]
        here = (places >= base) & (places < base + cap_of(name))
        want = jnp.where(here, jnp.broadcast_to(left - 1, want.shape) - (places - base), want)
        left = left - leaving[0:1, 0:1]
    plan_ref[0:8, :] = sent
    plan_ref[8:16, :] = got
    pick_ref[...] = slots_of(want)
    to_smem = pltpu.make_async_copy(pick_ref, pick_smem, sems.at[0])
    to_smem.start()
    to_smem.wait()

    copies = []
    for k, name in enumerate(PAIRS):
        for t in range(cap_of(name)):
            send_ref[BASES[name] + t] = bricks_ref[pick_smem[BASES[name] + t, 0]]
        part = pl.ds(BASES[name], cap_of(name))
        copies.append(
            send(send_ref.at[part], got_hbm.at[part], brick_send.at[k], brick_recv.at[k], partner_device(name))
        )
    feed_forward(s_ref, w_ref, layers // 2, layers)
    end(0)
    begin(1)
    feed_forward(s_ref, w_ref, 0, layers)
    end(1)
    for copy in copies:
        copy.wait()
    store.wait()


def spread(owner, features, gain, shift, w_in, w_out, w_down):
    slots, voxels, chan = features.shape
    layers, _, hid = w_in.shape
    vmem = pl.BlockSpec(memory_space=pltpu.VMEM)
    hbm = pl.BlockSpec(memory_space=pltpu.HBM)
    return pl.pallas_call(
        spread_kernel,
        out_shape=(
            jax.ShapeDtypeStruct((16, 128), jnp.int32),
            jax.ShapeDtypeStruct((EARLY, 128, chan), BF16),
            jax.ShapeDtypeStruct((PLACES, voxels, chan), BF16),
            jax.ShapeDtypeStruct((layers, hid + 2 * chan, 2 * chan), BF16),
        ),
        in_specs=[pl.BlockSpec(memory_space=pltpu.SMEM)] + [hbm] * 6,
        out_specs=(vmem, vmem, hbm, hbm),
        scratch_shapes=[
            pltpu.VMEM(features.shape, BF16),
            pltpu.VMEM((PLACES, voxels, chan), BF16),
            pltpu.VMEM((8, 128), jnp.int32),
            pltpu.VMEM((8, 8, 128), jnp.int32),
            pltpu.VMEM((16, 8, 128), jnp.int32),
            pltpu.VMEM((8, 128), jnp.int32),
            pltpu.VMEM((24, 128), jnp.int32),
            pltpu.SMEM((24, 128), jnp.int32),
            pltpu.VMEM((8, 128), jnp.int32),
            pltpu.SMEM((8, 128), jnp.int32),
            pltpu.VMEM(gain.shape, F32),
            pltpu.VMEM(shift.shape, F32),
            pltpu.VMEM(w_in.shape, BF16),
            pltpu.VMEM(w_out.shape, BF16),
            pltpu.VMEM(w_down.shape, BF16),
            pltpu.VMEM((layers, hid + 2 * chan, 2 * chan), BF16),
            pltpu.VMEM((chan, GROUP * voxels), F32),
            pltpu.VMEM((chan, GROUP * voxels), BF16),
            pltpu.VMEM((GROUP, voxels, chan), F32),
            pltpu.SemaphoreType.DMA((7,)),
            pltpu.SemaphoreType.DMA((23,)),
            pltpu.SemaphoreType.DMA((23,)),
            pltpu.SemaphoreType.DMA((7,)),
            pltpu.SemaphoreType.DMA((7,)),
        ],
        compiler_params=pltpu.CompilerParams(
            collective_id=0, has_side_effects=True, vmem_limit_bytes=FULL_VMEM
        ),
        name="spread",
    )(owner, features, gain, shift, w_in, w_out, w_down)


def coarse_kernel(
    owner_ref, plan_ref, early_ref, features_ref, got_ref, w_hbm, w_down_hbm,
    out_ref, back_ref, map_ref,
    list_ref, place_ref, buf_ref, s_ref, last_ref, t_ref, made_ref, grid_ref, w_ref, w_down_ref, sems, w_sems,
):
    cols_x, cols_y, zcap = owner_ref.shape
    slots = cols_x * cols_y * zcap
    chan = s_ref.shape[0]
    eye = identity(chan)
    weights = [
        pltpu.make_async_copy(src, dst, w_sems.at[n])
        for n, (src, dst) in enumerate(((w_hbm, w_ref), (w_down_hbm, w_down_ref)))
    ]
    for w in weights:
        w.start()

    total = 0
    for slot in range(slots):
        column, r = divmod(slot, zcap)
        map_ref[slot] = -1
        list_ref[total] = slot
        total = total + (owner_ref[column // cols_y, column % cols_y, r] >= 0).astype(jnp.int32)
    kept, others = total, 0
    for k, name in enumerate(PAIRS):
        sent, came = plan_ref[k, 0], plan_ref[8 + k, 0]
        for t in range(cap_of(name)):

            @pl.when(t < sent)
            def _():
                map_ref[list_ref[kept - 1 - t]] = BASES[name] + t

            @pl.when(t < came)
            def _():
                place_ref[others + t] = BASES[name] + t

        kept, others = kept - sent, others + came
    ours = jnp.maximum(kept - EARLY, 0)
    work = ours + others
    groups = (work + GROUP - 1) // GROUP

    def fetch(g):
        half = lax.rem(g, 2)
        for t in range(GROUP):
            k = jnp.minimum(g * GROUP + t, work - 1)

            @pl.when(k < ours)
            def _():
                slot = list_ref[EARLY + k]
                pltpu.make_async_copy(features_ref.at[slot], buf_ref.at[half, t], sems.at[half, t]).start()

            @pl.when(k >= ours)
            def _():
                place = place_ref[k - ours]
                pltpu.make_async_copy(got_ref.at[place], buf_ref.at[half, t], sems.at[half, t]).start()

    @pl.when(groups > 0)
    def _():
        fetch(0)

    grid_ref[...] = jnp.zeros_like(grid_ref)
    side = lax.broadcasted_iota(jnp.int32, (8, 1), 0) // 4

    def put(slot, made):
        column, r = slot // zcap, lax.rem(slot, zcap)
        x0, y0, zpair, odd = (column // 2) * 4, lax.rem(column, 2) * 4, r // 2, lax.rem(r, 2)
        for i in range(4):
            for j in range(4):
                old = grid_ref[x0 + i, y0 + j, zpair]
                grid_ref[x0 + i, y0 + j, zpair] = jnp.where(side == odd, made[4 * i + j], old)

    for t in range(EARLY):

        @pl.when(t < total)
        def _():
            put(list_ref[t], early_ref[t].astype(F32).reshape(16, 8, chan))

    for w in weights:
        w.wait()

    def reduce(t):
        made_ref[t] = reduced(t, eye, last_ref, t_ref, w_down_ref)

    def place_results(g):
        for t in range(GROUP):
            k = g * GROUP + t

            @pl.when((k >= 0) & (k < ours))
            def _():
                put(list_ref[EARLY + k], made_ref[t])

            @pl.when((k >= ours) & (k >= 0) & (k < work))
            def _():
                pair = made_ref[t].reshape(8, 2, 8, chan)
                packed = jnp.where(side == 0, pair[:, 0], pair[:, 1])
                back_ref[place_ref[k - ours]] = packed.reshape(64, chan).astype(BF16)

    def body(g, _):
        @pl.when(g + 1 < groups)
        def _():
            fetch(g + 1)

        for t in range(GROUP):
            pltpu.make_async_copy(features_ref.at[0], buf_ref.at[lax.rem(g, 2), t], sems.at[lax.rem(g, 2), t]).wait()
        for t in range(GROUP):
            s_ref[:, t * 512 : (t + 1) * 512] = transposed(eye, buf_ref[lax.rem(g, 2), t])

        def between(step):
            if step % 6 == 1 and step // 6 < GROUP:
                reduce(step // 6)

        feed_forward(s_ref, w_ref, 0, w_ref.shape[0], between)
        last_ref[...] = s_ref[...].astype(BF16)
        place_results(g - 1)
        return 0

    lax.fori_loop(0, groups, body, 0)

    @pl.when(groups > 0)
    def _():
        for t in range(GROUP):
            reduce(t)
        place_results(groups - 1)

    def finish(x, _):
        out_ref[x] = grid_ref[x].reshape(out_ref.shape[1:]).astype(BF16)
        return 0

    lax.fori_loop(0, out_ref.shape[0], finish, 0)


def coarse_grid(owner, plan, early, features, got, weights, w_down):
    slots, voxels, chan = features.shape
    vmem = pl.BlockSpec(memory_space=pltpu.VMEM)
    hbm = pl.BlockSpec(memory_space=pltpu.HBM)
    smem = pl.BlockSpec(memory_space=pltpu.SMEM)
    return pl.pallas_call(
        coarse_kernel,
        out_shape=(
            jax.ShapeDtypeStruct((8, 8, slots, chan), BF16),
            jax.ShapeDtypeStruct((PLACES, 64, chan), BF16),
            jax.ShapeDtypeStruct((slots,), jnp.int32),
        ),
        in_specs=[smem, smem, vmem, hbm, hbm, hbm, hbm],
        out_specs=(vmem, vmem, smem),
        scratch_shapes=[
            pltpu.SMEM((2 * slots,), jnp.int32),
            pltpu.SMEM((PLACES,), jnp.int32),
            pltpu.VMEM((2, GROUP, voxels, chan), BF16),
            pltpu.VMEM((chan, GROUP * voxels), F32),
            pltpu.VMEM((chan, GROUP * voxels), BF16),
            pltpu.VMEM((GROUP, voxels, chan), F32),
            pltpu.VMEM((GROUP, 16, 8, chan), F32),
            pltpu.VMEM((8, 8, slots // 8, 8, chan), F32),
            pltpu.VMEM(weights.shape, BF16),
            pltpu.VMEM(w_down.shape, BF16),
            pltpu.SemaphoreType.DMA((2, GROUP)),
            pltpu.SemaphoreType.DMA((2,)),
        ],
        compiler_params=pltpu.CompilerParams(vmem_limit_bytes=COARSE_VMEM),
        cost_estimate=pl.CostEstimate(flops=17 * 10**9, bytes_accessed=8 * 2**20, transcendentals=10**8),
        name="coarse",
    )(owner, plan, early, features, got, weights, w_down)


def lift_kernel(
    owner_ref, rim_ref, features_ref, w_conv_ref, w_up_ref,
    out_ref,
    wc_ref, a_ref,
):
    chan = rim_ref.shape[-1]
    gsz = rim_ref.shape[2]
    zcap = owner_ref.shape[2]
    step = pl.program_id(0)
    p, q = step // 2, lax.rem(step, 2)

    @pl.when(step == 0)
    def _():
        empty = jnp.zeros((chan, chan), BF16)
        for d in range(3):
            for k in range(4):
                for o in range(2):
                    e = k - o
                    for f in range(3):
                        col = (2 * f + o) * chan
                        wc_ref[d, k * chan : (k + 1) * chan, col : col + chan] = (
                            w_conv_ref[d, e, f] if 0 <= e <= 2 else empty
                        )
        a_ref[...] = jnp.zeros_like(a_ref)

    live = jnp.concatenate(
        [jnp.full((1, 16, chan), (owner_ref[p, q, r] >= 0).astype(F32)) for r in range(zcap)], axis=0
    )
    z = lax.rem(lax.broadcasted_iota(jnp.int32, (4 * gsz, 2 * chan), 0), gsz)

    def mix(column, pair):
        x0, y = (column // 2) * 4, lax.rem(column, 2) * 4 + 2 * pair
        total = jnp.zeros((4 * gsz, 6 * chan), F32)
        for d in range(3):
            rows = jnp.concatenate(
                [rim_ref[pl.ds(x0 + d, 4), y + k].reshape(4 * gsz, chan) for k in range(4)], axis=1
            )
            total += jnp.dot(rows, wc_ref[d], preferred_element_type=F32)
        below = pltpu.roll(total[:, : 2 * chan], 1, 0)
        above = pltpu.roll(total[:, 4 * chan :], 4 * gsz - 1, 0)
        summed = total[:, 2 * chan : 4 * chan] + jnp.where(z == 0, 0.0, below) + jnp.where(z == gsz - 1, 0.0, above)
        for o in range(2):
            own = rim_ref[pl.ds(x0 + 1, 4), y + o + 1].reshape(4 * gsz, chan).astype(F32)
            mixed = summed[:, o * chan : (o + 1) * chan] + own
            a_ref[2 * pair + o, 0, pl.ds(0, 4 * gsz, stride=2), :] = mixed
            a_ref[2 * pair + o, 1, pl.ds(1, 4 * gsz, stride=2), :] = mixed

    def raise_up(pair):
        for j in (2 * pair, 2 * pair + 1):
            spread_out = jnp.concatenate([a_ref[j, 0], a_ref[j, 1]], axis=1).astype(BF16)
            for a in range(2):
                weights = jnp.concatenate(
                    [jnp.concatenate([w_up_ref[a, b, c] for b in range(2)], axis=1) for c in range(2)], axis=0
                )
                upward = jnp.dot(spread_out, weights, preferred_element_type=F32)
                for i in range(4):
                    part = upward[2 * gsz * i : 2 * gsz * (i + 1)].reshape(gsz // 4, 8, 2 * chan)
                    part = jnp.concatenate([part[:, :, :chan], part[:, :, chan:]], axis=1)
                    base = 128 * i + 64 * a + 16 * j
                    given = features_ref[:, base : base + 16, :].astype(F32)
                    out_ref[:, base : base + 16, :] = ((given + part) * live).astype(BF16)

    @pl.when(step == 0)
    def _():
        mix(step, 0)

    mix(step, 1)
    raise_up(0)
    mix(jnp.minimum(step + 1, pl.num_programs(0) - 1), 0)
    raise_up(1)


def lift(owner, rim, features, w_conv, w_up):
    slots, voxels, chan = features.shape
    gsz = rim.shape[2]
    columns = 4
    vmem = pl.BlockSpec(memory_space=pltpu.VMEM)
    block = pl.BlockSpec((slots // columns, voxels, chan), lambda s: (s, 0, 0))
    return pl.pallas_call(
        lift_kernel,
        grid=(columns,),
        out_shape=jax.ShapeDtypeStruct(features.shape, BF16),
        in_specs=[pl.BlockSpec(memory_space=pltpu.SMEM), vmem, block, vmem, vmem],
        out_specs=block,
        scratch_shapes=[
            pltpu.VMEM((3, 4 * chan, 6 * chan), BF16),
            pltpu.VMEM((4, 2, 8 * gsz, chan), F32),
        ],
        compiler_params=pltpu.CompilerParams(vmem_limit_bytes=LIFT_VMEM),
        cost_estimate=pl.CostEstimate(flops=5 * 10**9, bytes_accessed=18 * 2**20, transcendentals=0),
        name="lift",
    )(owner, rim, features, w_conv, w_up)


def rim_kernel(
    map_ref, grid_hbm, back_hbm,
    out_ref,
    grid_ref, whole_ref, home_ref, send_sems, recv_sems, load_sem,
):
    gsx, gsy, gsz, chan = grid_ref.shape
    load = pltpu.make_async_copy(grid_hbm, grid_ref, load_sem)
    load.start()
    gx, gy = lax.axis_index("gx"), lax.axis_index("gy")
    nx, ny = lax.axis_size("gx"), lax.axis_size("gy")
    sides = [(dx, dy) for dx in (-1, 0, 1) for dy in (-1, 0, 1) if (dx, dy) != (0, 0)]
    devices = [(lax.rem(gx + dx + nx, nx), lax.rem(gy + dy + ny, ny)) for dx, dy in sides]
    partners = [partner_device(name) for name in PAIRS]

    barrier = pltpu.get_barrier_semaphore()
    for device in devices + partners:
        pl.semaphore_signal(barrier, inc=1, device_id=device, device_id_type=pl.DeviceIdType.MESH)
    pl.semaphore_wait(barrier, len(devices) + len(partners))

    def send(n, src, dst, device):
        copy = pltpu.make_async_remote_copy(
            src_ref=src, dst_ref=dst, send_sem=send_sems.at[n], recv_sem=recv_sems.at[n],
            device_id=device, device_id_type=pl.DeviceIdType.MESH,
        )
        copy.start()
        return copy

    copies = []
    for k, name in enumerate(PAIRS):
        places = pl.ds(BASES[name], cap_of(name))
        copies.append(send(len(sides) + k, back_hbm.at[places], home_ref.at[places], partners[k]))
    load.wait()
    for copy in copies:
        copy.wait()

    half = lax.broadcasted_iota(jnp.int32, (1, 8, chan), 1) // 4
    for column in range(4):
        x0, y0 = (column // 2) * 4, (column % 2) * 4

        def merge(m, _):
            zs = pl.ds(pl.multiple_of(m * 16, 16), 16)
            old = grid_ref[x0 : x0 + 4, y0 : y0 + 4, zs, :].astype(F32).reshape(8, 2, 16, chan)
            new = []
            for pair in range(2):
                first, second = old[:, 0, 8 * pair : 8 * pair + 8, :], old[:, 1, 8 * pair : 8 * pair + 8, :]
                for side in range(2):
                    place = map_ref[column * 16 + m * 4 + 2 * pair + side]
                    brick = home_ref[jnp.maximum(place, 0)].astype(F32).reshape(8, 8, chan)
                    other = jnp.concatenate([brick[:, 4:, :], brick[:, :4, :]], axis=1)
                    taken = (jnp.full((1, 8, chan), place, jnp.int32) >= 0) & (half == side)
                    first = jnp.where(taken, brick if side == 0 else other, first)
                    second = jnp.where(taken, other if side == 0 else brick, second)
                new.append(jnp.stack([first, second], axis=1))
            merged = jnp.concatenate(new, axis=2).reshape(4, 4, 16, chan).astype(BF16)
            whole_ref[x0 : x0 + 4, y0 : y0 + 4, zs, :] = merged
            return 0

        lax.fori_loop(0, gsz // 16, merge, 0)

    def cut(side, size):
        return {-1: pl.ds(0, 1), 0: pl.ds(0, size), 1: pl.ds(size - 1, 1)}[side]

    def place_of(side, size):
        return {-1: pl.ds(size + 1, 1), 0: pl.ds(1, size), 1: pl.ds(0, 1)}[side]

    copies = [
        send(
            n,
            whole_ref.at[cut(dx, gsx), cut(dy, gsy)],
            out_ref.at[place_of(dx, gsx), place_of(dy, gsy)],
            devices[n],
        )
        for n, (dx, dy) in enumerate(sides)
    ]
    out_ref[pl.ds(1, gsx), pl.ds(1, gsy)] = whole_ref[...]
    for copy in copies:
        copy.wait()

    @pl.when(gx == 0)
    def _():
        out_ref[0] = jnp.zeros_like(out_ref[0])

    @pl.when(gx == nx - 1)
    def _():
        out_ref[gsx + 1] = jnp.zeros_like(out_ref[gsx + 1])

    @pl.when(gy == 0)
    def _():
        out_ref[:, 0] = jnp.zeros_like(out_ref[:, 0])

    @pl.when(gy == ny - 1)
    def _():
        out_ref[:, gsy + 1] = jnp.zeros_like(out_ref[:, gsy + 1])


def with_rim(where, grid, back):
    gsx, gsy, gsz, chan = grid.shape
    vmem = pl.BlockSpec(memory_space=pltpu.VMEM)
    hbm = pl.BlockSpec(memory_space=pltpu.HBM)
    return pl.pallas_call(
        rim_kernel,
        out_shape=jax.ShapeDtypeStruct((gsx + 2, gsy + 2, gsz, chan), BF16),
        in_specs=[pl.BlockSpec(memory_space=pltpu.SMEM), hbm, hbm],
        out_specs=vmem,
        scratch_shapes=[
            pltpu.VMEM(grid.shape, BF16),
            pltpu.VMEM(grid.shape, BF16),
            pltpu.VMEM(back.shape, BF16),
            pltpu.SemaphoreType.DMA((15,)),
            pltpu.SemaphoreType.DMA((15,)),
            pltpu.SemaphoreType.DMA,
        ],
        compiler_params=pltpu.CompilerParams(
            collective_id=1, has_side_effects=True, vmem_limit_bytes=RIM_VMEM
        ),
        name="rim",
    )(where, grid, back)


def local(features, owner, norm_gain, time_shift, w_in, w_out, w_down, w_conv, w_up):
    cols_x, cols_y, zcap, voxels, chan = features.shape
    flat = features.reshape(cols_x * cols_y * zcap, voxels, chan)
    plan, early, got, weights = spread(owner, flat, norm_gain, time_shift, w_in, w_out, w_down)
    grid, back, where = coarse_grid(owner, plan, early, flat, got, weights, w_down)
    result = lift(owner, with_rim(where, grid, back), flat, w_conv, w_up)
    return result.reshape(features.shape)


def solution(mesh):
    in_specs = (
        P("gx", "gy", None, None, None),
        P("gx", "gy", None),
        P(),
        P(),
        P(),
        P(),
        P(),
        P(),
        P(),
    )
    out_specs = P("gx", "gy", None, None, None)
    return jax.shard_map(local, mesh=mesh, in_specs=in_specs, out_specs=out_specs, check_vma=False)
```

```python
import functools

import jax
import jax.numpy as jnp
from jax import lax
from jax.experimental import pallas as pl
from jax.experimental.pallas import tpu as pltpu
from jax.sharding import PartitionSpec as P

BF16 = jnp.bfloat16
F32 = jnp.float32
GROUP = 3
EARLY = 2 * GROUP
CHUNK = 512


def transposed(eye, block):
    return lax.dot_general(eye, block, (((1,), (1,)), ((), ())), preferred_element_type=F32)


def identity(n):
    rows = lax.broadcasted_iota(jnp.int32, (n, n), 0)
    return (rows == lax.broadcasted_iota(jnp.int32, (n, n), 1)).astype(BF16)


def shift_parts(shift):
    high = shift.astype(BF16).astype(F32)
    mid = (shift - high).astype(BF16).astype(F32)
    low = shift - high - mid
    rest = jnp.zeros((128 - 3 * shift.shape[0], shift.shape[1]), F32)
    return jnp.concatenate([high, mid, low, rest], axis=0).astype(BF16)


def prepare_weights(eye, gain_ref, shift_ref, w_in_ref, w_out_ref, w_ref):
    layers, chan, hid = w_in_ref.shape
    parts = shift_parts(shift_ref[...] * 0.5)
    columns = [transposed(eye, parts[:, m * chan : (m + 1) * chan]).astype(BF16) for m in range(hid // chan)]

    def one(l, _):
        gain = gain_ref[pl.ds(l, 1), :] * 0.5
        w_in = w_in_ref[l]
        w_out = transposed(eye, w_out_ref[l]).astype(BF16)
        for m in range(hid // chan):
            cut = slice(m * chan, (m + 1) * chan)
            w_ref[l, cut, :chan] = (transposed(eye, w_in[:, cut]) * gain).astype(BF16)
            w_ref[l, cut, chan:] = columns[m]
        w_ref[l, hid : hid + chan, :] = w_out[:, : 2 * chan]
        w_ref[l, hid + chan :, :] = w_out[:, 2 * chan :]
        return 0

    lax.fori_loop(0, layers, one, 0, unroll=2)


def hidden_units(x, chosen, wi):
    scale = lax.rsqrt(jnp.mean(x * x, axis=0, keepdims=True) + 1e-06)
    normed = jnp.concatenate([(x * scale).astype(BF16), chosen], axis=0)
    u = jnp.dot(wi, normed, preferred_element_type=F32)
    return (u * jnp.tanh(u) + u).astype(BF16)


def feed_forward(s_ref, w_ref, first, last, between=None):
    layers, rows, _ = w_ref.shape
    chan, width = s_ref.shape
    hid = rows - 2 * chan
    count = width // CHUNK
    row = lax.broadcasted_iota(jnp.int32, (chan, 128), 0)

    def hidden(l, c):
        chosen = ((lax.rem(row, layers) == l) & (row < 3 * layers)).astype(F32).astype(BF16)
        chosen = jnp.concatenate([chosen] * (CHUNK // 128), axis=1)
        return hidden_units(s_ref[:, c * CHUNK : (c + 1) * CHUNK], chosen, w_ref[l, :hid, :])

    def update(l, c, h):
        w_out = jnp.concatenate([w_ref[l, hid : hid + chan, :], w_ref[l, hid + chan :, :]], axis=1)
        s_ref[:, c * CHUNK : (c + 1) * CHUNK] += jnp.dot(w_out, h, preferred_element_type=F32)

    def run(steps):
        held = hidden(*steps[0])
        for k, step in enumerate(steps):
            following = hidden(*steps[k + 1]) if k + 1 < len(steps) else None
            if between is not None:
                between(k)
            update(*step, held)
            held = following

    if between is not None:
        run([divmod(step, count) for step in range(first * count, last * count)])
    else:

        def layer(l, _):
            run([(l, c) for c in range(count)])
            return 0

        lax.fori_loop(first, last, layer, 0, unroll=8)


def reduced(t, eye, last_ref, t_ref, w_down_ref):
    chan = last_ref.shape[0]
    half = lax.broadcasted_iota(jnp.int32, (16, 8, 1), 1) // 4
    for m in range(4):
        block = last_ref[:, t * 512 + m * 128 : t * 512 + (m + 1) * 128]
        t_ref[t, m * 128 : (m + 1) * 128, :] = transposed(eye, block)
    total = jnp.zeros((128, 2 * chan), F32)
    for a in range(2):
        for c in range(2):
            rows = jnp.concatenate(
                [t_ref[t, pl.ds(128 * i + 64 * a + c, 32, stride=2), :] for i in range(4)], axis=0
            ).astype(BF16)
            both_b = jnp.concatenate([w_down_ref[a, 0, c], w_down_ref[a, 1, c]], axis=1)
            total += jnp.dot(rows, both_b, preferred_element_type=F32)
    both = total.reshape(16, 8, 2 * chan)
    own = jnp.where(half == 0, both[:, :, :chan], both[:, :, chan:])
    down = own + jnp.concatenate([own[:, 4:, :], own[:, :4, :]], axis=1)
    return down / (1.0 + jnp.exp(-down))


PAIRS = ("x0", "y0", "z0", "x1", "y1", "z1", "c")
CAPS = {"c": 4}
NEAR = 3
SWEEPS = 3
FULL_VMEM = 127 * 2**19
COARSE_VMEM = 61 * 2**20
RIM_VMEM = 484 * 2**17
LIFT_VMEM = 62 * 2**20
FIRST_CUT, SECOND_CUT = 2, 6


def cap_of(name):
    return CAPS.get(name, NEAR)


BASES = {name: sum(cap_of(other) for other in PAIRS[:k]) for k, name in enumerate(PAIRS)}
PLACES = sum(cap_of(name) for name in PAIRS)


def partner_device(name):
    gx, gy = lax.axis_index("gx"), lax.axis_index("gy")
    if name == "c":
        return (gx + 1 - 2 * lax.rem(gx, 2), gy)
    parity = int(name[1])
    if name[0] == "x":
        sign = 1 - 2 * lax.rem(gx // 2 + parity, 2)
        return (lax.rem(gx + 2 * sign + 8, 8), gy)
    if name[0] == "y":
        sign = 1 - 2 * lax.rem(gy // 4 + parity, 2)
        return (gx, lax.rem(gy + 4 * sign + 16, 16))
    sign = 1 - 2 * lax.rem(lax.rem(gy, 4) + parity, 2)
    return (gx, (gy // 4) * 4 + lax.rem(lax.rem(gy, 4) + sign + 4, 4))


def make_plan(count):
    gx, gy = lax.axis_index("gx"), lax.axis_index("gy")
    ax = lax.rem(lax.broadcasted_iota(jnp.int32, count.shape, 0) + gx, 8)
    ay = lax.rem(lax.broadcasted_iota(jnp.int32, count.shape, 1) + gy, 16)
    core, x, y, z = lax.rem(ax, 2), ax // 2, ay // 4, lax.rem(ay, 4)

    def ahead(v, by, axis):
        return pltpu.roll(v, (-by) % v.shape[axis], axis)

    def partner(v, name, low):
        if name == "c":
            return jnp.where(low, ahead(v, 1, 0), ahead(v, -1, 0))
        if name[0] == "x":
            return jnp.where(low, ahead(v, 2, 0), ahead(v, -2, 0))
        if name[0] == "y":
            return jnp.where(low, ahead(v, 4, 1), ahead(v, -4, 1))
        if name == "z0":
            return jnp.where(low, ahead(v, 1, 1), ahead(v, -1, 1))
        up = jnp.where(z == 3, ahead(v, -3, 1), ahead(v, 1, 1))
        down = jnp.where(z == 0, ahead(v, 3, 1), ahead(v, -1, 1))
        return jnp.where(low, up, down)

    low = {"c": core == 0}
    for k in range(2):
        low.update({"x%d" % k: lax.rem(x, 2) == k, "y%d" % k: lax.rem(y, 2) == k, "z%d" % k: lax.rem(z, 2) == k})
    flow = {name: jnp.zeros_like(count) for name in PAIRS}
    load, spare = count, count
    order = ("c", "x0", "y0", "z0", "x1", "y1", "z1")
    for k in range(SWEEPS * len(order)):
        name = order[k % len(order)]
        up = k % 2
        given = flow[name]
        diff = load - partner(load, name, low[name])
        limit = jnp.maximum(given, 0) + spare
        want = given + jnp.where(low[name], (diff + up) >> 1, -((up - diff) >> 1))
        want = jnp.clip(want, -cap_of(name), cap_of(name))
        want = jnp.maximum(jnp.minimum(want, limit), -partner(limit, name, low[name]))
        spare = limit - jnp.maximum(want, 0)
        load = load + given - want
        flow[name] = want
    return flow


def spread_kernel(
    owner_ref, features_hbm, gain_hbm, shift_hbm, w_in_hbm, w_out_hbm, w_down_hbm,
    plan_ref, early_ref, got_hbm, w_hbm,
    bricks_ref, send_ref, count_ref, first_ref, second_ref, own_ref, pick_ref, pick_smem, head_ref, head_smem,
    gain_ref, shift_ref, w_in_ref, w_out_ref, w_down_ref, w_ref, s_ref, last_ref, t_ref,
    sems, count_send, count_recv, brick_send, brick_recv,
):
    gx, gy = lax.axis_index("gx"), lax.axis_index("gy")
    cols_x, cols_y, zcap = owner_ref.shape
    layers = w_in_ref.shape[0]
    eye = identity(w_out_ref.shape[2])
    loads = [
        pltpu.make_async_copy(src, dst, sems.at[n])
        for n, (src, dst) in enumerate(
            (
                (gain_hbm, gain_ref),
                (shift_hbm, shift_ref),
                (w_in_hbm, w_in_ref),
                (w_out_hbm, w_out_ref),
                (w_down_hbm, w_down_ref),
                (features_hbm, bricks_ref),
            )
        )
    ]
    for load in loads:
        load.start()

    along_x = [(lax.rem(gx + k, 8), gy) for k in range(1, 8)]
    along_y = [(gx, lax.rem(gy + k, 16)) for k in range(1, 16)]
    barrier = pltpu.get_barrier_semaphore()
    for device in along_x + along_y:
        pl.semaphore_signal(barrier, inc=1, device_id=device, device_id_type=pl.DeviceIdType.MESH)

    row = lax.broadcasted_iota(jnp.int32, count_ref.shape, 0)
    lane = lax.broadcasted_iota(jnp.int32, count_ref.shape, 1)
    alive = jnp.zeros_like(lane)
    total = 0
    for slot in range(cols_x * cols_y * zcap):
        column, r = divmod(slot, zcap)
        mark = (owner_ref[column // cols_y, column % cols_y, r] >= 0).astype(jnp.int32)
        alive = jnp.where(lane == slot, mark, alive)
        total = total + mark
    order = alive
    for by in (1, 2, 4, 8, 16, 32):
        order = order + jnp.where(lane >= by, pltpu.roll(order, by, 1), 0)
    order = order - alive
    count_ref[...] = jnp.full(count_ref.shape, total, jnp.int32)

    def slots_of(wanted):
        repeat = wanted.shape[0] // 8
        hit = (jnp.concatenate([order] * repeat, axis=0) == wanted) & (jnp.concatenate([alive] * repeat, axis=0) > 0)
        slot = jnp.where(hit, jnp.concatenate([lane] * repeat, axis=0), 0)
        for by in (1, 2, 4, 8, 16, 32, 64):
            slot = slot + pltpu.roll(slot, by, 1)
        return slot

    head_ref[...] = slots_of(row)
    head_to_smem = pltpu.make_async_copy(head_ref, head_smem, sems.at[6])
    head_to_smem.start()
    pl.semaphore_wait(barrier, len(along_x) + len(along_y))

    def send(src, dst, send_sem, recv_sem, device):
        copy = pltpu.make_async_remote_copy(
            src_ref=src, dst_ref=dst, send_sem=send_sem, recv_sem=recv_sem,
            device_id=device, device_id_type=pl.DeviceIdType.MESH,
        )
        copy.start()
        return copy

    copies = [
        send(count_ref, first_ref.at[k], count_send.at[k], count_recv.at[k], along_x[k - 1]) for k in range(1, 8)
    ]
    for load in loads[:5]:
        load.wait()
    prepare_weights(eye, gain_ref, shift_ref, w_in_ref, w_out_ref, w_ref)
    store = pltpu.make_async_copy(w_ref, w_hbm, sems.at[2])
    store.start()
    loads[5].wait()
    head_to_smem.wait()

    def begin(group):
        for t in range(GROUP):
            brick = bricks_ref[head_smem[group * GROUP + t, 0]]
            s_ref[:, t * 512 : (t + 1) * 512] = transposed(eye, brick)

    def end(group, t):
        made = reduced(t, eye, last_ref, t_ref, w_down_ref)
        early_ref[group * GROUP + t] = made.reshape(early_ref.shape[1:]).astype(BF16)

    begin(0)
    feed_forward(s_ref, w_ref, 0, FIRST_CUT)
    for copy in copies:
        copy.wait()
    column = count_ref[...]
    for k in range(1, 8):
        column = jnp.where(row == 8 - k, first_ref[k], column)
    own_ref[...] = column
    copies = [
        send(own_ref, second_ref.at[k], count_send.at[7 + k], count_recv.at[7 + k], along_y[k - 1])
        for k in range(1, 16)
    ]
    feed_forward(s_ref, w_ref, FIRST_CUT, SECOND_CUT)
    for copy in copies:
        copy.wait()
    counts = column
    for k in range(1, 16):
        counts = jnp.where(lax.rem(lane, 16) == 16 - k, second_ref[k], counts)

    flow = make_plan(jnp.maximum(counts - EARLY, 0))
    sent = jnp.zeros_like(counts)
    got = jnp.zeros_like(counts)
    places = lax.broadcasted_iota(jnp.int32, pick_ref.shape, 0)
    want = jnp.full_like(places, -1)
    left = jnp.full((1, 1), total, jnp.int32)
    for k, name in enumerate(PAIRS):
        leaving = jnp.maximum(flow[name], 0)
        sent = jnp.where(row == k, pltpu.roll(leaving, k, 0), sent)
        got = jnp.where(row == k, pltpu.roll(jnp.maximum(-flow[name], 0), k, 0), got)
        base = BASES[name]
        here = (places >= base) & (places < base + cap_of(name))
        want = jnp.where(here, jnp.broadcast_to(left - 1, want.shape) - (places - base), want)
        left = left - leaving[0:1, 0:1]
    plan_ref[0:8, :] = sent
    plan_ref[8:16, :] = got
    pick_ref[...] = slots_of(want)
    to_smem = pltpu.make_async_copy(pick_ref, pick_smem, sems.at[0])
    to_smem.start()
    to_smem.wait()

    copies = []
    for k, name in enumerate(PAIRS):
        for t in range(cap_of(name)):
            send_ref[BASES[name] + t] = bricks_ref[pick_smem[BASES[name] + t, 0]]
        part = pl.ds(BASES[name], cap_of(name))
        copies.append(
            send(send_ref.at[part], got_hbm.at[part], brick_send.at[k], brick_recv.at[k], partner_device(name))
        )
    feed_forward(s_ref, w_ref, SECOND_CUT, layers)
    last_ref[...] = s_ref[...].astype(BF16)
    for t in range(GROUP):
        end(0, t)
    begin(1)
    feed_forward(s_ref, w_ref, 0, layers)
    last_ref[...] = s_ref[...].astype(BF16)
    for t in range(GROUP):
        end(1, t)
    for copy in copies:
        copy.wait()
    store.wait()


def spread(owner, features, gain, shift, w_in, w_out, w_down):
    slots, voxels, chan = features.shape
    layers, _, hid = w_in.shape
    vmem = pl.BlockSpec(memory_space=pltpu.VMEM)
    hbm = pl.BlockSpec(memory_space=pltpu.HBM)
    return pl.pallas_call(
        spread_kernel,
        out_shape=(
            jax.ShapeDtypeStruct((16, 128), jnp.int32),
            jax.ShapeDtypeStruct((EARLY, 128, chan), BF16),
            jax.ShapeDtypeStruct((PLACES, voxels, chan), BF16),
            jax.ShapeDtypeStruct((layers, hid + 2 * chan, 2 * chan), BF16),
        ),
        in_specs=[pl.BlockSpec(memory_space=pltpu.SMEM)] + [hbm] * 6,
        out_specs=(vmem, vmem, hbm, hbm),
        scratch_shapes=[
            pltpu.VMEM(features.shape, BF16),
            pltpu.VMEM((PLACES, voxels, chan), BF16),
            pltpu.VMEM((8, 128), jnp.int32),
            pltpu.VMEM((8, 8, 128), jnp.int32),
            pltpu.VMEM((16, 8, 128), jnp.int32),
            pltpu.VMEM((8, 128), jnp.int32),
            pltpu.VMEM((24, 128), jnp.int32),
            pltpu.SMEM((24, 128), jnp.int32),
            pltpu.VMEM((8, 128), jnp.int32),
            pltpu.SMEM((8, 128), jnp.int32),
            pltpu.VMEM(gain.shape, F32),
            pltpu.VMEM(shift.shape, F32),
            pltpu.VMEM(w_in.shape, BF16),
            pltpu.VMEM(w_out.shape, BF16),
            pltpu.VMEM(w_down.shape, BF16),
            pltpu.VMEM((layers, hid + 2 * chan, 2 * chan), BF16),
            pltpu.VMEM((chan, GROUP * voxels), F32),
            pltpu.VMEM((chan, GROUP * voxels), BF16),
            pltpu.VMEM((GROUP, voxels, chan), F32),
            pltpu.SemaphoreType.DMA((7,)),
            pltpu.SemaphoreType.DMA((23,)),
            pltpu.SemaphoreType.DMA((23,)),
            pltpu.SemaphoreType.DMA((7,)),
            pltpu.SemaphoreType.DMA((7,)),
        ],
        compiler_params=pltpu.CompilerParams(
            collective_id=0, has_side_effects=True, vmem_limit_bytes=FULL_VMEM
        ),
        name="spread",
    )(owner, features, gain, shift, w_in, w_out, w_down)


def coarse_kernel(
    owner_ref, plan_ref, early_ref, features_ref, got_ref, w_hbm, w_down_hbm,
    out_ref, back_ref, map_ref,
    list_ref, place_ref, buf_ref, s_ref, last_ref, t_ref, made_ref, grid_ref, w_ref, w_down_ref, sems, w_sems,
):
    cols_x, cols_y, zcap = owner_ref.shape
    slots = cols_x * cols_y * zcap
    chan = s_ref.shape[0]
    eye = identity(chan)
    weights = [
        pltpu.make_async_copy(src, dst, w_sems.at[n])
        for n, (src, dst) in enumerate(((w_hbm, w_ref), (w_down_hbm, w_down_ref)))
    ]
    for w in weights:
        w.start()

    total = 0
    for slot in range(slots):
        column, r = divmod(slot, zcap)
        map_ref[slot] = -1
        list_ref[total] = slot
        total = total + (owner_ref[column // cols_y, column % cols_y, r] >= 0).astype(jnp.int32)
    kept, others = total, 0
    for k, name in enumerate(PAIRS):
        sent, came = plan_ref[k, 0], plan_ref[8 + k, 0]
        for t in range(cap_of(name)):
            slot = list_ref[jnp.maximum(kept - 1 - t, 0)]
            map_ref[jnp.where(t < sent, slot, slots)] = BASES[name] + t
            place_ref[others + t] = BASES[name] + t

        kept, others = kept - sent, others + came
    ours = jnp.maximum(kept - EARLY, 0)
    work = ours + others
    groups = (work + GROUP - 1) // GROUP

    def fetch(g):
        half = lax.rem(g, 2)
        for t in range(GROUP):
            k = jnp.minimum(g * GROUP + t, work - 1)

            @pl.when(k < ours)
            def _():
                slot = list_ref[EARLY + k]
                pltpu.make_async_copy(features_ref.at[slot], buf_ref.at[half, t], sems.at[half, t]).start()

            @pl.when(k >= ours)
            def _():
                place = place_ref[k - ours]
                pltpu.make_async_copy(got_ref.at[place], buf_ref.at[half, t], sems.at[half, t]).start()

    @pl.when(groups > 0)
    def _():
        fetch(0)

    grid_ref[...] = jnp.zeros_like(grid_ref)
    side = lax.broadcasted_iota(jnp.int32, (8, 1), 0) // 4

    def put(slot, made):
        column, r = slot // zcap, lax.rem(slot, zcap)
        x0, y0, zpair, odd = (column // 2) * 4, lax.rem(column, 2) * 4, r // 2, lax.rem(r, 2)
        for i in range(4):
            for j in range(4):
                old = grid_ref[x0 + i, y0 + j, zpair]
                grid_ref[x0 + i, y0 + j, zpair] = jnp.where(side == odd, made[4 * i + j], old)

    for t in range(EARLY):

        @pl.when(t < total)
        def _():
            put(list_ref[t], early_ref[t].astype(F32).reshape(16, 8, chan))

    for w in weights:
        w.wait()

    def reduce(t):
        made_ref[t] = reduced(t, eye, last_ref, t_ref, w_down_ref)

    def place_results(g):
        for t in range(GROUP):
            k = g * GROUP + t

            @pl.when((k >= 0) & (k < ours))
            def _():
                put(list_ref[EARLY + k], made_ref[t])

            @pl.when((k >= ours) & (k >= 0) & (k < work))
            def _():
                pair = made_ref[t].reshape(8, 2, 8, chan)
                packed = jnp.where(side == 0, pair[:, 0], pair[:, 1])
                back_ref[place_ref[k - ours]] = packed.reshape(64, chan).astype(BF16)

    def body(g, _):
        @pl.when(g + 1 < groups)
        def _():
            fetch(g + 1)

        for t in range(GROUP):
            pltpu.make_async_copy(features_ref.at[0], buf_ref.at[lax.rem(g, 2), t], sems.at[lax.rem(g, 2), t]).wait()
        for t in range(GROUP):
            s_ref[:, t * 512 : (t + 1) * 512] = transposed(eye, buf_ref[lax.rem(g, 2), t])

        def between(step):
            if step % 6 == 1 and step // 6 < GROUP:
                reduce(step // 6)

        feed_forward(s_ref, w_ref, 0, w_ref.shape[0], between)
        last_ref[...] = s_ref[...].astype(BF16)
        place_results(g - 1)
        return 0

    lax.fori_loop(0, groups, body, 0)

    @pl.when(groups > 0)
    def _():
        for t in range(GROUP):
            reduce(t)
        place_results(groups - 1)

    def finish(x, _):
        out_ref[x] = grid_ref[x].reshape(out_ref.shape[1:]).astype(BF16)
        return 0

    lax.fori_loop(0, out_ref.shape[0], finish, 0)


def coarse_grid(owner, plan, early, features, got, weights, w_down):
    slots, voxels, chan = features.shape
    vmem = pl.BlockSpec(memory_space=pltpu.VMEM)
    hbm = pl.BlockSpec(memory_space=pltpu.HBM)
    smem = pl.BlockSpec(memory_space=pltpu.SMEM)
    return pl.pallas_call(
        coarse_kernel,
        out_shape=(
            jax.ShapeDtypeStruct((8, 8, slots, chan), BF16),
            jax.ShapeDtypeStruct((PLACES, 64, chan), BF16),
            jax.ShapeDtypeStruct((2 * slots,), jnp.int32),
        ),
        in_specs=[smem, smem, vmem, hbm, hbm, hbm, hbm],
        out_specs=(vmem, vmem, smem),
        scratch_shapes=[
            pltpu.SMEM((2 * slots,), jnp.int32),
            pltpu.SMEM((2 * PLACES,), jnp.int32),
            pltpu.VMEM((2, GROUP, voxels, chan), BF16),
            pltpu.VMEM((chan, GROUP * voxels), F32),
            pltpu.VMEM((chan, GROUP * voxels), BF16),
            pltpu.VMEM((GROUP, voxels, chan), F32),
            pltpu.VMEM((GROUP, 16, 8, chan), F32),
            pltpu.VMEM((8, 8, slots // 8, 8, chan), F32),
            pltpu.VMEM(weights.shape, BF16),
            pltpu.VMEM(w_down.shape, BF16),
            pltpu.SemaphoreType.DMA((2, GROUP)),
            pltpu.SemaphoreType.DMA((2,)),
        ],
        compiler_params=pltpu.CompilerParams(vmem_limit_bytes=COARSE_VMEM),
        cost_estimate=pl.CostEstimate(flops=17 * 10**9, bytes_accessed=8 * 2**20, transcendentals=10**8),
        name="coarse",
    )(owner, plan, early, features, got, weights, w_down)


def lift_kernel(
    owner_ref, rim_ref, features_ref, w_conv_ref, w_up_ref,
    out_ref,
    wc_ref, a_ref,
):
    chan = rim_ref.shape[-1]
    gsz = rim_ref.shape[2]
    zcap = owner_ref.shape[2]
    step = pl.program_id(0)
    p, q = step // 2, lax.rem(step, 2)

    @pl.when(step == 0)
    def _():
        empty = jnp.zeros((chan, chan), BF16)
        for d in range(3):
            for k in range(4):
                for o in range(2):
                    e = k - o
                    for f in range(3):
                        col = (2 * f + o) * chan
                        wc_ref[d, k * chan : (k + 1) * chan, col : col + chan] = (
                            w_conv_ref[d, e, f] if 0 <= e <= 2 else empty
                        )
        a_ref[...] = jnp.zeros_like(a_ref)

    live = jnp.concatenate(
        [jnp.full((1, 16, chan), (owner_ref[p, q, r] >= 0).astype(F32)) for r in range(zcap)], axis=0
    )
    z = lax.rem(lax.broadcasted_iota(jnp.int32, (4 * gsz, 2 * chan), 0), gsz)

    def mix(column, pair):
        x0, y = (column // 2) * 4, lax.rem(column, 2) * 4 + 2 * pair
        total = jnp.zeros((4 * gsz, 6 * chan), F32)
        for d in range(3):
            rows = jnp.concatenate(
                [rim_ref[pl.ds(x0 + d, 4), y + k].reshape(4 * gsz, chan) for k in range(4)], axis=1
            )
            total += jnp.dot(rows, wc_ref[d], preferred_element_type=F32)
        below = pltpu.roll(total[:, : 2 * chan], 1, 0)
        above = pltpu.roll(total[:, 4 * chan :], 4 * gsz - 1, 0)
        summed = total[:, 2 * chan : 4 * chan] + jnp.where(z == 0, 0.0, below) + jnp.where(z == gsz - 1, 0.0, above)
        for o in range(2):
            own = rim_ref[pl.ds(x0 + 1, 4), y + o + 1].reshape(4 * gsz, chan).astype(F32)
            mixed = summed[:, o * chan : (o + 1) * chan] + own
            a_ref[2 * pair + o, 0, pl.ds(0, 4 * gsz, stride=2), :] = mixed
            a_ref[2 * pair + o, 1, pl.ds(1, 4 * gsz, stride=2), :] = mixed

    def raise_up(pair):
        for j in (2 * pair, 2 * pair + 1):
            spread_out = jnp.concatenate([a_ref[j, 0], a_ref[j, 1]], axis=1).astype(BF16)
            for a in range(2):
                weights = jnp.concatenate(
                    [jnp.concatenate([w_up_ref[a, b, c] for b in range(2)], axis=1) for c in range(2)], axis=0
                )
                upward = jnp.dot(spread_out, weights, preferred_element_type=F32)
                for i in range(4):
                    part = upward[2 * gsz * i : 2 * gsz * (i + 1)].reshape(gsz // 4, 8, 2 * chan)
                    part = jnp.concatenate([part[:, :, :chan], part[:, :, chan:]], axis=1)
                    base = 128 * i + 64 * a + 16 * j
                    given = features_ref[:, base : base + 16, :].astype(F32)
                    out_ref[:, base : base + 16, :] = ((given + part) * live).astype(BF16)

    @pl.when(step == 0)
    def _():
        mix(step, 0)

    mix(step, 1)
    raise_up(0)
    mix(jnp.minimum(step + 1, pl.num_programs(0) - 1), 0)
    raise_up(1)


def lift(owner, rim, features, w_conv, w_up):
    slots, voxels, chan = features.shape
    gsz = rim.shape[2]
    columns = 4
    vmem = pl.BlockSpec(memory_space=pltpu.VMEM)
    block = pl.BlockSpec((slots // columns, voxels, chan), lambda s: (s, 0, 0))
    return pl.pallas_call(
        lift_kernel,
        grid=(columns,),
        out_shape=jax.ShapeDtypeStruct(features.shape, BF16),
        in_specs=[pl.BlockSpec(memory_space=pltpu.SMEM), vmem, block, vmem, vmem],
        out_specs=block,
        scratch_shapes=[
            pltpu.VMEM((3, 4 * chan, 6 * chan), BF16),
            pltpu.VMEM((4, 2, 8 * gsz, chan), F32),
        ],
        compiler_params=pltpu.CompilerParams(vmem_limit_bytes=LIFT_VMEM),
        cost_estimate=pl.CostEstimate(flops=5 * 10**9, bytes_accessed=18 * 2**20, transcendentals=0),
        name="lift",
    )(owner, rim, features, w_conv, w_up)


def rim_kernel(
    map_ref, grid_hbm, back_hbm,
    out_ref,
    grid_ref, whole_ref, home_ref, send_sems, recv_sems, load_sem,
):
    gsx, gsy, gsz, chan = grid_ref.shape
    load = pltpu.make_async_copy(grid_hbm, grid_ref, load_sem)
    load.start()
    gx, gy = lax.axis_index("gx"), lax.axis_index("gy")
    nx, ny = lax.axis_size("gx"), lax.axis_size("gy")
    sides = [(dx, dy) for dx in (-1, 0, 1) for dy in (-1, 0, 1) if (dx, dy) != (0, 0)]
    devices = [(lax.rem(gx + dx + nx, nx), lax.rem(gy + dy + ny, ny)) for dx, dy in sides]
    partners = [partner_device(name) for name in PAIRS]

    barrier = pltpu.get_barrier_semaphore()
    for device in devices + partners:
        pl.semaphore_signal(barrier, inc=1, device_id=device, device_id_type=pl.DeviceIdType.MESH)
    pl.semaphore_wait(barrier, len(devices) + len(partners))

    def send(n, src, dst, device):
        copy = pltpu.make_async_remote_copy(
            src_ref=src, dst_ref=dst, send_sem=send_sems.at[n], recv_sem=recv_sems.at[n],
            device_id=device, device_id_type=pl.DeviceIdType.MESH,
        )
        copy.start()
        return copy

    copies = []
    for k, name in enumerate(PAIRS):
        places = pl.ds(BASES[name], cap_of(name))
        copies.append(send(len(sides) + k, back_hbm.at[places], home_ref.at[places], partners[k]))
    load.wait()
    for copy in copies:
        copy.wait()

    half = lax.broadcasted_iota(jnp.int32, (1, 8, chan), 1) // 4
    for column in range(4):
        x0, y0 = (column // 2) * 4, (column % 2) * 4

        def merge(m, _):
            zs = pl.ds(pl.multiple_of(m * 16, 16), 16)
            old = grid_ref[x0 : x0 + 4, y0 : y0 + 4, zs, :].astype(F32).reshape(8, 2, 16, chan)
            new = []
            for pair in range(2):
                first, second = old[:, 0, 8 * pair : 8 * pair + 8, :], old[:, 1, 8 * pair : 8 * pair + 8, :]
                for side in range(2):
                    place = map_ref[column * 16 + m * 4 + 2 * pair + side]
                    brick = home_ref[jnp.maximum(place, 0)].astype(F32).reshape(8, 8, chan)
                    other = jnp.concatenate([brick[:, 4:, :], brick[:, :4, :]], axis=1)
                    taken = (jnp.full((1, 8, chan), place, jnp.int32) >= 0) & (half == side)
                    first = jnp.where(taken, brick if side == 0 else other, first)
                    second = jnp.where(taken, other if side == 0 else brick, second)
                new.append(jnp.stack([first, second], axis=1))
            merged = jnp.concatenate(new, axis=2).reshape(4, 4, 16, chan).astype(BF16)
            whole_ref[x0 : x0 + 4, y0 : y0 + 4, zs, :] = merged
            return 0

        lax.fori_loop(0, gsz // 16, merge, 0, unroll=True)

    def cut(side, size):
        return {-1: pl.ds(0, 1), 0: pl.ds(0, size), 1: pl.ds(size - 1, 1)}[side]

    def place_of(side, size):
        return {-1: pl.ds(size + 1, 1), 0: pl.ds(1, size), 1: pl.ds(0, 1)}[side]

    copies = [
        send(
            n,
            whole_ref.at[cut(dx, gsx), cut(dy, gsy)],
            out_ref.at[place_of(dx, gsx), place_of(dy, gsy)],
            devices[n],
        )
        for n, (dx, dy) in enumerate(sides)
    ]
    out_ref[pl.ds(1, gsx), pl.ds(1, gsy)] = whole_ref[...]
    for copy in copies:
        copy.wait()

    @pl.when(gx == 0)
    def _():
        out_ref[0] = jnp.zeros_like(out_ref[0])

    @pl.when(gx == nx - 1)
    def _():
        out_ref[gsx + 1] = jnp.zeros_like(out_ref[gsx + 1])

    @pl.when(gy == 0)
    def _():
        out_ref[:, 0] = jnp.zeros_like(out_ref[:, 0])

    @pl.when(gy == ny - 1)
    def _():
        out_ref[:, gsy + 1] = jnp.zeros_like(out_ref[:, gsy + 1])


def with_rim(where, grid, back):
    gsx, gsy, gsz, chan = grid.shape
    vmem = pl.BlockSpec(memory_space=pltpu.VMEM)
    hbm = pl.BlockSpec(memory_space=pltpu.HBM)
    return pl.pallas_call(
        rim_kernel,
        out_shape=jax.ShapeDtypeStruct((gsx + 2, gsy + 2, gsz, chan), BF16),
        in_specs=[pl.BlockSpec(memory_space=pltpu.SMEM), hbm, hbm],
        out_specs=vmem,
        scratch_shapes=[
            pltpu.VMEM(grid.shape, BF16),
            pltpu.VMEM(grid.shape, BF16),
            pltpu.VMEM(back.shape, BF16),
            pltpu.SemaphoreType.DMA((15,)),
            pltpu.SemaphoreType.DMA((15,)),
            pltpu.SemaphoreType.DMA,
        ],
        compiler_params=pltpu.CompilerParams(
            collective_id=1, has_side_effects=True, vmem_limit_bytes=RIM_VMEM
        ),
        name="rim",
    )(where, grid, back)


def local(features, owner, norm_gain, time_shift, w_in, w_out, w_down, w_conv, w_up):
    cols_x, cols_y, zcap, voxels, chan = features.shape
    flat = features.reshape(cols_x * cols_y * zcap, voxels, chan)
    plan, early, got, weights = spread(owner, flat, norm_gain, time_shift, w_in, w_out, w_down)
    grid, back, where = coarse_grid(owner, plan, early, flat, got, weights, w_down)
    result = lift(owner, with_rim(where, grid, back), flat, w_conv, w_up)
    return result.reshape(features.shape)


def solution(mesh):
    in_specs = (
        P("gx", "gy", None, None, None),
        P("gx", "gy", None),
        P(),
        P(),
        P(),
        P(),
        P(),
        P(),
        P(),
    )
    out_specs = P("gx", "gy", None, None, None)
    return jax.shard_map(local, mesh=mesh, in_specs=in_specs, out_specs=out_specs, check_vma=False)
```

```python
import functools

import jax
import jax.numpy as jnp
from jax import lax
from jax.experimental import pallas as pl
from jax.experimental.pallas import tpu as pltpu
from jax.sharding import PartitionSpec as P

BF16 = jnp.bfloat16
F32 = jnp.float32
GROUP = 3
EARLY = 2 * GROUP
CHUNK = 512


def transposed(eye, block):
    return lax.dot_general(eye, block, (((1,), (1,)), ((), ())), preferred_element_type=F32)


def identity(n):
    rows = lax.broadcasted_iota(jnp.int32, (n, n), 0)
    return (rows == lax.broadcasted_iota(jnp.int32, (n, n), 1)).astype(BF16)


def shift_parts(shift):
    high = shift.astype(BF16).astype(F32)
    mid = (shift - high).astype(BF16).astype(F32)
    low = shift - high - mid
    rest = jnp.zeros((128 - 3 * shift.shape[0], shift.shape[1]), F32)
    return jnp.concatenate([high, mid, low, rest], axis=0).astype(BF16)


def prepare_weights(eye, gain_ref, shift_ref, w_in_ref, w_out_ref, w_ref):
    layers, chan, hid = w_in_ref.shape
    parts = shift_parts(shift_ref[...] * 0.5)
    columns = [transposed(eye, parts[:, m * chan : (m + 1) * chan]).astype(BF16) for m in range(hid // chan)]

    def one(l, _):
        gain = gain_ref[pl.ds(l, 1), :] * 0.5
        w_in = w_in_ref[l]
        w_out = transposed(eye, w_out_ref[l]).astype(BF16)
        for m in range(hid // chan):
            cut = slice(m * chan, (m + 1) * chan)
            w_ref[l, cut, :chan] = (transposed(eye, w_in[:, cut]) * gain).astype(BF16)
            w_ref[l, cut, chan:] = columns[m]
        w_ref[l, hid : hid + chan, :] = w_out[:, : 2 * chan]
        w_ref[l, hid + chan :, :] = w_out[:, 2 * chan :]
        return 0

    lax.fori_loop(0, layers, one, 0, unroll=2)


def hidden_units(x, chosen, wi):
    scale = lax.rsqrt(jnp.mean(x * x, axis=0, keepdims=True) + 1e-06)
    normed = jnp.concatenate([(x * scale).astype(BF16), chosen], axis=0)
    u = jnp.dot(wi, normed, preferred_element_type=F32)
    return (u * jnp.tanh(u) + u).astype(BF16)


def feed_forward(s_ref, w_ref, first, last, between=None):
    layers, rows, _ = w_ref.shape
    chan, width = s_ref.shape
    hid = rows - 2 * chan
    count = width // CHUNK
    row = lax.broadcasted_iota(jnp.int32, (chan, 128), 0)

    def hidden(l, c):
        chosen = ((lax.rem(row, layers) == l) & (row < 3 * layers)).astype(F32).astype(BF16)
        chosen = jnp.concatenate([chosen] * (CHUNK // 128), axis=1)
        return hidden_units(s_ref[:, c * CHUNK : (c + 1) * CHUNK], chosen, w_ref[l, :hid, :])

    def update(l, c, h):
        w_out = jnp.concatenate([w_ref[l, hid : hid + chan, :], w_ref[l, hid + chan :, :]], axis=1)
        s_ref[:, c * CHUNK : (c + 1) * CHUNK] += jnp.dot(w_out, h, preferred_element_type=F32)

    def run(steps):
        held = hidden(*steps[0])
        for k, step in enumerate(steps):
            following = hidden(*steps[k + 1]) if k + 1 < len(steps) else None
            if between is not None:
                between(k)
            update(*step, held)
            held = following

    if between is not None:
        run([divmod(step, count) for step in range(first * count, last * count)])
    else:

        def layer(l, _):
            run([(l, c) for c in range(count)])
            return 0

        lax.fori_loop(first, last, layer, 0, unroll=8)


def reduced(t, eye, last_ref, t_ref, w_down_ref):
    chan = last_ref.shape[0]
    half = lax.broadcasted_iota(jnp.int32, (16, 8, 1), 1) // 4
    for m in range(4):
        block = last_ref[:, t * 512 + m * 128 : t * 512 + (m + 1) * 128]
        t_ref[t, m * 128 : (m + 1) * 128, :] = transposed(eye, block)
    total = jnp.zeros((128, 2 * chan), F32)
    for a in range(2):
        for c in range(2):
            rows = jnp.concatenate(
                [t_ref[t, pl.ds(128 * i + 64 * a + c, 32, stride=2), :] for i in range(4)], axis=0
            ).astype(BF16)
            both_b = jnp.concatenate([w_down_ref[a, 0, c], w_down_ref[a, 1, c]], axis=1)
            total += jnp.dot(rows, both_b, preferred_element_type=F32)
    both = total.reshape(16, 8, 2 * chan)
    own = jnp.where(half == 0, both[:, :, :chan], both[:, :, chan:])
    down = own + jnp.concatenate([own[:, 4:, :], own[:, :4, :]], axis=1)
    return down / (1.0 + jnp.exp(-down))


PAIRS = ("x0", "y0", "z0", "x1", "y1", "z1", "c")
CAPS = {"c": 4}
NEAR = 3
SWEEPS = 3
FULL_VMEM = 127 * 2**19
COARSE_VMEM = 61 * 2**20
RIM_VMEM = 484 * 2**17
LIFT_VMEM = 62 * 2**20
FIRST_CUT, SECOND_CUT = 2, 6


def cap_of(name):
    return CAPS.get(name, NEAR)


BASES = {name: sum(cap_of(other) for other in PAIRS[:k]) for k, name in enumerate(PAIRS)}
PLACES = sum(cap_of(name) for name in PAIRS)


def partner_device(name):
    gx, gy = lax.axis_index("gx"), lax.axis_index("gy")
    if name == "c":
        return (gx + 1 - 2 * lax.rem(gx, 2), gy)
    parity = int(name[1])
    if name[0] == "x":
        sign = 1 - 2 * lax.rem(gx // 2 + parity, 2)
        return (lax.rem(gx + 2 * sign + 8, 8), gy)
    if name[0] == "y":
        sign = 1 - 2 * lax.rem(gy // 4 + parity, 2)
        return (gx, lax.rem(gy + 4 * sign + 16, 16))
    sign = 1 - 2 * lax.rem(lax.rem(gy, 4) + parity, 2)
    return (gx, (gy // 4) * 4 + lax.rem(lax.rem(gy, 4) + sign + 4, 4))


def make_plan(count):
    gx, gy = lax.axis_index("gx"), lax.axis_index("gy")
    ax = lax.rem(lax.broadcasted_iota(jnp.int32, count.shape, 0) + gx, 8)
    ay = lax.rem(lax.broadcasted_iota(jnp.int32, count.shape, 1) + gy, 16)
    core, x, y, z = lax.rem(ax, 2), ax // 2, ay // 4, lax.rem(ay, 4)

    def ahead(v, by, axis):
        return pltpu.roll(v, (-by) % v.shape[axis], axis)

    def partner(v, name, low):
        if name == "c":
            return jnp.where(low, ahead(v, 1, 0), ahead(v, -1, 0))
        if name[0] == "x":
            return jnp.where(low, ahead(v, 2, 0), ahead(v, -2, 0))
        if name[0] == "y":
            return jnp.where(low, ahead(v, 4, 1), ahead(v, -4, 1))
        if name == "z0":
            return jnp.where(low, ahead(v, 1, 1), ahead(v, -1, 1))
        up = jnp.where(z == 3, ahead(v, -3, 1), ahead(v, 1, 1))
        down = jnp.where(z == 0, ahead(v, 3, 1), ahead(v, -1, 1))
        return jnp.where(low, up, down)

    low = {"c": core == 0}
    for k in range(2):
        low.update({"x%d" % k: lax.rem(x, 2) == k, "y%d" % k: lax.rem(y, 2) == k, "z%d" % k: lax.rem(z, 2) == k})
    flow = {name: jnp.zeros_like(count) for name in PAIRS}
    load, spare = count, count
    order = ("c", "x0", "y0", "z0", "x1", "y1", "z1")
    for k in range(SWEEPS * len(order)):
        name = order[k % len(order)]
        up = k % 2
        given = flow[name]
        diff = load - partner(load, name, low[name])
        limit = jnp.maximum(given, 0) + spare
        want = given + jnp.where(low[name], (diff + up) >> 1, -((up - diff) >> 1))
        want = jnp.clip(want, -cap_of(name), cap_of(name))
        want = jnp.maximum(jnp.minimum(want, limit), -partner(limit, name, low[name]))
        spare = limit - jnp.maximum(want, 0)
        load = load + given - want
        flow[name] = want
    return flow


def spread_kernel(
    owner_ref, features_hbm, gain_hbm, shift_hbm, w_in_hbm, w_out_hbm, w_down_hbm,
    plan_ref, early_ref, got_hbm, w_hbm,
    bricks_ref, send_ref, count_ref, first_ref, second_ref, own_ref, pick_ref, pick_smem, head_ref, head_smem,
    gain_ref, shift_ref, w_in_ref, w_out_ref, w_down_ref, w_ref, s_ref, last_ref, t_ref,
    sems, count_send, count_recv, brick_send, brick_recv,
):
    gx, gy = lax.axis_index("gx"), lax.axis_index("gy")
    cols_x, cols_y, zcap = owner_ref.shape
    layers = w_in_ref.shape[0]
    eye = identity(w_out_ref.shape[2])
    loads = [
        pltpu.make_async_copy(src, dst, sems.at[n])
        for n, (src, dst) in enumerate(
            (
                (gain_hbm, gain_ref),
                (shift_hbm, shift_ref),
                (w_in_hbm, w_in_ref),
                (w_out_hbm, w_out_ref),
                (w_down_hbm, w_down_ref),
                (features_hbm, bricks_ref),
            )
        )
    ]
    for load in loads:
        load.start()

    along_x = [(lax.rem(gx + k, 8), gy) for k in range(1, 8)]
    along_y = [(gx, lax.rem(gy + k, 16)) for k in range(1, 16)]
    barrier = pltpu.get_barrier_semaphore()
    for device in along_x + along_y:
        pl.semaphore_signal(barrier, inc=1, device_id=device, device_id_type=pl.DeviceIdType.MESH)

    row = lax.broadcasted_iota(jnp.int32, count_ref.shape, 0)
    lane = lax.broadcasted_iota(jnp.int32, count_ref.shape, 1)
    alive = jnp.zeros_like(lane)
    total = 0
    for slot in range(cols_x * cols_y * zcap):
        column, r = divmod(slot, zcap)
        mark = (owner_ref[column // cols_y, column % cols_y, r] >= 0).astype(jnp.int32)
        alive = jnp.where(lane == slot, mark, alive)
        total = total + mark
    order = alive
    for by in (1, 2, 4, 8, 16, 32):
        order = order + jnp.where(lane >= by, pltpu.roll(order, by, 1), 0)
    order = order - alive
    count_ref[...] = jnp.full(count_ref.shape, total, jnp.int32)

    def slots_of(wanted):
        repeat = wanted.shape[0] // 8
        hit = (jnp.concatenate([order] * repeat, axis=0) == wanted) & (jnp.concatenate([alive] * repeat, axis=0) > 0)
        slot = jnp.where(hit, jnp.concatenate([lane] * repeat, axis=0), 0)
        for by in (1, 2, 4, 8, 16, 32, 64):
            slot = slot + pltpu.roll(slot, by, 1)
        return slot

    head_ref[...] = slots_of(row)
    head_to_smem = pltpu.make_async_copy(head_ref, head_smem, sems.at[6])
    head_to_smem.start()
    pl.semaphore_wait(barrier, len(along_x) + len(along_y))

    def send(src, dst, send_sem, recv_sem, device):
        copy = pltpu.make_async_remote_copy(
            src_ref=src, dst_ref=dst, send_sem=send_sem, recv_sem=recv_sem,
            device_id=device, device_id_type=pl.DeviceIdType.MESH,
        )
        copy.start()
        return copy

    copies = [
        send(count_ref, first_ref.at[k], count_send.at[k], count_recv.at[k], along_x[k - 1]) for k in range(1, 8)
    ]
    for load in loads[:5]:
        load.wait()
    prepare_weights(eye, gain_ref, shift_ref, w_in_ref, w_out_ref, w_ref)
    store = pltpu.make_async_copy(w_ref, w_hbm, sems.at[2])
    store.start()
    loads[5].wait()
    head_to_smem.wait()

    def begin(group):
        for t in range(GROUP):
            brick = bricks_ref[head_smem[group * GROUP + t, 0]]
            s_ref[:, t * 512 : (t + 1) * 512] = transposed(eye, brick)

    def end(group, t):
        made = reduced(t, eye, last_ref, t_ref, w_down_ref)
        early_ref[group * GROUP + t] = made.reshape(early_ref.shape[1:]).astype(BF16)

    begin(0)
    feed_forward(s_ref, w_ref, 0, FIRST_CUT)
    for copy in copies:
        copy.wait()
    column = count_ref[...]
    for k in range(1, 8):
        column = jnp.where(row == 8 - k, first_ref[k], column)
    own_ref[...] = column
    copies = [
        send(own_ref, second_ref.at[k], count_send.at[7 + k], count_recv.at[7 + k], along_y[k - 1])
        for k in range(1, 16)
    ]
    feed_forward(s_ref, w_ref, FIRST_CUT, SECOND_CUT)
    for copy in copies:
        copy.wait()
    counts = column
    for k in range(1, 16):
        counts = jnp.where(lax.rem(lane, 16) == 16 - k, second_ref[k], counts)

    flow = make_plan(jnp.maximum(counts - EARLY, 0))
    sent = jnp.zeros_like(counts)
    got = jnp.zeros_like(counts)
    places = lax.broadcasted_iota(jnp.int32, pick_ref.shape, 0)
    want = jnp.full_like(places, -1)
    left = jnp.full((1, 1), total, jnp.int32)
    for k, name in enumerate(PAIRS):
        leaving = jnp.maximum(flow[name], 0)
        sent = jnp.where(row == k, pltpu.roll(leaving, k, 0), sent)
        got = jnp.where(row == k, pltpu.roll(jnp.maximum(-flow[name], 0), k, 0), got)
        base = BASES[name]
        here = (places >= base) & (places < base + cap_of(name))
        want = jnp.where(here, jnp.broadcast_to(left - 1, want.shape) - (places - base), want)
        left = left - leaving[0:1, 0:1]
    plan_ref[0:8, :] = sent
    plan_ref[8:16, :] = got
    pick_ref[...] = slots_of(want)
    to_smem = pltpu.make_async_copy(pick_ref, pick_smem, sems.at[0])
    to_smem.start()
    to_smem.wait()

    copies = []
    for k, name in enumerate(PAIRS):
        for t in range(cap_of(name)):
            send_ref[BASES[name] + t] = bricks_ref[pick_smem[BASES[name] + t, 0]]
        part = pl.ds(BASES[name], cap_of(name))
        copies.append(
            send(send_ref.at[part], got_hbm.at[part], brick_send.at[k], brick_recv.at[k], partner_device(name))
        )
    feed_forward(s_ref, w_ref, SECOND_CUT, layers)
    last_ref[...] = s_ref[...].astype(BF16)
    for t in range(GROUP):
        end(0, t)
    begin(1)
    feed_forward(s_ref, w_ref, 0, layers)
    last_ref[...] = s_ref[...].astype(BF16)
    for t in range(GROUP):
        end(1, t)
    for copy in copies:
        copy.wait()
    store.wait()


def spread(owner, features, gain, shift, w_in, w_out, w_down):
    slots, voxels, chan = features.shape
    layers, _, hid = w_in.shape
    vmem = pl.BlockSpec(memory_space=pltpu.VMEM)
    hbm = pl.BlockSpec(memory_space=pltpu.HBM)
    return pl.pallas_call(
        spread_kernel,
        out_shape=(
            jax.ShapeDtypeStruct((16, 128), jnp.int32),
            jax.ShapeDtypeStruct((EARLY, 128, chan), BF16),
            jax.ShapeDtypeStruct((PLACES, voxels, chan), BF16),
            jax.ShapeDtypeStruct((layers, hid + 2 * chan, 2 * chan), BF16),
        ),
        in_specs=[pl.BlockSpec(memory_space=pltpu.SMEM)] + [hbm] * 6,
        out_specs=(vmem, vmem, hbm, hbm),
        scratch_shapes=[
            pltpu.VMEM(features.shape, BF16),
            pltpu.VMEM((PLACES, voxels, chan), BF16),
            pltpu.VMEM((8, 128), jnp.int32),
            pltpu.VMEM((8, 8, 128), jnp.int32),
            pltpu.VMEM((16, 8, 128), jnp.int32),
            pltpu.VMEM((8, 128), jnp.int32),
            pltpu.VMEM((24, 128), jnp.int32),
            pltpu.SMEM((24, 128), jnp.int32),
            pltpu.VMEM((8, 128), jnp.int32),
            pltpu.SMEM((8, 128), jnp.int32),
            pltpu.VMEM(gain.shape, F32),
            pltpu.VMEM(shift.shape, F32),
            pltpu.VMEM(w_in.shape, BF16),
            pltpu.VMEM(w_out.shape, BF16),
            pltpu.VMEM(w_down.shape, BF16),
            pltpu.VMEM((layers, hid + 2 * chan, 2 * chan), BF16),
            pltpu.VMEM((chan, GROUP * voxels), F32),
            pltpu.VMEM((chan, GROUP * voxels), BF16),
            pltpu.VMEM((GROUP, voxels, chan), F32),
            pltpu.SemaphoreType.DMA((7,)),
            pltpu.SemaphoreType.DMA((23,)),
            pltpu.SemaphoreType.DMA((23,)),
            pltpu.SemaphoreType.DMA((7,)),
            pltpu.SemaphoreType.DMA((7,)),
        ],
        compiler_params=pltpu.CompilerParams(
            collective_id=0, has_side_effects=True, vmem_limit_bytes=FULL_VMEM
        ),
        name="spread",
    )(owner, features, gain, shift, w_in, w_out, w_down)


def coarse_kernel(
    owner_ref, plan_ref, early_ref, features_ref, got_ref, w_hbm, w_down_hbm,
    out_ref, back_ref, map_ref,
    list_ref, place_ref, buf_ref, s_ref, last_ref, t_ref, made_ref, grid_ref, w_ref, w_down_ref, sems, w_sems,
):
    cols_x, cols_y, zcap = owner_ref.shape
    slots = cols_x * cols_y * zcap
    chan = s_ref.shape[0]
    eye = identity(chan)
    weights = [
        pltpu.make_async_copy(src, dst, w_sems.at[n])
        for n, (src, dst) in enumerate(((w_hbm, w_ref), (w_down_hbm, w_down_ref)))
    ]
    for w in weights:
        w.start()

    total = 0
    for slot in range(slots):
        column, r = divmod(slot, zcap)
        map_ref[slot] = -1
        list_ref[total] = slot
        total = total + (owner_ref[column // cols_y, column % cols_y, r] >= 0).astype(jnp.int32)
    kept, others = total, 0
    for k, name in enumerate(PAIRS):
        sent, came = plan_ref[k, 0], plan_ref[8 + k, 0]
        for t in range(cap_of(name)):
            slot = list_ref[jnp.maximum(kept - 1 - t, 0)]
            map_ref[jnp.where(t < sent, slot, slots)] = BASES[name] + t
            place_ref[others + t] = BASES[name] + t

        kept, others = kept - sent, others + came
    ours = jnp.maximum(kept - EARLY, 0)
    work = ours + others
    groups = (work + GROUP - 1) // GROUP

    def fetch(g):
        half = lax.rem(g, 2)
        for t in range(GROUP):
            k = jnp.minimum(g * GROUP + t, work - 1)

            @pl.when(k < ours)
            def _():
                slot = list_ref[EARLY + k]
                pltpu.make_async_copy(features_ref.at[slot], buf_ref.at[half, t], sems.at[half, t]).start()

            @pl.when(k >= ours)
            def _():
                place = place_ref[k - ours]
                pltpu.make_async_copy(got_ref.at[place], buf_ref.at[half, t], sems.at[half, t]).start()

    @pl.when(groups > 0)
    def _():
        fetch(0)

    grid_ref[...] = jnp.zeros_like(grid_ref)
    side = lax.broadcasted_iota(jnp.int32, (8, 1), 0) // 4

    def put(slot, made):
        column, r = slot // zcap, lax.rem(slot, zcap)
        x0, y0, zpair, odd = (column // 2) * 4, lax.rem(column, 2) * 4, r // 2, lax.rem(r, 2)
        for i in range(4):
            for j in range(4):
                old = grid_ref[x0 + i, y0 + j, zpair]
                grid_ref[x0 + i, y0 + j, zpair] = jnp.where(side == odd, made[4 * i + j], old)

    for t in range(EARLY):

        @pl.when(t < total)
        def _():
            put(list_ref[t], early_ref[t].astype(F32).reshape(16, 8, chan))

    for w in weights:
        w.wait()

    def reduce(t):
        made_ref[t] = reduced(t, eye, last_ref, t_ref, w_down_ref)

    def place_results(g):
        for t in range(GROUP):
            k = g * GROUP + t

            @pl.when((k >= 0) & (k < ours))
            def _():
                put(list_ref[EARLY + k], made_ref[t])

            @pl.when((k >= ours) & (k >= 0) & (k < work))
            def _():
                pair = made_ref[t].reshape(8, 2, 8, chan)
                packed = jnp.where(side == 0, pair[:, 0], pair[:, 1])
                back_ref[place_ref[k - ours]] = packed.reshape(64, chan).astype(BF16)

    def body(g, _):
        @pl.when(g + 1 < groups)
        def _():
            fetch(g + 1)

        for t in range(GROUP):
            pltpu.make_async_copy(features_ref.at[0], buf_ref.at[lax.rem(g, 2), t], sems.at[lax.rem(g, 2), t]).wait()
        for t in range(GROUP):
            s_ref[:, t * 512 : (t + 1) * 512] = transposed(eye, buf_ref[lax.rem(g, 2), t])

        def between(step):
            if step % 6 == 1 and step // 6 < GROUP:
                reduce(step // 6)

        feed_forward(s_ref, w_ref, 0, w_ref.shape[0], between)
        last_ref[...] = s_ref[...].astype(BF16)
        place_results(g - 1)
        return 0

    lax.fori_loop(0, groups, body, 0)

    @pl.when(groups > 0)
    def _():
        for t in range(GROUP):
            reduce(t)
        place_results(groups - 1)

    def finish(x, _):
        out_ref[x] = grid_ref[x].reshape(out_ref.shape[1:]).astype(BF16)
        return 0

    lax.fori_loop(0, out_ref.shape[0], finish, 0)


def coarse_grid(owner, plan, early, features, got, weights, w_down):
    slots, voxels, chan = features.shape
    vmem = pl.BlockSpec(memory_space=pltpu.VMEM)
    hbm = pl.BlockSpec(memory_space=pltpu.HBM)
    smem = pl.BlockSpec(memory_space=pltpu.SMEM)
    return pl.pallas_call(
        coarse_kernel,
        out_shape=(
            jax.ShapeDtypeStruct((8, 8, slots, chan), BF16),
            jax.ShapeDtypeStruct((PLACES, 64, chan), BF16),
            jax.ShapeDtypeStruct((2 * slots,), jnp.int32),
        ),
        in_specs=[smem, smem, vmem, hbm, hbm, hbm, hbm],
        out_specs=(vmem, vmem, smem),
        scratch_shapes=[
            pltpu.SMEM((2 * slots,), jnp.int32),
            pltpu.SMEM((2 * PLACES,), jnp.int32),
            pltpu.VMEM((2, GROUP, voxels, chan), BF16),
            pltpu.VMEM((chan, GROUP * voxels), F32),
            pltpu.VMEM((chan, GROUP * voxels), BF16),
            pltpu.VMEM((GROUP, voxels, chan), F32),
            pltpu.VMEM((GROUP, 16, 8, chan), F32),
            pltpu.VMEM((8, 8, slots // 8, 8, chan), F32),
            pltpu.VMEM(weights.shape, BF16),
            pltpu.VMEM(w_down.shape, BF16),
            pltpu.SemaphoreType.DMA((2, GROUP)),
            pltpu.SemaphoreType.DMA((2,)),
        ],
        compiler_params=pltpu.CompilerParams(vmem_limit_bytes=COARSE_VMEM),
        cost_estimate=pl.CostEstimate(flops=17 * 10**9, bytes_accessed=8 * 2**20, transcendentals=10**8),
        name="coarse",
    )(owner, plan, early, features, got, weights, w_down)


def lift_kernel(
    owner_ref, rim_ref, features_ref, w_conv_ref, w_up_ref,
    out_ref,
    wc_ref, a_ref,
):
    chan = rim_ref.shape[-1]
    gsz = rim_ref.shape[2]
    zcap = owner_ref.shape[2]
    step = pl.program_id(0)
    p, q = step // 2, lax.rem(step, 2)

    @pl.when(step == 0)
    def _():
        empty = jnp.zeros((chan, chan), BF16)
        for d in range(3):
            for k in range(4):
                for o in range(2):
                    e = k - o
                    for f in range(3):
                        col = (2 * f + o) * chan
                        wc_ref[d, k * chan : (k + 1) * chan, col : col + chan] = (
                            w_conv_ref[d, e, f] if 0 <= e <= 2 else empty
                        )
        a_ref[...] = jnp.zeros_like(a_ref)

    live = jnp.concatenate(
        [jnp.full((1, 16, chan), (owner_ref[p, q, r] >= 0).astype(F32)) for r in range(zcap)], axis=0
    )
    z = lax.rem(lax.broadcasted_iota(jnp.int32, (4 * gsz, 2 * chan), 0), gsz)

    def mix(column, pair):
        x0, y = (column // 2) * 4, lax.rem(column, 2) * 4 + 2 * pair
        total = jnp.zeros((4 * gsz, 6 * chan), F32)
        for d in range(3):
            rows = jnp.concatenate(
                [rim_ref[pl.ds(x0 + d, 4), y + k].reshape(4 * gsz, chan) for k in range(4)], axis=1
            )
            total += jnp.dot(rows, wc_ref[d], preferred_element_type=F32)
        below = pltpu.roll(total[:, : 2 * chan], 1, 0)
        above = pltpu.roll(total[:, 4 * chan :], 4 * gsz - 1, 0)
        summed = total[:, 2 * chan : 4 * chan] + jnp.where(z == 0, 0.0, below) + jnp.where(z == gsz - 1, 0.0, above)
        for o in range(2):
            own = rim_ref[pl.ds(x0 + 1, 4), y + o + 1].reshape(4 * gsz, chan).astype(F32)
            mixed = summed[:, o * chan : (o + 1) * chan] + own
            a_ref[2 * pair + o, 0, pl.ds(0, 4 * gsz, stride=2), :] = mixed
            a_ref[2 * pair + o, 1, pl.ds(1, 4 * gsz, stride=2), :] = mixed

    def raise_up(pair):
        for j in (2 * pair, 2 * pair + 1):
            spread_out = jnp.concatenate([a_ref[j, 0], a_ref[j, 1]], axis=1).astype(BF16)
            for a in range(2):
                weights = jnp.concatenate(
                    [jnp.concatenate([w_up_ref[a, b, c] for b in range(2)], axis=1) for c in range(2)], axis=0
                )
                upward = jnp.dot(spread_out, weights, preferred_element_type=F32)
                for i in range(4):
                    part = upward[2 * gsz * i : 2 * gsz * (i + 1)].reshape(gsz // 4, 8, 2 * chan)
                    part = jnp.concatenate([part[:, :, :chan], part[:, :, chan:]], axis=1)
                    base = 128 * i + 64 * a + 16 * j
                    given = features_ref[:, base : base + 16, :].astype(F32)
                    out_ref[:, base : base + 16, :] = ((given + part) * live).astype(BF16)

    @pl.when(step == 0)
    def _():
        mix(step, 0)

    mix(step, 1)
    raise_up(0)
    mix(jnp.minimum(step + 1, pl.num_programs(0) - 1), 0)
    raise_up(1)


def lift(owner, rim, features, w_conv, w_up):
    slots, voxels, chan = features.shape
    gsz = rim.shape[2]
    columns = 4
    vmem = pl.BlockSpec(memory_space=pltpu.VMEM)
    block = pl.BlockSpec((slots // columns, voxels, chan), lambda s: (s, 0, 0))
    return pl.pallas_call(
        lift_kernel,
        grid=(columns,),
        out_shape=jax.ShapeDtypeStruct(features.shape, BF16),
        in_specs=[pl.BlockSpec(memory_space=pltpu.SMEM), vmem, block, vmem, vmem],
        out_specs=block,
        scratch_shapes=[
            pltpu.VMEM((3, 4 * chan, 6 * chan), BF16),
            pltpu.VMEM((4, 2, 8 * gsz, chan), F32),
        ],
        compiler_params=pltpu.CompilerParams(vmem_limit_bytes=LIFT_VMEM),
        cost_estimate=pl.CostEstimate(flops=5 * 10**9, bytes_accessed=18 * 2**20, transcendentals=0),
        name="lift",
    )(owner, rim, features, w_conv, w_up)


def rim_kernel(
    map_ref, grid_hbm, back_hbm,
    out_ref,
    grid_ref, whole_ref, home_ref, send_sems, recv_sems, load_sem,
):
    gsx, gsy, gsz, chan = grid_ref.shape
    load = pltpu.make_async_copy(grid_hbm, grid_ref, load_sem)
    load.start()
    gx, gy = lax.axis_index("gx"), lax.axis_index("gy")
    nx, ny = lax.axis_size("gx"), lax.axis_size("gy")
    sides = [(0, -1), (0, 1), (-1, 0), (1, 0), (-1, -1), (-1, 1), (1, -1), (1, 1)]
    devices = [(lax.rem(gx + dx + nx, nx), lax.rem(gy + dy + ny, ny)) for dx, dy in sides]
    partners = [partner_device(name) for name in PAIRS]

    barrier = pltpu.get_barrier_semaphore()
    for device in devices + partners:
        pl.semaphore_signal(barrier, inc=1, device_id=device, device_id_type=pl.DeviceIdType.MESH)
    pl.semaphore_wait(barrier, len(devices) + len(partners))

    def send(n, src, dst, device):
        copy = pltpu.make_async_remote_copy(
            src_ref=src, dst_ref=dst, send_sem=send_sems.at[n], recv_sem=recv_sems.at[n],
            device_id=device, device_id_type=pl.DeviceIdType.MESH,
        )
        copy.start()
        return copy

    copies = []
    for k, name in enumerate(PAIRS):
        places = pl.ds(BASES[name], cap_of(name))
        copies.append(send(len(sides) + k, back_hbm.at[places], home_ref.at[places], partners[k]))
    load.wait()
    for copy in copies:
        copy.wait()

    def cut(side, size):
        return {-1: pl.ds(0, 1), 0: pl.ds(0, size), 1: pl.ds(size - 1, 1)}[side]

    def place_of(side, size):
        return {-1: pl.ds(size + 1, 1), 0: pl.ds(1, size), 1: pl.ds(0, 1)}[side]

    def send_side(n):
        dx, dy = sides[n]
        return send(
            n,
            whole_ref.at[cut(dx, gsx), cut(dy, gsy)],
            out_ref.at[place_of(dx, gsx), place_of(dy, gsy)],
            devices[n],
        )

    half = lax.broadcasted_iota(jnp.int32, (1, 8, chan), 1) // 4
    copies = []
    for column in (0, 2, 1, 3):
        x0, y0 = (column // 2) * 4, (column % 2) * 4

        def merge(m, _):
            zs = pl.ds(pl.multiple_of(m * 16, 16), 16)
            old = grid_ref[x0 : x0 + 4, y0 : y0 + 4, zs, :].astype(F32).reshape(8, 2, 16, chan)
            new = []
            for pair in range(2):
                first, second = old[:, 0, 8 * pair : 8 * pair + 8, :], old[:, 1, 8 * pair : 8 * pair + 8, :]
                for side in range(2):
                    place = map_ref[column * 16 + m * 4 + 2 * pair + side]
                    brick = home_ref[jnp.maximum(place, 0)].astype(F32).reshape(8, 8, chan)
                    other = jnp.concatenate([brick[:, 4:, :], brick[:, :4, :]], axis=1)
                    taken = (jnp.full((1, 8, chan), place, jnp.int32) >= 0) & (half == side)
                    first = jnp.where(taken, brick if side == 0 else other, first)
                    second = jnp.where(taken, other if side == 0 else brick, second)
                new.append(jnp.stack([first, second], axis=1))
            merged = jnp.concatenate(new, axis=2).reshape(4, 4, 16, chan).astype(BF16)
            whole_ref[x0 : x0 + 4, y0 : y0 + 4, zs, :] = merged
            return 0

        lax.fori_loop(0, gsz // 16, merge, 0, unroll=True)
        if column == 2:
            copies.append(send_side(0))

    copies.extend(send_side(n) for n in range(1, len(sides)))
    out_ref[pl.ds(1, gsx), pl.ds(1, gsy)] = whole_ref[...]
    for copy in copies:
        copy.wait()

    @pl.when(gx == 0)
    def _():
        out_ref[0] = jnp.zeros_like(out_ref[0])

    @pl.when(gx == nx - 1)
    def _():
        out_ref[gsx + 1] = jnp.zeros_like(out_ref[gsx + 1])

    @pl.when(gy == 0)
    def _():
        out_ref[:, 0] = jnp.zeros_like(out_ref[:, 0])

    @pl.when(gy == ny - 1)
    def _():
        out_ref[:, gsy + 1] = jnp.zeros_like(out_ref[:, gsy + 1])


def with_rim(where, grid, back):
    gsx, gsy, gsz, chan = grid.shape
    vmem = pl.BlockSpec(memory_space=pltpu.VMEM)
    hbm = pl.BlockSpec(memory_space=pltpu.HBM)
    return pl.pallas_call(
        rim_kernel,
        out_shape=jax.ShapeDtypeStruct((gsx + 2, gsy + 2, gsz, chan), BF16),
        in_specs=[pl.BlockSpec(memory_space=pltpu.SMEM), hbm, hbm],
        out_specs=vmem,
        scratch_shapes=[
            pltpu.VMEM(grid.shape, BF16),
            pltpu.VMEM(grid.shape, BF16),
            pltpu.VMEM(back.shape, BF16),
            pltpu.SemaphoreType.DMA((15,)),
            pltpu.SemaphoreType.DMA((15,)),
            pltpu.SemaphoreType.DMA,
        ],
        compiler_params=pltpu.CompilerParams(
            collective_id=1, has_side_effects=True, vmem_limit_bytes=RIM_VMEM
        ),
        name="rim",
    )(where, grid, back)


def local(features, owner, norm_gain, time_shift, w_in, w_out, w_down, w_conv, w_up):
    cols_x, cols_y, zcap, voxels, chan = features.shape
    flat = features.reshape(cols_x * cols_y * zcap, voxels, chan)
    plan, early, got, weights = spread(owner, flat, norm_gain, time_shift, w_in, w_out, w_down)
    grid, back, where = coarse_grid(owner, plan, early, flat, got, weights, w_down)
    result = lift(owner, with_rim(where, grid, back), flat, w_conv, w_up)
    return result.reshape(features.shape)


def solution(mesh):
    in_specs = (
        P("gx", "gy", None, None, None),
        P("gx", "gy", None),
        P(),
        P(),
        P(),
        P(),
        P(),
        P(),
        P(),
    )
    out_specs = P("gx", "gy", None, None, None)
    return jax.shard_map(local, mesh=mesh, in_specs=in_specs, out_specs=out_specs, check_vma=False)
```
